32 devices in a mesh: seq: 8 (over z, x), head: 4 (over y, core).
Axes of the slice: x: 2, y: 2, z: 4, core: 2. Of those that a mesh axis runs over, the one named last changes fastest.
Arguments:
- hidden_in: bfloat16 [4, 3072, 1536], P(None, 'seq'), may hold values from -6 to 6
- norm_gain: float32 [1536], replicated, may hold values from 0.5 to 1.5
- proj_gate: bfloat16 [1536, 3072], P(None, 'head'), may hold values from -0.15625 to 0.15625
- proj_inner: bfloat16 [1536, 3072], P(None, 'head'), may hold values from -0.15625 to 0.15625
- proj_step: bfloat16 [1536, 48], P(None, 'head'), may hold values from -0.21875 to 0.21875
- proj_shared: bfloat16 [1536, 256], replicated, may hold values from -0.15625 to 0.15625
- filter_inner: float32 [4, 3072], P(None, 'head'), may hold values from -3 to 3
- filter_inner_bias: float32 [3072], P('head'), may hold values from -1.5 to 1.5
- filter_shared: float32 [4, 256], replicated, may hold values from -3 to 3
- filter_shared_bias: float32 [256], replicated, may hold values from -1.5 to 1.5
- step_bias: float32 [48], P('head'), may hold values from -8 to -3, as said below
- log_rate: float32 [48], P('head'), may hold values from -4 to 1, as said below
- skip_gain: float32 [48], P('head'), may hold values from 0.5 to 2
- gate_gain: float32 [3072], P('head'), may hold values from 0.5 to 1.5
- proj_out: bfloat16 [3072, 1536], P('head'), may hold values from -0.109375 to 0.109375
- cotangent: bfloat16 [4, 3072, 1536], P(None, 'seq', 'head'), may hold values from -6 to 6
Outputs:
- activations: bfloat16 [4, 3072, 1536], P(None, 'seq', 'head')
- grad_input: float32 [4, 3072, 1536], P(None, 'seq', 'head')
- grad_norm_gain: float32 [1536], P('head')
- grad_proj_gate: float32 [1536, 3072], P(None, 'head')
- grad_proj_inner: float32 [1536, 3072], P(None, 'head')
- grad_proj_step: float32 [1536, 48], P(None, 'head')
- grad_proj_shared: float32 [1536, 256], replicated
- grad_filter_inner: float32 [4, 3072], P(None, 'head')
- grad_filter_inner_bias: float32 [3072], P('head')
- grad_filter_shared: float32 [4, 256], replicated
- grad_filter_shared_bias: float32 [256], replicated
- grad_step_bias: float32 [48], P('head')
- grad_log_rate: float32 [48], P('head')
- grad_skip_gain: float32 [48], P('head')
- grad_gate_gain: float32 [3072], P('head')
- grad_proj_out: float32 [3072, 1536], P('head')
The draws below stay inside these ranges and needn't reach their ends.
Inputs may be any that keep to these rules, and one draw needn't show every extreme that they name: `step_bias`: one value per head. `log_rate`: one value per head.
All inputs are finite; a program needn't handle non-finite values.
Results may differ from the reference program's by a relative error of at most 0.0097.
Values may be sent and summed in bfloat16 or wider, within the bound.
No kernel may reach another device: no remote copies, remote signals or barrier semaphores. Data moves between devices by JAX's collectives and lax.ppermute only.
A program may use at most 320 MiB of HBM per device.

```python
import jax
import jax.numpy as jnp
from jax import lax

D = 1536
NH = 48
HD = 64
NS = 128
DI = 3072
KCONV = 4
TOK_SEQ = 384
SEQS = 4
SEQ_LEN = 3072


def head_spread(key):
    low_end = jnp.log(jnp.sqrt(0.5 / SEQ_LEN))
    return jnp.exp(jax.random.uniform(key, (NH,), jnp.float32, low_end, jnp.log(0.2)))


def draw_log_rate(key, part):
    spread = head_spread(key)
    key = jax.random.fold_in(key, 5)
    jitter = jax.random.uniform(key, (NH,), jnp.float32, 0.8, 1.25)
    return jnp.log(10.0 * spread * jitter)


def draw_step_bias(key, part):
    spread = head_spread(key)
    key = jax.random.fold_in(key, 7)
    jitter = jax.random.uniform(key, (NH,), jnp.float32, 0.8, 1.25)
    return jnp.log(0.1 * spread * jitter)


def levels(rng, dims, shards, smallest, top_value):
    gain = 1.0
    for axis_at, shards_of in shards:
        steps = jax.random.uniform(jax.random.fold_in(jax.random.fold_in(rng, 6), axis_at), (shards_of,), jnp.float32, smallest / len(shards), top_value / len(shards))
        gain = gain * jnp.repeat(jnp.exp(steps), dims[axis_at] // shards_of).reshape((-1,) + (1,) * (len(dims) - 1 - axis_at))
    return gain


def gaussian(stream_key, extent, deviation, most, cuts=(), dtype=jnp.bfloat16):
    level = levels(stream_key, extent, cuts, -0.22, 0.18) if cuts else 1.0
    array = jax.random.normal(stream_key, extent, jnp.float32) * deviation * level
    return jnp.minimum(jnp.maximum(array, -most), most).astype(dtype)


def setup_inputs(seed: int = 0) -> dict:
    streams_of = jax.random.split(jax.random.key(seed), 17)
    hidden_in = gaussian(streams_of[0], (SEQS, SEQ_LEN, D), 1.0, 6.0, ((1, 8),))
    norm_gain = jnp.clip(1.0 + 0.1 * jax.random.normal(streams_of[1], (D,), jnp.float32), 0.5, 1.5)
    proj_gate = gaussian(streams_of[2], (D, DI), D ** -0.5, 0.15625, ((1, 4),))
    proj_inner = gaussian(streams_of[3], (D, DI), D ** -0.5, 0.15625, ((1, 4),))
    proj_step = gaussian(streams_of[4], (D, NH), (D // 2) ** -0.5, 0.21875, ((1, 4),))
    proj_shared = gaussian(streams_of[5], (D, 2 * NS), D ** -0.5, 0.15625)
    filter_inner = gaussian(streams_of[6], (KCONV, DI), KCONV ** -0.5, 3.0, ((1, 4),), jnp.float32)
    filter_inner_bias = gaussian(streams_of[7], (DI,), 0.3, 1.5, ((0, 4),), jnp.float32)
    filter_shared = gaussian(streams_of[8], (KCONV, 2 * NS), KCONV ** -0.5, 3.0, (), jnp.float32)
    filter_shared_bias = gaussian(streams_of[9], (2 * NS,), 0.3, 1.5, (), jnp.float32)
    step_bias = draw_step_bias(jax.random.fold_in(streams_of[16], 71), 0)
    log_rate = draw_log_rate(jax.random.fold_in(streams_of[16], 71), 0)
    skip_gain = jnp.clip(0.5 + 1.5 * jax.random.uniform(streams_of[12], (NH,), jnp.float32) ** levels(streams_of[12], (NH,), ((0, 4),), -0.2, 0.2), 0.5, 2.0)
    gate_gain = jnp.clip(1.0 + 0.1 * jax.random.normal(streams_of[13], (DI,), jnp.float32), 0.5, 1.5)
    proj_out = gaussian(streams_of[14], (DI, D), DI ** -0.5, 0.109375, ((0, 4),))
    cotangent = gaussian(streams_of[15], (SEQS, SEQ_LEN, D), 1.0, 6.0, ((1, 8), (2, 4)))
    return {"hidden_in": hidden_in, "norm_gain": norm_gain, "proj_gate": proj_gate, "proj_inner": proj_inner, "proj_step": proj_step, "proj_shared": proj_shared, "filter_inner": filter_inner, "filter_inner_bias": filter_inner_bias, "filter_shared": filter_shared, "filter_shared_bias": filter_shared_bias, "step_bias": step_bias, "log_rate": log_rate, "skip_gain": skip_gain, "gate_gain": gate_gain, "proj_out": proj_out, "cotangent": cotangent}


@jax.custom_vjp
def low(v):
    return lax.optimization_barrier(v.astype(jnp.bfloat16)).astype(jnp.float32)

@jax.custom_vjp
def low_back(v):
    return v

def low_keep(v):
    return (low(v), None)

def low_pass(kept, grad):
    return (grad,)

def back_keep(v):
    return (v, None)

def back_low(kept, grad):
    return (low(grad),)
low.defvjp(low_keep, low_pass)
low_back.defvjp(back_keep, back_low)
epsilon = 1e-05
highest = lax.Precision.HIGHEST

def sigmoid_gated(value):
    return value * jax.nn.sigmoid(value)

def product(left, right):
    return jnp.dot(left, right, precision=highest)

def causal_filter(extended, kernel, offset):
    kernel_len = kernel.shape[0]
    length = extended.shape[1] - kernel_len + 1
    summed = offset + kernel[0] * extended[:, 0:length]
    for tap_index in range(1, kernel_len):
        summed = summed + kernel[tap_index] * extended[:, tap_index:tap_index + length]
    return sigmoid_gated(summed)

def decay_terms(step_raw, step_bias, log_rate):
    step_size = jax.nn.softplus(step_raw + step_bias)
    log_decay = jnp.cumsum(-step_size * jnp.exp(log_rate), axis=1)
    return (jnp.swapaxes(step_size, 1, 2), jnp.swapaxes(log_decay, 1, 2))

def block_output(inner_heads, step_raw, step_bias, log_rate, shared_b, shared_c, skip_gain, state_in):
    step_size, log_decay = decay_terms(step_raw, step_bias, log_rate)
    length = inner_heads.shape[1]
    position = jnp.arange(length)
    causal = position[:, None] >= position[None, :]
    log_gap = jnp.where(causal, log_decay[:, :, :, None] - log_decay[:, :, None, :], 0.0)
    weights = jnp.where(causal, jnp.exp(log_gap), 0.0) * step_size[:, :, None, :]
    scores = jnp.einsum('sqn,skn->sqk', shared_c, shared_b, precision=highest)
    mixing = scores[:, None] * weights
    local_out = jnp.einsum('shqk,skhp->sqhp', mixing, inner_heads, precision=highest)
    carried = jnp.einsum('sqn,shpn,shq->sqhp', shared_c, state_in, jnp.exp(log_decay), precision=highest)
    return local_out + carried + skip_gain[:, None] * inner_heads

def block_state(inner_heads, step_raw, step_bias, log_rate, shared_b):
    step_size, log_decay = decay_terms(step_raw, step_bias, log_rate)
    final_log = log_decay[:, :, -1:]
    weighting = jnp.exp(final_log - log_decay) * step_size
    state_local = jnp.einsum('shk,skn,skhp->shpn', weighting, shared_b, inner_heads, precision=highest)
    return (state_local, jnp.exp(final_log[:, :, 0]))

def reference(hidden_in, norm_gain, proj_gate, proj_inner, proj_step, proj_shared, filter_inner, filter_inner_bias, filter_shared, filter_shared_bias, step_bias, log_rate, skip_gain, gate_gain, proj_out, cotangent):

    def forward(hidden, norm_g, w_gate, w_inner, w_step, w_shared, kernel_inner, offset_inner, kernel_shared, offset_shared, bias_step, rate_log, gain_skip, gain_gate, w_out):
        batch_seqs, length, width_d = hidden.shape
        inv_rms = lax.rsqrt(lax.optimization_barrier(jnp.mean(hidden * hidden, axis=-1, keepdims=True)) + epsilon)
        normed = low(hidden * inv_rms * norm_g)
        gate_pre = low_back(product(normed, w_gate))
        inner_pre = low_back(product(normed, w_inner))
        step_raw = low_back(product(normed, w_step))
        shared_pre = low_back(product(normed, w_shared))
        kernel_len = kernel_inner.shape[0]
        padding = ((0, 0), (kernel_len - 1, 0), (0, 0))
        inner_act = causal_filter(jnp.pad(inner_pre, padding), kernel_inner, offset_inner)
        shared_act = causal_filter(jnp.pad(shared_pre, padding), kernel_shared, offset_shared)
        blocks = length // TOK_SEQ
        inner_blocks = jnp.moveaxis(inner_act.reshape(batch_seqs, blocks, TOK_SEQ, NH, HD), 1, 0)
        step_blocks = jnp.moveaxis(step_raw.reshape(batch_seqs, blocks, TOK_SEQ, NH), 1, 0)
        shared_blocks = jnp.moveaxis(shared_act.reshape(batch_seqs, blocks, TOK_SEQ, 2 * NS), 1, 0)

        def advance(state, pieces):
            inner_block, step_block, shared_block = pieces
            shared_b = shared_block[..., :NS]
            shared_c = shared_block[..., NS:]
            output = block_output(inner_block, step_block, bias_step, rate_log, shared_b, shared_c, gain_skip, state)
            state_local, block_decay = block_state(inner_block, step_block, bias_step, rate_log, shared_b)
            return (block_decay[:, :, None, None] * state + state_local, output)
        start_state = jnp.zeros((batch_seqs, NH, HD, NS), jnp.float32)
        _, outputs = lax.scan(jax.checkpoint(advance), start_state, (inner_blocks, step_blocks, shared_blocks))
        ssm_out = jnp.moveaxis(outputs, 0, 1).reshape(batch_seqs, length, NH * HD)
        gated = ssm_out * sigmoid_gated(gate_pre)
        gate_rms = lax.rsqrt(lax.optimization_barrier(jnp.mean(gated * gated, axis=-1, keepdims=True)) + epsilon)
        mixer_in = low(gated * gate_rms * gain_gate)
        return hidden + product(mixer_in, w_out)
    inputs = (hidden_in.astype(jnp.float32), norm_gain, proj_gate.astype(jnp.float32), proj_inner.astype(jnp.float32), proj_step.astype(jnp.float32), proj_shared.astype(jnp.float32), filter_inner, filter_inner_bias, filter_shared, filter_shared_bias, step_bias, log_rate, skip_gain, gate_gain, proj_out.astype(jnp.float32))
    output, pullback = jax.vjp(forward, *inputs)
    grads = pullback(cotangent.astype(jnp.float32))
    return (output.astype(jnp.bfloat16), grads[0], grads[1], grads[2], grads[3], grads[4], grads[5], grads[6], grads[7], grads[8], grads[9], grads[10], grads[11], grads[12], grads[13], grads[14])
```

```python
import functools

import jax
import jax.numpy as jnp
import numpy as np
from jax import lax
from jax.experimental import pallas as pl
from jax.experimental.pallas import tpu as pltpu
from jax.sharding import PartitionSpec as P

epsilon = 1e-05
lanes = 128
chunk = 128
rim = 16
f32 = jnp.float32
bf16 = jnp.bfloat16
vmem_limit = 56 * 1024 * 1024


def nn(left, right):
    return jnp.dot(left, right, preferred_element_type=f32)


def nt(left, right):
    return lax.dot_general(left, right, (((1,), (1,)), ((), ())), preferred_element_type=f32)


def tn(left, right):
    return lax.dot_general(left, right, (((0,), (0,)), ((), ())), preferred_element_type=f32)


def two_parts(value):
    high = value.astype(bf16)
    return jnp.concatenate([high, (value - high.astype(f32)).astype(bf16)], axis=1)


def three_parts(value):
    high = value.astype(bf16)
    rest = value - high.astype(f32)
    middle = rest.astype(bf16)
    low = (rest - middle.astype(f32)).astype(bf16)
    return jnp.concatenate([high, middle, low], axis=1)


def summed_by(triangle, value):
    parts = nn(triangle, three_parts(value))
    return parts[:, :lanes] + parts[:, lanes : 2 * lanes] + parts[:, 2 * lanes :]


def iota(shape, dim):
    return lax.broadcasted_iota(jnp.int32, shape, dim)


def triangle_of(kind):
    row, col = iota((chunk, chunk), 0), iota((chunk, chunk), 1)
    keep = {"upto": row >= col, "from": row <= col, "before": row > col}[kind]
    return jnp.where(keep, 1.0, 0.0).astype(bf16)


def sigmoid(value):
    return 0.5 * jnp.tanh(0.5 * value) + 0.5


def softplus(value):
    return jnp.maximum(value, 0.0) + jnp.log1p(jnp.exp(-jnp.abs(value)))


def whole(shape):
    return pl.BlockSpec(shape, lambda s: (0,) * len(shape))


def per_seq(*dims, first=0):
    return pl.BlockSpec((None,) + dims, lambda s: (s + first,) + (0,) * len(dims))


def grid_call(kernel, seqs, in_specs, out_specs, out_shape, scratch, cost, into=()):
    given = len(in_specs)

    def filling(*refs):
        kernel(*refs[:given], *refs[given + len(into) :])

    call = pl.pallas_call(
        filling,
        grid=(seqs,),
        in_specs=in_specs + [pl.BlockSpec(memory_space=pl.ANY)] * len(into),
        input_output_aliases={given + at: at for at in range(len(into))},
        out_specs=out_specs,
        out_shape=out_shape,
        scratch_shapes=scratch,
        compiler_params=pltpu.CompilerParams(
            vmem_limit_bytes=vmem_limit, dimension_semantics=("arbitrary",)
        ),
        cost_estimate=pl.CostEstimate(flops=cost, bytes_accessed=cost, transcendentals=0),
    )
    return lambda *operands: call(*operands, *into)


def cheap(width):
    return pltpu.CompilerParams(vmem_limit_bytes=vmem_limit, dimension_semantics=("arbitrary",)), (
        pl.CostEstimate(flops=width, bytes_accessed=width, transcendentals=0)
    )


def product_kernel(at_ref, left_ref, right_ref, out_ref, *, dot):
    out_ref[...] = dot(left_ref[...], right_ref[...]).astype(out_ref.dtype)


def product(dot, left, right, dtype, start=0, rows=None):
    depth, total = left.shape if dot is tn else left.shape[::-1]
    rows = total if rows is None else rows
    size = rows // 2 if rows % 256 == 0 else rows
    cols = right.shape[0] if dot is nt else right.shape[1]
    if dot is tn:
        left_spec = pl.BlockSpec((depth, size), lambda i, at: (0, at[0] + i))
    else:
        left_spec = pl.BlockSpec((size, depth), lambda i, at: (at[0] + i, 0))
    params, cost = cheap(10**5)
    return pl.pallas_call(
        functools.partial(product_kernel, dot=dot),
        grid_spec=pltpu.PrefetchScalarGridSpec(
            num_scalar_prefetch=1,
            grid=(rows // size,),
            in_specs=[left_spec, pl.BlockSpec(right.shape, lambda i, at: (0, 0))],
            out_specs=pl.BlockSpec((size, cols), lambda i, at: (i, 0)),
        ),
        out_shape=jax.ShapeDtypeStruct((rows, cols), dtype),
        compiler_params=params,
        cost_estimate=cost,
    )(jnp.asarray(start // size, jnp.int32).reshape(1), left, right)


def back_kernel(
    blocks_ref, gate_ref, inner_ref, raw_ref, *refs, parts,
):
    weight_refs, out_ref, buffers = refs[: 3 * parts], refs[3 * parts], refs[3 * parts + 1 :]
    size = weight_refs[0].shape[0]

    @pl.when(pl.program_id(0) == 0)
    def _():
        for part in range(parts):
            rows = slice(part * size, (part + 1) * size)
            buffers[0][rows, :] = weight_refs[part][...]
            buffers[1][rows, :] = weight_refs[parts + part][...]
            buffers[2][:, rows] = weight_refs[2 * parts + part][...]

    out = nt(gate_ref[...], buffers[0][...]) + nt(inner_ref[...], buffers[1][...])
    out = out + nn(raw_ref[:, : buffers[2].shape[0]], buffers[2][...])
    out_ref[...] = out.astype(out_ref.dtype)


def back_product(blocks, size, gate, inner, raw, gate_w, inner_w, step_w, dtype):
    seqs, length, width = gate.shape
    parts = blocks.shape[0]

    def at_seq(array):
        return pl.BlockSpec((None, length, array.shape[2]), lambda s, at: (s, 0, 0))

    rows = [
        pl.BlockSpec((size, width), lambda s, at, part=part: (at[part], 0))
        for part in range(parts)
    ]
    cols = [
        pl.BlockSpec((step_w.shape[0], size), lambda s, at, part=part: (0, at[part]))
        for part in range(parts)
    ]
    params, cost = cheap(10**5)
    return pl.pallas_call(
        functools.partial(back_kernel, parts=parts),
        grid_spec=pltpu.PrefetchScalarGridSpec(
            num_scalar_prefetch=1,
            grid=(seqs,),
            in_specs=[at_seq(gate), at_seq(inner), at_seq(raw)] + rows + rows + cols,
            out_specs=pl.BlockSpec((length, parts * size), lambda s, at: (s, 0)),
            scratch_shapes=[
                pltpu.VMEM((parts * size, width), bf16),
                pltpu.VMEM((parts * size, width), bf16),
                pltpu.VMEM((step_w.shape[0], parts * size), bf16),
            ],
        ),
        out_shape=jax.ShapeDtypeStruct((seqs * length, parts * size), dtype),
        compiler_params=params,
        cost_estimate=cost,
    )(blocks, gate, inner, raw, *[gate_w] * parts, *[inner_w] * parts, *[step_w] * parts)


def spans(total, width):
    return [slice(at, at + width) for at in range(0, total, width)]


def project_kernel(
    hidden_ref, gain_ref, inner_w_ref, shared_w_ref, step_w_ref,
    normed_ref, inner_ref, shared_ref, raw_ref, inv_ref, rim_inner_ref, rim_shared_ref,
):
    length = hidden_ref.shape[0]
    heads = step_w_ref.shape[0]
    for rows in spans(length, chunk):
        hidden = hidden_ref[rows, :].astype(f32)
        inv = lax.rsqrt(jnp.mean(hidden * hidden, axis=1, keepdims=True) + epsilon)
        normed_ref[rows, :] = (hidden * inv * gain_ref[...]).astype(bf16)
        inv_ref[rows, :] = jnp.broadcast_to(inv, (chunk, lanes))
    normed = normed_ref[...]
    inner_ref[...] = nn(normed, inner_w_ref[...])
    shared_ref[...] = nn(normed, shared_w_ref[...])
    raw_ref[...] = jnp.zeros((length, lanes), f32)
    raw_ref[:, :heads] = nt(normed, step_w_ref[...])
    rim_inner_ref[...] = inner_ref[length - rim :, :]
    rim_shared_ref[...] = shared_ref[length - rim :, :]


def filter_forward(buffer, taps_ref, bias_ref, start, column, taps):
    summed = bias_ref[0:1, column]
    for tap in range(taps):
        summed = summed + taps_ref[tap : tap + 1, column] * buffer[
            pl.ds(rim + start - taps + 1 + tap, chunk), column
        ]
    s = sigmoid(summed)
    return summed * s, s * (1.0 + summed * (1.0 - s))


def states_kernel(
    inner_ref, rim_inner_ref, shared_ref, rim_shared_ref, raw_ref,
    taps_ref, bias_ref, taps_s_ref, bias_s_ref, step_bias_ref, rate_ref, spread_ref,
    x_ref, slope_ref, shared_act_ref, slope_s_ref, step_ref, decay_ref, decay_t_ref, local_ref,
    total_ref, state_ref,
    inner_buf, shared_buf, act_buf,
    *, taps, states,
):
    length, width = inner_ref.shape
    inner_buf[0:rim, :] = rim_inner_ref[...]
    inner_buf[rim:, :] = inner_ref[...]
    shared_buf[0:rim, :] = rim_shared_ref[...]
    shared_buf[rim:, :] = shared_ref[...]
    upto = triangle_of("upto")
    spread = spread_ref[...]
    base = jnp.zeros((1, lanes), f32)
    state = jnp.zeros((states, width), f32)
    for index, rows in enumerate(spans(length, chunk)):
        for column in spans(width, lanes):
            value, slope = filter_forward(
                inner_buf, taps_ref, bias_ref, rows.start, column, taps
            )
            x_ref[rows, column] = value
            slope_ref[rows, column] = slope.astype(bf16)
        for column in spans(2 * states, lanes):
            value, slope = filter_forward(
                shared_buf, taps_s_ref, bias_s_ref, rows.start, column, taps
            )
            shared_act_ref[rows, column] = value.astype(bf16)
            slope_s_ref[rows, column] = slope
        step = softplus(raw_ref[rows, :] + step_bias_ref[...])
        local = summed_by(upto, step * rate_ref[...])
        last = local[chunk - 1 : chunk, :]
        step_ref[rows, :] = step
        decay = local + base
        decay_ref[rows, :] = decay
        decay_t_ref[:, rows] = jnp.transpose(decay)[:16, :]
        weight = nn(two_parts(jnp.exp(last - local) * step), spread)
        act_buf[...] = (weight * x_ref[rows, :]).astype(bf16)
        local_ref[index, :, :] = state.astype(bf16)
        kept = nn(two_parts(jnp.broadcast_to(jnp.exp(last), (8, lanes))), spread)[0:1, :]
        state = kept * state + tn(shared_act_ref[rows, 0:states], act_buf[...])
        base = base + last
    state_ref[...] = state.astype(bf16)
    total_ref[...] = jnp.broadcast_to(base, (8, lanes))


def pair_masks():
    low = iota((chunk, lanes), 1) < lanes // 2
    return low, jnp.logical_not(low)


def halves(value, masks):
    zero = jnp.zeros_like(value)
    return jnp.concatenate(
        [jnp.where(masks[0], value, zero), jnp.where(masks[1], value, zero)], axis=0
    )


def fade(decay, decay_t, head, causal):
    gap = decay[:, head : head + 1] - decay_t[head : head + 1, :]
    return jnp.exp(jnp.where(causal, gap, -1e30))


def mix_kernel(
    x_ref, shared_act_ref, step_ref, decay_ref, decay_t_ref, local_ref, skip_ref, spread_ref,
    out_ref,
    *, states,
):
    length, width = x_ref.shape
    causal = iota((chunk, chunk), 0) >= iota((chunk, chunk), 1)
    masks = pair_masks()
    spread = spread_ref[...]
    base = jnp.zeros((1, lanes), f32)
    for index, rows in enumerate(spans(length, chunk)):
        b, c = shared_act_ref[rows, 0:states], shared_act_ref[rows, states:]
        scores = nt(c, b)
        x = x_ref[rows, :]
        decay = decay_ref[rows, :]
        decay_t = decay_t_ref[:, rows]
        stepped = (x * nn(two_parts(step_ref[rows, :]), spread)).astype(bf16)
        out = skip_ref[...] * x
        if index > 0:
            out = out + nn(two_parts(jnp.exp(decay - base)), spread) * nn(c, local_ref[index])
        base = decay[chunk - 1 : chunk, :]
        for pair, column in enumerate(spans(width, lanes)):
            mixing = jnp.concatenate(
                [
                    (fade(decay, decay_t, 2 * pair + side, causal) * scores).astype(bf16)
                    for side in range(2)
                ],
                axis=1,
            )
            part = nn(mixing, halves(stepped[:, column], masks))
            out_ref[rows, column] = out[:, column] + part


def gate_kernel(
    local_out_ref, shared_act_ref, decay_ref, state_in_ref, gate_ref, mixer_grad_ref, gain_ref,
    spread_ref,
    out_ref, sums_ref,
    square_buf, product_buf,
    *, states,
):
    length, width = local_out_ref.shape
    spread = spread_ref[...]
    for rows in spans(length, chunk):
        faded = nn(two_parts(jnp.exp(decay_ref[rows, :])), spread)
        out = local_out_ref[rows, :] + faded * nn(
            shared_act_ref[rows, states:], state_in_ref[...]
        )
        out_ref[rows, :] = out
        gate = gate_ref[rows, :]
        gated = out * gate * sigmoid(gate)
        square_buf[rows, :] = (gated * gated).astype(bf16)
        product_buf[rows, :] = (
            gated * mixer_grad_ref[rows, :] * gain_ref[...]
        ).astype(bf16)
    ones = jnp.ones((8, width), bf16)
    first = nt(ones, square_buf[...])
    second = nt(ones, product_buf[...])
    sums_ref[...] = jnp.where(iota((8, length), 0) < 4, first, second)


def gate_back_kernel(
    out_ref, gate_ref, mixer_grad_ref, sums_ref, gain_ref, shared_act_ref, decay_ref, spread_ref,
    mixer_in_ref, d_gate_ref, d_ssm_ref, lam_ref, gain_grad_ref,
    *, states, full,
):
    length, width = out_ref.shape
    spread = spread_ref[...]
    gain = gain_ref[...]
    summed = jnp.sum(sums_ref[...], axis=0)
    square = summed[0:1, :] * (1.0 / full)
    product = summed[4:5, :] * (1.0 / full)
    rms = lax.rsqrt(square + epsilon)
    scalars = jnp.concatenate([rms, rms * rms * rms * product, jnp.zeros((6, length), f32)], axis=0)
    gain_grad = jnp.zeros((1, width), f32)
    lam = jnp.zeros((states, width), f32)
    for rows in spans(length, chunk):
        columns = jnp.transpose(scalars[:, rows])
        rms_c, row_c = columns[:, 0:1], columns[:, 1:2]
        out = out_ref[rows, :]
        gate = gate_ref[rows, :]
        mixer_grad = mixer_grad_ref[rows, :]
        s = sigmoid(gate)
        act = gate * s
        gated = out * act
        normal = gated * rms_c
        mixer_in_ref[rows, :] = (normal * gain).astype(bf16)
        gain_grad = gain_grad + jnp.sum(mixer_grad * normal, axis=0, keepdims=True)
        d_gated = rms_c * (mixer_grad * gain) - gated * row_c
        d_ssm = d_gated * act
        d_ssm_ref[rows, :] = d_ssm
        d_gate_ref[rows, :] = (d_gated * out * s * (1.0 + gate * (1.0 - s))).astype(bf16)
        faded = nn(two_parts(jnp.exp(decay_ref[rows, :])), spread)
        lam = lam + tn(shared_act_ref[rows, states:], (faded * d_ssm).astype(bf16))
    lam_ref[...] = lam.astype(bf16)
    gain_grad_ref[...] = jnp.broadcast_to(gain_grad, (8, width))


def mix_back_kernel(
    x_ref, shared_act_ref, step_ref, decay_ref, decay_t_ref, local_ref, state_in_ref, d_ssm_ref,
    spread_ref, gather_ref,
    d_x_ref, d_shared_ref, d_decay_ref,
    column_buf,
    *, states,
):
    length, width = x_ref.shape
    causal = iota((chunk, chunk), 0) >= iota((chunk, chunk), 1)
    masks = pair_masks()
    spread, gather = spread_ref[...], gather_ref[...]
    since, before = triangle_of("from"), triangle_of("before")
    lam = jnp.zeros((states, width), f32)
    heads_here = 2 * (width // lanes)
    column_buf[...] = jnp.zeros_like(column_buf)
    row_at, col_at = iota((2 * chunk, lanes), 0), iota((2 * chunk, lanes), 1)
    all_rows = spans(length, chunk)
    for index in reversed(range(len(all_rows))):
        rows = all_rows[index]
        b, c = shared_act_ref[rows, 0:states], shared_act_ref[rows, states:]
        xf = x_ref[rows, :]
        d_out = d_ssm_ref[rows, :]
        decay = decay_ref[rows, :]
        decay_t = decay_t_ref[:, rows]
        step = step_ref[rows, :]
        if index > 0:
            base = decay_ref[rows.start - 1 : rows.start, :]
        else:
            base = jnp.zeros((1, lanes), f32)
        last = decay[chunk - 1 : chunk, :]
        heads = jnp.concatenate([jnp.exp(base), jnp.exp(last - base), jnp.zeros((6, lanes), f32)])
        heads = nn(two_parts(heads), spread)
        entered = local_ref[index].astype(f32) + heads[0:1, :] * state_in_ref[...].astype(f32)
        entered16 = entered.astype(bf16)
        lam16 = lam.astype(bf16)
        scores = nt(c, b)
        faded = nn(two_parts(jnp.exp(decay - base)), spread)
        fading = nn(two_parts(jnp.exp(last - decay)), spread)
        steps = nn(two_parts(step), spread)
        stepped = (xf * steps).astype(bf16)
        d_faded = (faded * d_out).astype(bf16)
        x_faded = (fading * steps * xf).astype(bf16)
        d_c = nt(d_faded, entered16)
        d_b = nt(x_faded, lam16)
        carried = nn(c, entered16)
        carrying = nn(b, lam16)
        queries = nn((d_faded.astype(f32) * carried).astype(bf16), gather)
        keys = nn((x_faded.astype(f32) * carrying).astype(bf16), gather)
        across = jnp.sum(lam * entered, axis=0, keepdims=True) * heads[1:2, :]
        across = nn(jnp.broadcast_to(across, (8, width)).astype(bf16), gather)[0:1, :]
        d_x = fading * carrying
        d_scores = jnp.zeros((chunk, chunk), f32)
        for pair, column in enumerate(spans(width, lanes)):
            d_stack = halves(d_out[:, column].astype(bf16), masks)
            d_mixing = nt(d_stack, stepped[:, column])
            mixed, grads = [], []
            for side in range(2):
                head = 2 * pair + side
                faint = fade(decay, decay_t, head, causal)
                d_score = faint * d_mixing[side * chunk : (side + 1) * chunk, :]
                d_scores = d_scores + d_score
                mixed.append((faint * scores).astype(bf16))
                grad = (d_score * scores).astype(bf16)
                grads.append(grad)
                column_buf[head : head + 1, :] = jnp.sum(
                    grad.astype(f32), axis=0, keepdims=True
                )
            code = jnp.where(col_at == 2 * pair + row_at // chunk, 1.0, 0.0).astype(bf16)
            queries = queries + nn(jnp.concatenate(grads, axis=1), code)
            part = tn(jnp.concatenate(mixed, axis=0), d_stack)
            d_x_ref[rows, column] = d_x[:, column] + part
        queries = queries - jnp.transpose(column_buf[...])
        d_decay_ref[rows, :] = summed_by(since, queries) + summed_by(before, keys) + across
        d_scores16 = d_scores.astype(bf16)
        d_shared_ref[rows, 0:states] = d_b + tn(d_scores16, c)
        d_shared_ref[rows, states:] = d_c + nn(d_scores16, b)
        lam = heads[1:2, :] * lam + tn(c, d_faded)


def filter_backward(buffer, taps_ref, start, size, column, taps):
    total = None
    for tap in range(taps):
        term = taps_ref[tap : tap + 1, column] * buffer[
            pl.ds(rim + start + taps - 1 - tap, size), column
        ]
        total = term if total is None else total + term
    return total


def filter_adjoint(buffer, inner_buf, taps_ref, length, width, taps, body_ref, edge_ref, tail_ref,
                   taps_grad_ref):
    for column in spans(width, lanes):
        edge_ref[:, column] = filter_backward(buffer, taps_ref, -rim, rim, column, taps).astype(
            bf16
        )
        rows_grad = [jnp.zeros((8, lanes), f32) for _ in range(taps + 1)]
        for rows in spans(length, chunk):
            body = filter_backward(buffer, taps_ref, rows.start, chunk, column, taps)
            body_ref[rows, column] = body.astype(bf16)
            if rows.stop == length:
                tail_ref[:, column] = body[chunk - rim :, :]
            grad = buffer[pl.ds(rim + rows.start, chunk), column]
            for tap in range(taps):
                moved = inner_buf[pl.ds(rim + rows.start - taps + 1 + tap, chunk), column]
                rows_grad[tap] = rows_grad[tap] + jnp.sum(
                    (grad * moved).reshape(chunk // 8, 8, lanes), axis=0
                )
            rows_grad[taps] = rows_grad[taps] + jnp.sum(
                grad.reshape(chunk // 8, 8, lanes), axis=0
            )
        sums = [jnp.sum(part, axis=0, keepdims=True) for part in rows_grad]
        sums.append(jnp.zeros((8 - taps - 1, lanes), f32))
        taps_grad_ref[:, column] = jnp.concatenate(sums, axis=0)


def finish_kernel(
    x_ref, slope_ref, shared_act_ref, raw_ref, step_ref, decay_ref, d_x_ref, d_shared_ref,
    d_decay_ref, d_ssm_ref, state_in_ref, later_ref, inner_ref, rim_inner_ref,
    taps_ref, step_bias_ref, rate_ref, skip_ref, spread_ref, gather_ref,
    body_ref, edge_ref, tail_ref, taps_grad_ref, d_raw_ref, heads_ref, d_shared_out_ref,
    grad_buf, inner_buf,
    *, taps, states,
):
    length, width = x_ref.shape
    spread, gather = spread_ref[...], gather_ref[...]
    before = triangle_of("before")
    later = later_ref[...]
    grad_buf[0:rim, :] = jnp.zeros((rim, width), f32)
    grad_buf[rim + length :, :] = jnp.zeros((rim, width), f32)
    inner_buf[0:rim, :] = rim_inner_ref[...]
    inner_buf[rim:, :] = inner_ref[...]
    last = decay_ref[length - 1 : length, :]
    final = nn(two_parts(jnp.broadcast_to(jnp.exp(last), (8, lanes))), spread)[0:1, :]
    across = final * jnp.sum(
        later.astype(f32) * state_in_ref[...].astype(f32), axis=0, keepdims=True
    )
    running = nn(jnp.broadcast_to(across, (8, width)).astype(bf16), gather)[0:1, :]
    skip = skip_ref[...]
    skip_grad = jnp.zeros((1, width), f32)
    rate_grad = jnp.zeros((1, lanes), f32)
    bias_grad = jnp.zeros((1, lanes), f32)
    for rows in spans(length, chunk):
        b = shared_act_ref[rows, 0:states]
        x = x_ref[rows, :]
        step = step_ref[rows, :]
        d_ssm = d_ssm_ref[rows, :]
        fading = nn(two_parts(jnp.exp(last - decay_ref[rows, :])), spread)
        steps = nn(two_parts(step), spread)
        carrying = fading * nn(b, later)
        x_stepped = x * steps
        keys = nn((x_stepped * carrying).astype(bf16), gather)
        d_x = d_x_ref[rows, :] + carrying
        direct = nn((x * d_x).astype(bf16), gather)
        d_decay = d_decay_ref[rows, :] + running + summed_by(before, keys)
        running = running + jnp.sum(keys, axis=0, keepdims=True)
        d_shared_out_ref[rows, 0:states] = (
            d_shared_ref[rows, 0:states] + nt((x_stepped * fading).astype(bf16), later)
        )
        d_shared_out_ref[rows, states:] = d_shared_ref[rows, states:]
        skip_grad = skip_grad + jnp.sum(d_ssm * x, axis=0, keepdims=True)
        rate_grad = rate_grad + jnp.sum(step * d_decay, axis=0, keepdims=True)
        d_raw = (direct + rate_ref[...] * d_decay) * sigmoid(
            raw_ref[rows, :] + step_bias_ref[...]
        )
        d_raw_ref[rows, :] = d_raw.astype(bf16)
        bias_grad = bias_grad + jnp.sum(d_raw, axis=0, keepdims=True)
        grad_buf[pl.ds(rim + rows.start, chunk), :] = (
            skip * d_ssm + steps * d_x
        ) * slope_ref[rows, :].astype(f32)
    parts = two_parts(jnp.broadcast_to(skip_grad, (8, width)))
    skip_heads = nn(parts[:, :width], gather) + nn(parts[:, width:], gather)
    heads_ref[...] = jnp.concatenate(
        [bias_grad, rate_grad * rate_ref[...], skip_heads[0:1, :], jnp.zeros((5, lanes), f32)],
        axis=0,
    )
    filter_adjoint(
        grad_buf, inner_buf, taps_ref, length, width, taps, body_ref, edge_ref, tail_ref,
        taps_grad_ref,
    )


def shared_kernel(
    d_act_ref, slope_ref, shared_ref, rim_ref, taps_ref,
    body_ref, edge_ref, tail_ref, taps_grad_ref,
    grad_buf, inner_buf,
    *, taps,
):
    length, width = d_act_ref.shape
    grad_buf[0:rim, :] = jnp.zeros((rim, width), f32)
    grad_buf[rim + length :, :] = jnp.zeros((rim, width), f32)
    inner_buf[0:rim, :] = rim_ref[...]
    inner_buf[rim:, :] = shared_ref[...]
    grad_buf[rim : rim + length, :] = d_act_ref[...] * slope_ref[...]
    filter_adjoint(
        grad_buf, inner_buf, taps_ref, length, width, taps, body_ref, edge_ref, tail_ref,
        taps_grad_ref,
    )


def chain_kernel(pieces_ref, totals_ref, spread_ref, out_ref, *, backward):
    count = pieces_ref.shape[0]
    decays = nn(two_parts(jnp.exp(totals_ref[...])), spread_ref[...])
    state = jnp.zeros(pieces_ref.shape[1:], f32)
    order = reversed(range(count)) if backward else range(count)
    for block in order:
        out_ref[block, :, :] = state.astype(bf16)
        state = decays[block : block + 1, :] * state + pieces_ref[block].astype(f32)


def after(ready, *values):
    if not ready:
        return values if len(values) > 1 else values[0]
    tied = lax.optimization_barrier((tuple(ready), tuple(values)))[1]
    return tied if len(values) > 1 else tied[0]


def landed(ready, *transfers):
    flat = [value for transfer in transfers for value in transfer]
    flat = list(lax.optimization_barrier((tuple(ready), tuple(flat)))[1])
    return [[flat.pop(0) for _ in transfer] for transfer in transfers]


def bits_of(axis):
    return [1 << bit for bit in range(lax.axis_size(axis).bit_length() - 1)]


def swapped(value, axis, bit):
    size = lax.axis_size(axis)
    return lax.ppermute(value, axis, [(i, i ^ bit) for i in range(size)])


def passed_along(value, axis, by):
    size = lax.axis_size(axis)
    pairs = [(i, i + by) for i in range(size) if 0 <= i + by < size]
    return lax.ppermute(value, axis, pairs)


def block_at(value, index, size, dim):
    return lax.dynamic_slice_in_dim(value, index * size, size, dim)


def reversed_order(axis):
    order = [0]
    for bit in reversed(bits_of(axis)):
        order = order + [at + bit for at in order]
    return order


def relative_blocks(value, axis, dim):
    count, mine = lax.axis_size(axis), lax.axis_index(axis)
    size = value.shape[dim] // count
    blocks = [block_at(value, mine ^ other, size, dim) for other in reversed_order(axis)]
    half = len(blocks) // 2
    return [
        jnp.concatenate(blocks[:half], axis=dim),
        jnp.concatenate(blocks[half:], axis=dim),
    ]


def gathered_relative(value, axis, dim, ready=()):
    for bit in reversed(bits_of(axis)):
        value = jnp.concatenate([value, after(ready, swapped(value, axis, bit))], axis=dim)
    return value


def halves_added(kept, got, dim):
    half = got.shape[dim] // 2
    parts = [
        lax.slice_in_dim(value, at * half, (at + 1) * half, axis=dim)
        for at in range(2)
        for value in (kept, got)
    ]
    return parts[0].astype(f32) + parts[1].astype(f32), parts[2].astype(f32) + parts[3].astype(f32)


def in_place_order(value, axis, dim):
    count, mine = lax.axis_size(axis), lax.axis_index(axis)
    size = value.shape[dim] // count
    bits = bits_of(axis)

    def place(at):
        return sum(((at // bit) % 2) * back for bit, back in zip(bits, reversed(bits)))

    return jnp.concatenate(
        [block_at(value, place(mine ^ other), size, dim) for other in range(count)], axis=dim
    )


def rank_in(axis, group):
    mine = lax.axis_index(axis)
    return sum(((mine // bit) % 2) << at for at, bit in enumerate(group))


def mask_of(group, distance):
    return sum(bit for at, bit in enumerate(group) if distance >> at & 1)


class Reduction:
    def __init__(self, value, axis, groups, wire=bf16, halves=None):
        self.axis, self.wire, self.value = axis, wire, value
        self.left, self.taken = list(groups), []
        if halves is None:
            self.split()
        else:
            self.kept, self.sent = halves[0], [halves[1]]

    def split(self):
        if self.left:
            count = 1 << len(self.left[0])
            rank = rank_in(self.axis, self.left[0])
            size = self.value.shape[0] // count
            self.kept = block_at(self.value, rank, size, 0)
            self.sent = [
                block_at(self.value, rank ^ other, size, 0).astype(self.wire)
                for other in range(1, count)
            ]
        else:
            self.value = self.value.astype(bf16)
            self.sent = [self.value]

    def start(self):
        group = self.left[0] if self.left else self.taken[-1]
        count = 1 << len(group)
        sent = self.sent if self.left else self.sent * (count - 1)
        return [
            swapped(value, self.axis, mask_of(group, other))
            for other, value in enumerate(sent, 1)
        ]

    def take(self, got):
        if self.left:
            self.taken.append(self.left.pop(0))
            total = self.kept.astype(f32)
            for value in got:
                total = total + value.astype(f32)
            self.value = total.astype(self.wire)
        else:
            group = self.taken.pop()
            count = 1 << len(group)
            rank = rank_in(self.axis, group)
            if count == 2:
                low = rank == 0
                self.value = jnp.concatenate(
                    [jnp.where(low, self.value, got[0]), jnp.where(low, got[0], self.value)]
                )
            else:
                size = self.value.shape[0]
                whole = jnp.zeros((count * size,) + self.value.shape[1:], bf16)
                for other, value in enumerate([self.value] + got):
                    whole = lax.dynamic_update_slice_in_dim(
                        whole, value, (rank ^ other) * size, 0
                    )
                self.value = whole
        if self.left or self.taken:
            self.split()
        else:
            self.sent = [self.value]
        return self.sent


def exchanged_sum(value, axis):
    for bit in bits_of(axis):
        value = (value.astype(f32) + swapped(value, axis, bit).astype(f32)).astype(value.dtype)
    return value


def exchanged_all(value, axis):
    mine = lax.axis_index(axis)
    value = value[None]
    for bit in bits_of(axis):
        got = swapped(value, axis, bit)
        low = (mine // bit) % 2 == 0
        value = jnp.concatenate([jnp.where(low, value, got), jnp.where(low, got, value)], axis=0)
    return value


def to_owners(state):
    count, width = lax.axis_size("seq"), state.shape[-1]
    return [lax.all_to_all(state.reshape(count, -1, width), "seq", 0, 0, tiled=True)]


def chained(pieces, totals, states, spread, backward):
    count, size, width = pieces.shape
    mine = lax.axis_index("seq")
    here = lax.dynamic_index_in_dim(totals, mine * size // states, 1, keepdims=False)
    params, cost = cheap(10**5)
    return pl.pallas_call(
        functools.partial(chain_kernel, backward=backward),
        out_shape=jax.ShapeDtypeStruct((count, size, width), bf16),
        compiler_params=pltpu.CompilerParams(vmem_limit_bytes=vmem_limit),
        cost_estimate=cost,
    )(pieces, here, spread)


def to_blocks(scanned):
    return [lax.all_to_all(scanned, "seq", 0, 0, tiled=True)]


def on_device(
    hidden_in, norm_gain, proj_gate, proj_inner, proj_step, proj_shared, filter_inner,
    filter_inner_bias, filter_shared, filter_shared_bias, step_bias, log_rate, skip_gain,
    gate_gain, proj_out, cotangent,
):
    seqs, length, width_d = hidden_in.shape
    width = proj_gate.shape[1]
    heads = proj_step.shape[1]
    per_head = width // heads
    states = proj_shared.shape[1] // 2
    taps = filter_inner.shape[0]
    count_h = lax.axis_size("head")
    mine_h = lax.axis_index("head")
    full = width * count_h
    columns = width_d // count_h
    tokens = seqs * length
    per_device_seqs = seqs // count_h

    spread_np = np.zeros((2 * lanes, width), np.float32)
    for head in range(heads):
        spread_np[head, head * per_head : (head + 1) * per_head] = 1
        spread_np[lanes + head, head * per_head : (head + 1) * per_head] = 1
    spread = jnp.asarray(spread_np, bf16)
    gather = jnp.asarray(spread_np[:lanes].T, bf16)

    def on_lanes(vector):
        return jnp.pad(vector.astype(f32), (0, lanes - heads)).reshape(1, lanes)

    rate = on_lanes(-jnp.exp(log_rate))
    bias_row = on_lanes(step_bias)
    skip_row = jnp.repeat(skip_gain, per_head).reshape(1, width)
    gain_row = gate_gain.reshape(1, width)

    shape = jax.ShapeDtypeStruct
    wide = per_seq(length, width)
    narrow = per_seq(length, 2 * states)
    slim = per_seq(length, lanes)
    slim_t = per_seq(16, length)
    state_spec = per_seq(states, width)
    chunks = length // chunk

    normed, inner_pre, shared_pre, step_raw, inv_rms, end_inner, end_shared = grid_call(
        project_kernel,
        seqs,
        [
            per_seq(length, width_d), whole((1, width_d)), whole((width_d, width)),
            whole((width_d, 2 * states)), whole((heads, width_d)),
        ],
        [
            per_seq(length, width_d), wide, narrow, slim, slim, per_seq(rim, width),
            per_seq(rim, 2 * states),
        ],
        [
            shape((seqs, length, width_d), bf16),
            shape((seqs, length, width), f32),
            shape((seqs, length, 2 * states), f32),
            shape((seqs, length, lanes), f32),
            shape((seqs, length, lanes), f32),
            shape((seqs, rim, width), f32),
            shape((seqs, rim, 2 * states), f32),
        ],
        [],
        10**5,
    )(
        hidden_in, norm_gain.reshape(1, width_d), proj_inner, proj_shared, proj_step.T,
    )
    normed = normed.reshape(tokens, width_d)
    rim_inner = passed_along(end_inner, "seq", 1)
    rim_shared = passed_along(end_shared, "seq", 1)

    x, slope, shared_act, slope_s, step, decay, decay_t, local, total, state = grid_call(
        functools.partial(states_kernel, taps=taps, states=states),
        seqs,
        [
            wide, per_seq(rim, width), narrow, per_seq(rim, 2 * states), slim,
            whole((taps, width)), whole((1, width)), whole((taps, 2 * states)),
            whole((1, 2 * states)), whole((1, lanes)), whole((1, lanes)), whole((2 * lanes, width)),
        ],
        [
            wide, wide, narrow, narrow, slim, slim, slim_t, per_seq(chunks, states, width),
            per_seq(8, lanes), state_spec,
        ],
        [
            shape((seqs, length, width), f32),
            shape((seqs, length, width), bf16),
            shape((seqs, length, 2 * states), bf16),
            shape((seqs, length, 2 * states), f32),
            shape((seqs, length, lanes), f32),
            shape((seqs, length, lanes), f32),
            shape((seqs, 16, length), f32),
            shape((seqs, chunks, states, width), bf16),
            shape((seqs, 8, lanes), f32),
            shape((seqs, states, width), bf16),
        ],
        [
            pltpu.VMEM((rim + length, width), f32),
            pltpu.VMEM((rim + length, 2 * states), f32),
            pltpu.VMEM((chunk, width), bf16),
        ],
        10**5,
    )(
        inner_pre, rim_inner, shared_pre, rim_shared, step_raw, filter_inner,
        filter_inner_bias.reshape(1, width), filter_shared,
        filter_shared_bias.reshape(1, 2 * states), bias_row, rate, spread,
    )
    local_out = grid_call(
        functools.partial(mix_kernel, states=states),
        seqs,
        [
            wide, narrow, slim, slim, slim_t, per_seq(chunks, states, width), whole((1, width)),
            whole((2 * lanes, width)),
        ],
        wide,
        shape((seqs, length, width), f32),
        [],
        10**5,
    )(x, shared_act, step, decay, decay_t, local, skip_row, spread)

    cot_near = after([state], cotangent.reshape(tokens, columns))
    totals = exchanged_all(after([local_out], total[:, 0, :]), "seq")
    (pieces,), (cot_far,) = landed(
        [totals], to_owners(state), [swapped(cot_near, "head", bits_of("head")[-1])]
    )
    scanned = chained(pieces, totals, states, spread, False)
    cot_all = jnp.concatenate([cot_near, cot_far], axis=1)
    for bit in reversed(bits_of("head")[:-1]):
        cot_all = jnp.concatenate([cot_all, swapped(cot_all, "head", bit)], axis=1)
    gate_pre = nn(after([scanned], normed), proj_gate).reshape(seqs, length, width)
    out_kept, out_sent = relative_blocks(after([scanned], proj_out), "head", 1)
    out_kept, out_sent = after([gate_pre], out_kept, out_sent)
    middle = cot_all.shape[1] // 2
    mixer_grad = nt(cot_all[:, :middle], out_kept) + nt(cot_all[:, middle:], out_sent)
    mixer_grad = mixer_grad.reshape(seqs, length, width)
    ((state_in,),) = landed([gate_pre, mixer_grad], to_blocks(scanned))
    cot_all = after([gate_pre], cot_all)
    state_in = state_in.reshape(seqs, states, width)

    ssm_out, sums = grid_call(
        functools.partial(gate_kernel, states=states),
        seqs,
        [
            wide, narrow, slim, state_spec, wide, wide, whole((1, width)),
            whole((2 * lanes, width)),
        ],
        [wide, per_seq(8, length)],
        [shape((seqs, length, width), f32), shape((seqs, 8, length), f32)],
        [pltpu.VMEM((length, width), bf16), pltpu.VMEM((length, width), bf16)],
        10**5,
    )(local_out, shared_act, decay, state_in, gate_pre, mixer_grad, gain_row, spread)
    sums_all = lax.all_gather(sums, "head")

    mixer_in, d_gate, d_ssm, lam, gain_grad = grid_call(
        functools.partial(gate_back_kernel, states=states, full=float(full)),
        seqs,
        [
            wide, wide, wide,
            pl.BlockSpec((count_h, None, 8, length), lambda s: (0, s, 0, 0)),
            whole((1, width)), narrow, slim, whole((2 * lanes, width)),
        ],
        [wide, wide, wide, state_spec, per_seq(8, width)],
        [
            shape((seqs, length, width), bf16),
            shape((seqs, length, width), bf16),
            shape((seqs, length, width), f32),
            shape((seqs, states, width), bf16),
            shape((seqs, 8, width), f32),
        ],
        [],
        10**5,
    )(ssm_out, gate_pre, mixer_grad, sums_all, gain_row, shared_act, decay, spread)

    mixer_flat = mixer_in.reshape(tokens, width)
    d_gate_flat = d_gate.reshape(tokens, width)
    bits = bits_of("seq")
    groups = [bits[:1], bits[1:]]

    def in_parts(left, right, first, rows, ready):
        half, upper = rows // 2, rank_in("seq", bits[:1])
        far = product(tn, after(ready, left), right, bf16, first + (1 - upper) * half, half)
        near = product(tn, after([far], left), right, bf16, first + upper * half, half)
        return near, far

    near_bit, far_bit = bits_of("head")
    out_parts = in_parts(mixer_flat, cot_all, 0, width, ())
    out_sum = Reduction(None, "seq", groups, halves=out_parts)
    gate_parts = in_parts(normed, d_gate_flat, 0, width_d, out_parts[:1])
    gate_sum = Reduction(None, "seq", groups, halves=gate_parts)

    def mix_back(first, count, d_ssm, into):
        def at(*dims):
            return per_seq(*dims, first=first)

        wide, narrow, slim = at(length, width), at(length, 2 * states), at(length, lanes)
        return grid_call(
            functools.partial(mix_back_kernel, states=states),
            count,
            [
                wide, narrow, slim, slim, at(16, length), at(chunks, states, width),
                at(states, width), wide, whole((2 * lanes, width)), whole((width, lanes)),
            ],
            [wide, narrow, slim],
            [
                shape((seqs, length, width), f32),
                shape((seqs, length, 2 * states), f32),
                shape((seqs, length, lanes), f32),
            ],
            [pltpu.VMEM((lanes, chunk), f32)],
            10**5,
            into,
        )(x, shared_act, step, decay, decay_t, local, state_in, d_ssm, spread, gather)

    quarter = seqs // 4
    back_parts = mix_back(0, quarter, after(gate_parts[:1], d_ssm), ())
    (pieces,), got = landed([back_parts[2]], to_owners(lam), out_sum.start())
    scanned = chained(pieces, totals, states, spread, True)
    ready = [scanned] + out_sum.take(got) + gate_sum.sent
    back_parts = mix_back(quarter, seqs - quarter, after(ready, d_ssm), back_parts)
    d_x, d_shared, d_decay = back_parts
    sent_out = product(nn, after([d_decay], mixer_flat), out_sent, bf16)
    kept_out = product(nn, after([sent_out], mixer_flat), out_kept, bf16)
    (later,), got, got_gate = landed(
        [kept_out], to_blocks(scanned), out_sum.start(), gate_sum.start()
    )
    later = later.reshape(seqs, states, width)
    out_sum.take(got)
    ready = gate_sum.take(got_gate)
    sent_out = after(ready, sent_out)

    def finish(first, count, later, into):
        def at(*dims):
            return per_seq(*dims, first=first)

        wide, narrow, slim = at(length, width), at(length, 2 * states), at(length, lanes)
        state_spec = at(states, width)
        return grid_call(
            functools.partial(finish_kernel, taps=taps, states=states),
            count,
            [
                wide, wide, narrow, slim, slim, slim, wide, narrow, slim, wide, state_spec, state_spec,
                wide, at(rim, width), whole((taps, width)), whole((1, lanes)), whole((1, lanes)),
                whole((1, width)), whole((2 * lanes, width)), whole((width, lanes)),
            ],
            [
                wide, at(rim, width), at(rim, width), at(8, width), slim,
                at(8, lanes), narrow,
            ],
            [
                shape((seqs, length, width), bf16),
                shape((seqs, rim, width), bf16),
                shape((seqs, rim, width), f32),
                shape((seqs, 8, width), f32),
                shape((seqs, length, lanes), bf16),
                shape((seqs, 8, lanes), f32),
                shape((seqs, length, 2 * states), f32),
            ],
            [
                pltpu.VMEM((2 * rim + length, width), f32),
                pltpu.VMEM((rim + length, width), f32),
            ],
            10**5,
            into,
        )(
            x, slope, shared_act, step_raw, step, decay, d_x, d_shared, d_decay, d_ssm, state_in,
            later, inner_pre, rim_inner, filter_inner, bias_row, rate, skip_row, spread, gather,
        )


    body, edge, tail, taps_grad, d_raw, heads_grad, d_act = finish(
        0, seqs, after(ready, later), ()
    )

    def joined(body, edge, tail):
        ends = (tail + passed_along(edge, "seq", -1).astype(f32)).astype(bf16)
        return lax.dynamic_update_slice_in_dim(body, ends, length - rim, 1)

    d_act_kept, d_act_sent = relative_blocks(d_act, "head", 0)
    got, (got_out,) = landed(
        [body], gate_sum.start(), [swapped(sent_out, "head", near_bit)]
    )
    mixed, sent_out = halves_added(kept_out, got_out, 1)
    sent_out = sent_out.astype(bf16)
    ready = gate_sum.take(got) + [sent_out]
    step_grad = product(tn, after(ready, d_raw.reshape(tokens, lanes)), normed, f32)
    (edge,), (got_act,) = landed(
        [step_grad], [passed_along(edge, "seq", -1)], [swapped(d_act_sent, "head", near_bit)]
    )
    d_act_kept, d_act_sent = halves_added(d_act_kept, got_act, 0)

    def joined(body, edge, tail):
        ends = (tail + edge.astype(f32)).astype(bf16)
        return lax.dynamic_update_slice_in_dim(body, ends, length - rim, 1)

    d_inner = joined(body, edge, tail)
    d_inner_flat = d_inner.reshape(tokens, width)
    inner_parts = in_parts(normed, d_inner_flat, 0, width_d, [d_inner, d_act_sent])
    inner_sum = Reduction(None, "seq", groups, halves=inner_parts)
    (got_act,), got, (got_out,) = landed(
        inner_parts[:1], [swapped(d_act_sent, "head", far_bit)], out_sum.start(),
        [swapped(sent_out, "head", far_bit)],
    )
    ready = out_sum.take(got)
    mixed = (mixed + got_out.astype(f32)).reshape(seqs, length, columns)
    blocks = [mine_h ^ other for other in reversed_order("head")]
    middle = len(blocks) // 2
    step_rows = jnp.pad(after([d_inner], proj_step).T, ((0, 16 - heads), (0, 0)))
    ready, back = ready + [step_rows], []
    for picked in (blocks[middle:], blocks[:middle]):
        back.append(
            back_product(
                jnp.stack(picked), columns, d_gate, after(ready, d_inner), d_raw, proj_gate,
                proj_inner, step_rows, bf16,
            )
        )
        ready = back[-1:]
    got, got_gate = landed(ready, inner_sum.start(), gate_sum.start())
    ready = inner_sum.take(got) + gate_sum.take(got_gate)
    back = list(after(ready, *back))

    d_act_own = d_act_kept + got_act
    own = [
        block_at(value, mine_h, per_device_seqs, 0)
        for value in after(ready, slope_s, shared_pre, rim_shared)
    ]
    s_body, s_edge, s_tail, s_taps_grad = grid_call(
        functools.partial(shared_kernel, taps=taps),
        per_device_seqs,
        [narrow, narrow, narrow, per_seq(rim, 2 * states), whole((taps, 2 * states))],
        [narrow, per_seq(rim, 2 * states), per_seq(rim, 2 * states), per_seq(8, 2 * states)],
        [
            shape((per_device_seqs, length, 2 * states), bf16),
            shape((per_device_seqs, rim, 2 * states), bf16),
            shape((per_device_seqs, rim, 2 * states), f32),
            shape((per_device_seqs, 8, 2 * states), f32),
        ],
        [
            pltpu.VMEM((2 * rim + length, 2 * states), f32),
            pltpu.VMEM((rim + length, 2 * states), f32),
        ],
        10**5,
    )(after(ready, d_act_own), own[0], own[1], own[2], filter_shared)
    (s_edge,), (got_back,) = landed(
        [s_body], [passed_along(s_edge, "seq", -1)], [swapped(back[0], "head", near_bit)]
    )
    d_normed, back_sent = halves_added(back[1], got_back, 1)
    back_sent = back_sent.astype(bf16)
    s_edge = after([back_sent], s_edge)
    taps_rows = jnp.zeros((per_device_seqs, rim, 2 * states), bf16)
    taps_rows = lax.dynamic_update_slice(taps_rows, s_taps_grad.astype(bf16), (0, 0, 0))
    d_shared_all = jnp.concatenate([joined(s_body, s_edge, s_tail), taps_rows], axis=1)
    d_shared_all = gathered_relative(d_shared_all, "head", 0)
    d_shared_all = in_place_order(d_shared_all, "head", 0)
    s_taps_sum = jnp.sum(d_shared_all[:, length:].astype(f32), axis=0)
    d_shared_flat = d_shared_all[:, :length].reshape(tokens, 2 * states)
    shared_rows = product(tn, normed, d_shared_flat, f32, mine_h * columns, columns)
    shared_rows = jnp.concatenate([shared_rows, s_taps_sum[:8], jnp.zeros((16, 2 * states), f32)])

    got, got_out, (got_back,) = landed(
        [shared_rows], inner_sum.start(), out_sum.start(),
        [swapped(back_sent, "head", far_bit)],
    )
    ready = inner_sum.take(got)
    out_sum.take(got_out)
    d_normed = after(ready, d_normed) + got_back.astype(f32)
    d_normed = d_normed + nt(d_shared_flat, block_at(proj_shared, mine_h, columns, 0))
    d_normed = d_normed.reshape(seqs, length, columns)
    ready = ready + [shared_rows]
    hidden_own = block_at(after(ready, hidden_in), mine_h, columns, 2).astype(f32)
    activations = (hidden_own + mixed).astype(bf16)
    scaled = d_normed * block_at(after(ready, norm_gain), mine_h, columns, 0)
    norm_row = jnp.sum(scaled * hidden_own, axis=-1)
    inv_rms = after(ready, inv_rms)[:, :, :1]
    norm_row = jnp.sum(lax.all_gather(norm_row, "head"), axis=0)[..., None] / width_d
    grad_input = (
        cotangent.astype(f32)
        + inv_rms * scaled
        - hidden_own * inv_rms * inv_rms * inv_rms * norm_row
    )
    norm_gain_grad = jnp.sum(d_normed * hidden_own * inv_rms, axis=(0, 1))

    step_grad, taps_grad, gain_grad, heads_grad = after(
        ready, step_grad, taps_grad, gain_grad, heads_grad
    )
    step_grad = step_grad[:16].reshape(32, width_d // 2)
    rows_small = jnp.concatenate(
        [
            jnp.sum(taps_grad, axis=0),
            jnp.sum(gain_grad, axis=0)[:1],
            jnp.pad(jnp.sum(heads_grad, axis=0)[:3], ((0, 0), (0, width - lanes))),
            jnp.zeros((4, width), f32),
        ],
        axis=0,
    )
    part = shared_rows.shape[0] * 2 * states // width
    shared_wide = jnp.concatenate(
        [shared_rows[at * part : (at + 1) * part] for at in range(width // (2 * states))], axis=1
    )
    small = jnp.concatenate([rows_small, step_grad, shared_wide], axis=0)
    count = lax.axis_size("seq")
    small = jnp.pad(small, ((0, -small.shape[0] % (8 * count)), (0, 0)))
    small = lax.all_to_all(small.reshape(count, -1, width), "seq", 0, 0, tiled=True)
    small = jnp.broadcast_to(jnp.sum(small, axis=0, keepdims=True).astype(bf16), small.shape)
    small = lax.all_to_all(small, "seq", 0, 0, tiled=True).astype(f32).reshape(-1, width)
    norm_gain_grad = exchanged_sum(norm_gain_grad, "seq")
    step_out = small[16:48].reshape(16, width_d)[:heads].T
    shared_back = jnp.concatenate(
        [
            small[48 : 48 + part, at * 2 * states : (at + 1) * 2 * states]
            for at in range(width // (2 * states))
        ],
        axis=0,
    ).astype(bf16)
    shared_full = in_place_order(gathered_relative(shared_back[None], "head", 0), "head", 0)
    shared_full = shared_full.astype(f32)
    shared_out = shared_full[:, :columns].reshape(width_d, 2 * states)
    shared_extra = shared_full[0, columns : columns + 8]

    out_grad = in_place_order(out_sum.value, "head", 1).astype(f32)
    got, got_gate = landed([grad_input, norm_gain_grad], inner_sum.start(), gate_sum.start())
    ready = inner_sum.take(got)
    gate_out = gate_sum.take(got_gate)[0].astype(f32)
    out_grad, gate_out, small = after(ready, out_grad, gate_out, small)
    ((*got,),) = landed([out_grad, gate_out, small], inner_sum.start())
    inner_out = inner_sum.take(got)[0].astype(f32)
    return (
        activations,
        grad_input,
        norm_gain_grad,
        gate_out,
        inner_out,
        step_out,
        shared_out,
        small[:taps],
        small[taps],
        shared_extra[:taps],
        shared_extra[taps],
        small[9, :heads],
        small[10, :heads],
        small[11, :heads],
        small[8],
        out_grad,
    )


def solution(mesh):
    in_specs = (
        P(None, "seq", None),
        P(),
        P(None, "head"),
        P(None, "head"),
        P(None, "head"),
        P(),
        P(None, "head"),
        P("head"),
        P(),
        P(),
        P("head"),
        P("head"),
        P("head"),
        P("head"),
        P("head", None),
        P(None, "seq", "head"),
    )
    out_specs = (
        P(None, "seq", "head"),
        P(None, "seq", "head"),
        P("head"),
        P(None, "head"),
        P(None, "head"),
        P(None, "head"),
        P(),
        P(None, "head"),
        P("head"),
        P(),
        P(),
        P("head"),
        P("head"),
        P("head"),
        P("head"),
        P("head", None),
    )
    return jax.shard_map(
        on_device, mesh=mesh, in_specs=in_specs, out_specs=out_specs, check_vma=False
    )
```

```python
import functools

import jax
import jax.numpy as jnp
import numpy as np
from jax import lax
from jax.experimental import pallas as pl
from jax.experimental.pallas import tpu as pltpu
from jax.sharding import PartitionSpec as P

epsilon = 1e-05
lanes = 128
chunk = 128
rim = 16
f32 = jnp.float32
bf16 = jnp.bfloat16
vmem_limit = 56 * 1024 * 1024


def nn(left, right):
    return jnp.dot(left, right, preferred_element_type=f32)


def nt(left, right):
    return lax.dot_general(left, right, (((1,), (1,)), ((), ())), preferred_element_type=f32)


def tn(left, right):
    return lax.dot_general(left, right, (((0,), (0,)), ((), ())), preferred_element_type=f32)


def two_parts(value):
    high = value.astype(bf16)
    return jnp.concatenate([high, (value - high.astype(f32)).astype(bf16)], axis=1)


def three_parts(value):
    high = value.astype(bf16)
    rest = value - high.astype(f32)
    middle = rest.astype(bf16)
    low = (rest - middle.astype(f32)).astype(bf16)
    return jnp.concatenate([high, middle, low], axis=1)


def summed_by(triangle, value):
    parts = nn(triangle, three_parts(value))
    return parts[:, :lanes] + parts[:, lanes : 2 * lanes] + parts[:, 2 * lanes :]


def iota(shape, dim):
    return lax.broadcasted_iota(jnp.int32, shape, dim)


def triangle_of(kind):
    row, col = iota((chunk, chunk), 0), iota((chunk, chunk), 1)
    keep = {"upto": row >= col, "from": row <= col, "before": row > col}[kind]
    return jnp.where(keep, 1.0, 0.0).astype(bf16)


def sigmoid(value):
    return 0.5 * jnp.tanh(0.5 * value) + 0.5


def softplus(value):
    return jnp.maximum(value, 0.0) + jnp.log1p(jnp.exp(-jnp.abs(value)))


def whole(shape):
    return pl.BlockSpec(shape, lambda s: (0,) * len(shape))


def per_seq(*dims, first=0):
    return pl.BlockSpec((None,) + dims, lambda s: (s + first,) + (0,) * len(dims))


def grid_call(kernel, seqs, in_specs, out_specs, out_shape, scratch, cost, into=()):
    given = len(in_specs)

    def filling(*refs):
        kernel(*refs[:given], *refs[given + len(into) :])

    call = pl.pallas_call(
        filling,
        grid=(seqs,),
        in_specs=in_specs + [pl.BlockSpec(memory_space=pl.ANY)] * len(into),
        input_output_aliases={given + at: at for at in range(len(into))},
        out_specs=out_specs,
        out_shape=out_shape,
        scratch_shapes=scratch,
        compiler_params=pltpu.CompilerParams(
            vmem_limit_bytes=vmem_limit, dimension_semantics=("arbitrary",)
        ),
        cost_estimate=pl.CostEstimate(flops=cost, bytes_accessed=cost, transcendentals=0),
    )
    return lambda *operands: call(*operands, *into)


def cheap(width):
    return pltpu.CompilerParams(vmem_limit_bytes=vmem_limit, dimension_semantics=("arbitrary",)), (
        pl.CostEstimate(flops=width, bytes_accessed=width, transcendentals=0)
    )


def product_kernel(at_ref, left_ref, *refs, dot):
    *right_refs, out_ref = refs
    width = out_ref.shape[1] // len(right_refs)
    for at, right_ref in enumerate(right_refs):
        part = dot(left_ref[...], right_ref[...])
        out_ref[:, at * width : (at + 1) * width] = part.astype(out_ref.dtype)


def product(dot, left, right, dtype, start=0, rows=None):
    depth, total = left.shape if dot is tn else left.shape[::-1]
    rows = total if rows is None else rows
    size = rows // 2 if rows % 256 == 0 else rows
    rights = list(right) if isinstance(right, (list, tuple)) else [right]
    cols = rights[0].shape[0] if dot is nt else rights[0].shape[1]
    cols = cols * len(rights)
    if dot is tn:
        left_spec = pl.BlockSpec((depth, size), lambda i, at: (0, at[0] + i))
    else:
        left_spec = pl.BlockSpec((size, depth), lambda i, at: (at[0] + i, 0))
    params, cost = cheap(10**5)
    return pl.pallas_call(
        functools.partial(product_kernel, dot=dot),
        grid_spec=pltpu.PrefetchScalarGridSpec(
            num_scalar_prefetch=1,
            grid=(rows // size,),
            in_specs=[left_spec]
            + [pl.BlockSpec(one.shape, lambda i, at: (0, 0)) for one in rights],
            out_specs=pl.BlockSpec((size, cols), lambda i, at: (i, 0)),
        ),
        out_shape=jax.ShapeDtypeStruct((rows, cols), dtype),
        compiler_params=params,
        cost_estimate=cost,
    )(jnp.asarray(start // size, jnp.int32).reshape(1), left, *rights)


def rows_kernel(taps_grad_ref, gain_grad_ref, heads_grad_ref, step_grad_ref, out_ref, rows_buf):
    width = rows_buf.shape[1]
    rows_buf[...] = jnp.zeros_like(rows_buf)
    rows_buf[0:8, :] = jnp.sum(taps_grad_ref[...], axis=0)
    rows_buf[8:9, :] = jnp.sum(gain_grad_ref[...], axis=0)[0:1, :]
    rows_buf[9:12, 0:lanes] = jnp.sum(heads_grad_ref[...], axis=0)[0:3, :]
    for at, column in enumerate(spans(step_grad_ref.shape[1], width)):
        rows_buf[16 * (at + 1) : 16 * (at + 2), :] = step_grad_ref[0:16, column]
    wide = out_ref.shape[1]
    for at in range(rows_buf.shape[0] // 8):
        for part, column in enumerate(spans(width, wide)):
            first = (at * (width // wide) + part) * 8
            out_ref[first : first + 8, :] = rows_buf[8 * at : 8 * at + 8, column]


def pieces_kernel(*refs):
    *pairs, out_ref = refs
    count = len(pairs) // 2
    out = nt(pairs[0][...], pairs[count][...])
    for at in range(1, count):
        out = out + nt(pairs[at][...], pairs[count + at][...])
    out_ref[...] = out.astype(out_ref.dtype)


def pieces_product(lefts, rights, dtype):
    tokens, cols = lefts[0].shape[0], rights[0].shape[0]
    size = tokens // 4
    params, cost = cheap(10**5)
    return pl.pallas_call(
        pieces_kernel,
        grid=(tokens // size,),
        in_specs=[pl.BlockSpec((size, left.shape[1]), lambda i: (i, 0)) for left in lefts]
        + [pl.BlockSpec(right.shape, lambda i: (0, 0)) for right in rights],
        out_specs=pl.BlockSpec((size, cols), lambda i: (i, 0)),
        out_shape=jax.ShapeDtypeStruct((tokens, cols), dtype),
        compiler_params=params,
        cost_estimate=cost,
    )(*lefts, *rights)


def shared_grad_kernel(own_ref, normed_ref, d_shared_ref, taps_grad_ref, out_ref):
    rows, (padded, wide) = normed_ref.shape[1], out_ref.shape
    out_ref[0:rows, :] = tn(normed_ref[...], d_shared_ref[...])
    out_ref[rows:, :] = jnp.zeros((padded - rows, wide), f32)

    @pl.when(pl.program_id(0) == 0)
    def _():
        out_ref[rows : rows + 8, :] = taps_grad_ref[...]


def shared_product(own, normed, d_shared, taps_grad, count, padded):
    tokens, wide = d_shared.shape
    rows = normed.shape[1] // count
    params, cost = cheap(10**5)
    return pl.pallas_call(
        shared_grad_kernel,
        grid_spec=pltpu.PrefetchScalarGridSpec(
            num_scalar_prefetch=1,
            grid=(count,),
            in_specs=[
                pl.BlockSpec((tokens, rows), lambda i, own: (own[0], i)),
                pl.BlockSpec((tokens, wide), lambda i, own: (0, 0)),
                pl.BlockSpec((8, wide), lambda i, own: (0, 0)),
            ],
            out_specs=pl.BlockSpec((padded, wide), lambda i, own: (i, 0)),
        ),
        out_shape=jax.ShapeDtypeStruct((count * padded, wide), f32),
        compiler_params=params,
        cost_estimate=cost,
    )(own.reshape(1), normed, d_shared, taps_grad)


def back_kernel(
    blocks_ref, gate_ref, inner_ref, raw_ref, shared_ref, *refs, parts, per_device,
):
    weight_refs, out_ref, buffers = refs[: 4 * parts], refs[4 * parts], refs[4 * parts + 1 :]
    size = weight_refs[0].shape[0]

    @pl.when(pl.program_id(0) == 0)
    def _():
        for part in range(parts):
            rows = slice(part * size, (part + 1) * size)
            buffers[0][rows, :] = weight_refs[part][...]
            buffers[1][rows, :] = weight_refs[parts + part][...]
            buffers[2][:, rows] = weight_refs[2 * parts + part][...]
            buffers[3][rows, :] = weight_refs[3 * parts + part][...]

    out = nt(gate_ref[...], buffers[0][...]) + nt(inner_ref[...], buffers[1][...])
    out = out + nn(raw_ref[:, : buffers[2].shape[0]], buffers[2][...])
    out_ref[...] = out.astype(out_ref.dtype)

    @pl.when(pl.program_id(0) // per_device == blocks_ref[parts])
    def _():
        out_ref[...] = (out + nt(shared_ref[...], buffers[3][...])).astype(out_ref.dtype)


def back_product(blocks, mine, size, gate, inner, raw, shared, gate_w, inner_w, step_w, shared_w, dtype):
    seqs, length, width = gate.shape
    parts, per_device, wide = len(blocks), shared.shape[0], shared.shape[2]

    def at_seq(array):
        return pl.BlockSpec((None, length, array.shape[2]), lambda s, at: (s, 0, 0))

    rows = [
        pl.BlockSpec((size, width), lambda s, at, part=part: (at[part], 0))
        for part in range(parts)
    ]
    cols = [
        pl.BlockSpec((step_w.shape[0], size), lambda s, at, part=part: (0, at[part]))
        for part in range(parts)
    ]
    shared_rows = [
        pl.BlockSpec((size, wide), lambda s, at, part=part: (at[part], 0))
        for part in range(parts)
    ]
    own = pl.BlockSpec((None, length, wide), lambda s, at: (lax.rem(s, per_device), 0, 0))
    params, cost = cheap(10**5)
    return pl.pallas_call(
        functools.partial(back_kernel, parts=parts, per_device=per_device),
        grid_spec=pltpu.PrefetchScalarGridSpec(
            num_scalar_prefetch=1,
            grid=(seqs,),
            in_specs=[at_seq(gate), at_seq(inner), at_seq(raw), own] + rows * 2 + cols + shared_rows,
            out_specs=pl.BlockSpec((length, parts * size), lambda s, at: (s, 0)),
            scratch_shapes=[
                pltpu.VMEM((parts * size, width), bf16),
                pltpu.VMEM((parts * size, width), bf16),
                pltpu.VMEM((step_w.shape[0], parts * size), bf16),
                pltpu.VMEM((parts * size, wide), bf16),
            ],
        ),
        out_shape=jax.ShapeDtypeStruct((seqs * length, parts * size), dtype),
        compiler_params=params,
        cost_estimate=cost,
    )(
        jnp.stack(blocks + [mine]), gate, inner, raw, shared, *[gate_w] * parts,
        *[inner_w] * parts, *[step_w] * parts, *[shared_w] * parts,
    )


def assemble_kernel(place_ref, *refs):
    pieces, out_ref = refs[:-1], refs[-1]
    for at, piece in enumerate(pieces):

        @pl.when(pl.program_id(0) == at)
        def _(piece=piece):
            out_ref[...] = piece[...].astype(out_ref.dtype)


def assembled(pieces, rank, dtype, column_from=None, columns=1):
    count, (size, width) = len(pieces), pieces[0].shape
    block = width // columns
    if column_from is None:
        column_from = [jnp.int32(at) for at in range(columns)]
    place = jnp.stack([jnp.asarray(rank, jnp.int32)] + [at.astype(jnp.int32) for at in column_from])
    params, cost = cheap(10**5)
    params = pltpu.CompilerParams(
        vmem_limit_bytes=vmem_limit, dimension_semantics=("arbitrary", "arbitrary")
    )
    return pl.pallas_call(
        assemble_kernel,
        grid_spec=pltpu.PrefetchScalarGridSpec(
            num_scalar_prefetch=1,
            grid=(count, columns),
            in_specs=[
                pl.BlockSpec(
                    (size, block),
                    lambda i, j, at, own=own: (0, jnp.where(i == own, at[1 + j], 0)),
                )
                for own in range(count)
            ],
            out_specs=pl.BlockSpec((size, block), lambda i, j, at: (at[0] ^ i, j)),
        ),
        out_shape=jax.ShapeDtypeStruct((count * size, width), dtype),
        compiler_params=params,
        cost_estimate=cost,
    )(place, *pieces)


def spans(total, width):
    return [slice(at, at + width) for at in range(0, total, width)]


def project_kernel(
    hidden_ref, gain_ref, inner_w_ref, shared_w_ref, step_w_ref, step_bias_ref, rate_ref,
    normed_ref, inner_ref, shared_ref, raw_ref, inv_ref, ends_ref, total_ref,
):
    length = hidden_ref.shape[0]
    heads = step_w_ref.shape[0]
    for rows in spans(length, chunk):
        hidden = hidden_ref[rows, :].astype(f32)
        inv = lax.rsqrt(jnp.mean(hidden * hidden, axis=1, keepdims=True) + epsilon)
        normed_ref[rows, :] = (hidden * inv * gain_ref[...][None, :]).astype(bf16)
        inv_ref[rows, :] = jnp.broadcast_to(inv, (chunk, lanes))
    normed = normed_ref[...]
    inner_ref[...] = nn(normed, inner_w_ref[...])
    shared_ref[...] = nn(normed, shared_w_ref[...])
    raw_ref[...] = jnp.zeros((length, lanes), f32)
    raw_ref[:, :heads] = nt(normed, step_w_ref[...])
    decays = softplus(raw_ref[...] + step_bias_ref[...]) * rate_ref[...]
    total_ref[...] = jnp.broadcast_to(jnp.sum(decays, axis=0, keepdims=True), (8, lanes))
    split = inner_ref.shape[1]
    ends_ref[:, :split] = inner_ref[length - rim :, :]
    ends_ref[:, split:] = shared_ref[length - rim :, :]


def filter_forward(buffer, taps_ref, bias_ref, start, column, taps):
    summed = bias_ref[0:1, column]
    for tap in range(taps):
        summed = summed + taps_ref[tap : tap + 1, column] * buffer[
            pl.ds(rim + start - taps + 1 + tap, chunk), column
        ]
    s = sigmoid(summed)
    return summed * s, s * (1.0 + summed * (1.0 - s))


def states_kernel(
    inner_ref, rims_ref, shared_ref, raw_ref,
    taps_ref, bias_ref, taps_s_ref, bias_s_ref, step_bias_ref, rate_ref, spread_ref, _,
    x_ref, slope_ref, shared_act_ref, slope_s_ref, step_ref, decay_ref, decay_t_ref, local_ref,
    state_ref,
    inner_buf, shared_buf, act_buf,
    *, taps, states,
):
    length, width = inner_ref.shape
    inner_buf[0:rim, :] = rims_ref[:, :width]
    inner_buf[rim:, :] = inner_ref[...]
    shared_buf[0:rim, :] = rims_ref[:, width:]
    shared_buf[rim:, :] = shared_ref[...]
    upto = triangle_of("upto")
    spread = spread_ref[...]
    base = jnp.zeros((1, lanes), f32)
    state = jnp.zeros((states, width), f32)
    for index, rows in enumerate(spans(length, chunk)):
        for column in spans(width, lanes):
            value, slope = filter_forward(
                inner_buf, taps_ref, bias_ref, rows.start, column, taps
            )
            x_ref[rows, column] = value
            slope_ref[rows, column] = slope.astype(bf16)
        for column in spans(2 * states, lanes):
            value, slope = filter_forward(
                shared_buf, taps_s_ref, bias_s_ref, rows.start, column, taps
            )
            shared_act_ref[rows, column] = value.astype(bf16)
            slope_s_ref[rows, column] = slope
        step = softplus(raw_ref[rows, :] + step_bias_ref[...])
        local = summed_by(upto, step * rate_ref[...])
        last = local[chunk - 1 : chunk, :]
        step_ref[rows, :] = step
        decay = local + base
        decay_ref[rows, :] = decay
        decay_t_ref[:, rows] = jnp.transpose(decay)[:16, :]
        weight = nn(two_parts(jnp.exp(last - local) * step), spread)
        act_buf[...] = (weight * x_ref[rows, :]).astype(bf16)
        local_ref[index, :, :] = state.astype(bf16)
        kept = nn(two_parts(jnp.broadcast_to(jnp.exp(last), (8, lanes))), spread)[0:1, :]
        state = kept * state + tn(shared_act_ref[rows, 0:states], act_buf[...])
        base = base + last
    state_ref[...] = state.astype(bf16)


def pair_masks():
    low = iota((chunk, lanes), 1) < lanes // 2
    return low, jnp.logical_not(low)


def halves(value, masks):
    zero = jnp.zeros_like(value)
    return jnp.concatenate(
        [jnp.where(masks[0], value, zero), jnp.where(masks[1], value, zero)], axis=0
    )


def fade(decay, decay_t, head, causal):
    gap = decay[:, head : head + 1] - decay_t[head : head + 1, :]
    return jnp.exp(jnp.where(causal, gap, -1e30))


def mix_kernel(
    x_ref, shared_act_ref, step_ref, decay_ref, decay_t_ref, local_ref, skip_ref, spread_ref,
    out_ref,
    *, states,
):
    length, width = x_ref.shape
    causal = iota((chunk, chunk), 0) >= iota((chunk, chunk), 1)
    masks = pair_masks()
    spread = spread_ref[...]
    base = jnp.zeros((1, lanes), f32)
    for index, rows in enumerate(spans(length, chunk)):
        b, c = shared_act_ref[rows, 0:states], shared_act_ref[rows, states:]
        scores = nt(c, b)
        x = x_ref[rows, :]
        decay = decay_ref[rows, :]
        decay_t = decay_t_ref[:, rows]
        stepped = (x * nn(two_parts(step_ref[rows, :]), spread)).astype(bf16)
        out = skip_ref[...] * x
        if index > 0:
            out = out + nn(two_parts(jnp.exp(decay - base)), spread) * nn(c, local_ref[index])
        base = decay[chunk - 1 : chunk, :]
        for pair, column in enumerate(spans(width, lanes)):
            mixing = jnp.concatenate(
                [
                    (fade(decay, decay_t, 2 * pair + side, causal) * scores).astype(bf16)
                    for side in range(2)
                ],
                axis=1,
            )
            part = nn(mixing, halves(stepped[:, column], masks))
            out_ref[rows, column] = out[:, column] + part


def gate_kernel(
    local_out_ref, shared_act_ref, decay_ref, state_in_ref, gate_ref, mixer_grad_ref, gain_ref,
    spread_ref,
    out_ref, sums_ref,
    square_buf, product_buf,
    *, states,
):
    length, width = local_out_ref.shape
    spread = spread_ref[...]
    for rows in spans(length, chunk):
        faded = nn(two_parts(jnp.exp(decay_ref[rows, :])), spread)
        out = local_out_ref[rows, :] + faded * nn(
            shared_act_ref[rows, states:], state_in_ref[...]
        )
        out_ref[rows, :] = out
        gate = gate_ref[rows, :]
        gated = out * gate * sigmoid(gate)
        square_buf[rows, :] = (gated * gated).astype(bf16)
        product_buf[rows, :] = (
            gated * mixer_grad_ref[rows, :] * gain_ref[...]
        ).astype(bf16)
    ones = jnp.ones((8, width), bf16)
    first = nt(ones, square_buf[...])
    second = nt(ones, product_buf[...])
    sums_ref[...] = jnp.where(iota((8, length), 0) < 4, first, second)


def gate_back_kernel(
    out_ref, gate_ref, mixer_grad_ref, sums_ref, gain_ref, shared_act_ref, decay_ref, spread_ref,
    mixer_in_ref, d_gate_ref, d_ssm_ref, lam_ref, gain_grad_ref,
    *, states, full,
):
    length, width = out_ref.shape
    spread = spread_ref[...]
    gain = gain_ref[...]
    summed = jnp.sum(sums_ref[...], axis=0)
    square = summed[0:1, :] * (1.0 / full)
    product = summed[4:5, :] * (1.0 / full)
    rms = lax.rsqrt(square + epsilon)
    scalars = jnp.concatenate([rms, rms * rms * rms * product, jnp.zeros((6, length), f32)], axis=0)
    gain_grad = jnp.zeros((1, width), f32)
    lam = jnp.zeros((states, width), f32)
    for rows in spans(length, chunk):
        columns = jnp.transpose(scalars[:, rows])
        rms_c, row_c = columns[:, 0:1], columns[:, 1:2]
        out = out_ref[rows, :]
        gate = gate_ref[rows, :]
        mixer_grad = mixer_grad_ref[rows, :]
        s = sigmoid(gate)
        act = gate * s
        gated = out * act
        normal = gated * rms_c
        mixer_in_ref[rows, :] = (normal * gain).astype(bf16)
        gain_grad = gain_grad + jnp.sum(mixer_grad * normal, axis=0, keepdims=True)
        d_gated = rms_c * (mixer_grad * gain) - gated * row_c
        d_ssm = d_gated * act
        d_ssm_ref[rows, :] = d_ssm
        d_gate_ref[rows, :] = (d_gated * out * s * (1.0 + gate * (1.0 - s))).astype(bf16)
        faded = nn(two_parts(jnp.exp(decay_ref[rows, :])), spread)
        lam = lam + tn(shared_act_ref[rows, states:], (faded * d_ssm).astype(bf16))
    lam_ref[...] = lam.astype(bf16)
    gain_grad_ref[...] = jnp.broadcast_to(gain_grad, (8, width))


def mix_back_kernel(
    x_ref, shared_act_ref, step_ref, decay_ref, decay_t_ref, local_ref, state_in_ref, d_ssm_ref,
    spread_ref, gather_ref,
    d_x_ref, d_shared_ref, d_decay_ref,
    column_buf,
    *, states,
):
    length, width = x_ref.shape
    causal = iota((chunk, chunk), 0) >= iota((chunk, chunk), 1)
    masks = pair_masks()
    spread, gather = spread_ref[...], gather_ref[...]
    since, before = triangle_of("from"), triangle_of("before")
    lam = jnp.zeros((states, width), f32)
    heads_here = 2 * (width // lanes)
    column_buf[...] = jnp.zeros_like(column_buf)
    row_at, col_at = iota((2 * chunk, lanes), 0), iota((2 * chunk, lanes), 1)
    all_rows = spans(length, chunk)
    for index in reversed(range(len(all_rows))):
        rows = all_rows[index]
        b, c = shared_act_ref[rows, 0:states], shared_act_ref[rows, states:]
        xf = x_ref[rows, :]
        d_out = d_ssm_ref[rows, :]
        decay = decay_ref[rows, :]
        decay_t = decay_t_ref[:, rows]
        step = step_ref[rows, :]
        if index > 0:
            base = decay_ref[rows.start - 1 : rows.start, :]
        else:
            base = jnp.zeros((1, lanes), f32)
        last = decay[chunk - 1 : chunk, :]
        heads = jnp.concatenate([jnp.exp(base), jnp.exp(last - base), jnp.zeros((6, lanes), f32)])
        heads = nn(two_parts(heads), spread)
        entered = local_ref[index].astype(f32) + heads[0:1, :] * state_in_ref[...].astype(f32)
        entered16 = entered.astype(bf16)
        lam16 = lam.astype(bf16)
        scores = nt(c, b)
        faded = nn(two_parts(jnp.exp(decay - base)), spread)
        fading = nn(two_parts(jnp.exp(last - decay)), spread)
        steps = nn(two_parts(step), spread)
        stepped = (xf * steps).astype(bf16)
        d_faded = (faded * d_out).astype(bf16)
        x_faded = (fading * steps * xf).astype(bf16)
        d_c = nt(d_faded, entered16)
        d_b = nt(x_faded, lam16)
        carried = nn(c, entered16)
        carrying = nn(b, lam16)
        queries = nn((d_faded.astype(f32) * carried).astype(bf16), gather)
        keys = nn((x_faded.astype(f32) * carrying).astype(bf16), gather)
        across = jnp.sum(lam * entered, axis=0, keepdims=True) * heads[1:2, :]
        across = nn(jnp.broadcast_to(across, (8, width)).astype(bf16), gather)[0:1, :]
        d_x = fading * carrying
        d_scores = jnp.zeros((chunk, chunk), f32)
        for pair, column in enumerate(spans(width, lanes)):
            d_stack = halves(d_out[:, column].astype(bf16), masks)
            d_mixing = nt(d_stack, stepped[:, column])
            mixed, grads = [], []
            for side in range(2):
                head = 2 * pair + side
                faint = fade(decay, decay_t, head, causal)
                d_score = faint * d_mixing[side * chunk : (side + 1) * chunk, :]
                d_scores = d_scores + d_score
                mixed.append((faint * scores).astype(bf16))
                grad = (d_score * scores).astype(bf16)
                grads.append(grad)
                column_buf[head : head + 1, :] = jnp.sum(
                    grad.astype(f32), axis=0, keepdims=True
                )
            code = jnp.where(col_at == 2 * pair + row_at // chunk, 1.0, 0.0).astype(bf16)
            queries = queries + nn(jnp.concatenate(grads, axis=1), code)
            part = tn(jnp.concatenate(mixed, axis=0), d_stack)
            d_x_ref[rows, column] = d_x[:, column] + part
        queries = queries - jnp.transpose(column_buf[...])
        d_decay_ref[rows, :] = summed_by(since, queries) + summed_by(before, keys) + across
        d_scores16 = d_scores.astype(bf16)
        d_shared_ref[rows, 0:states] = d_b + tn(d_scores16, c)
        d_shared_ref[rows, states:] = d_c + nn(d_scores16, b)
        lam = heads[1:2, :] * lam + tn(c, d_faded)


def filter_backward(buffer, taps_ref, start, size, column, taps):
    total = None
    for tap in range(taps):
        term = taps_ref[tap : tap + 1, column] * buffer[
            pl.ds(rim + start + taps - 1 - tap, size), column
        ]
        total = term if total is None else total + term
    return total


def filter_adjoint(buffer, inner_buf, taps_ref, length, width, taps, body_ref, edge_ref, tail_ref,
                   taps_grad_ref):
    for column in spans(width, lanes):
        edge_ref[:, column] = filter_backward(buffer, taps_ref, -rim, rim, column, taps).astype(
            bf16
        )
        rows_grad = [jnp.zeros((8, lanes), f32) for _ in range(taps + 1)]
        for rows in spans(length, chunk):
            body = filter_backward(buffer, taps_ref, rows.start, chunk, column, taps)
            body_ref[rows, column] = body.astype(bf16)
            if rows.stop == length:
                tail_ref[:, column] = body[chunk - rim :, :]
            grad = buffer[pl.ds(rim + rows.start, chunk), column]
            for tap in range(taps):
                moved = inner_buf[pl.ds(rim + rows.start - taps + 1 + tap, chunk), column]
                rows_grad[tap] = rows_grad[tap] + jnp.sum(
                    (grad * moved).reshape(chunk // 8, 8, lanes), axis=0
                )
            rows_grad[taps] = rows_grad[taps] + jnp.sum(
                grad.reshape(chunk // 8, 8, lanes), axis=0
            )
        sums = [jnp.sum(part, axis=0, keepdims=True) for part in rows_grad]
        sums.append(jnp.zeros((8 - taps - 1, lanes), f32))
        taps_grad_ref[:, column] = jnp.concatenate(sums, axis=0)


def act_kernel(
    x_ref, step_ref, decay_ref, d_shared_ref, later_ref, spread_ref, out_ref, *, states
):
    length = x_ref.shape[0]
    last = decay_ref[length - 1 : length, :]
    weight = nn(two_parts(jnp.exp(last - decay_ref[...]) * step_ref[...]), spread_ref[...])
    weighted = (x_ref[...] * weight).astype(bf16)
    out_ref[:, 0:states] = d_shared_ref[:, 0:states] + nt(weighted, later_ref[...])
    out_ref[:, states:] = d_shared_ref[:, states:]


def finish_kernel(
    x_ref, slope_ref, shared_act_ref, raw_ref, step_ref, decay_ref, d_x_ref,
    d_decay_ref, d_ssm_ref, state_in_ref, later_ref, inner_ref, rims_ref,
    taps_ref, step_bias_ref, rate_ref, skip_ref, spread_ref, gather_ref,
    body_ref, edge_ref, tail_ref, taps_grad_ref, d_raw_ref, heads_ref,
    grad_buf, inner_buf,
    *, taps, states,
):
    length, width = x_ref.shape
    spread, gather = spread_ref[...], gather_ref[...]
    before = triangle_of("before")
    later = later_ref[...]
    grad_buf[0:rim, :] = jnp.zeros((rim, width), f32)
    grad_buf[rim + length :, :] = jnp.zeros((rim, width), f32)
    inner_buf[0:rim, :] = rims_ref[:, :width]
    inner_buf[rim:, :] = inner_ref[...]
    last = decay_ref[length - 1 : length, :]
    final = nn(two_parts(jnp.broadcast_to(jnp.exp(last), (8, lanes))), spread)[0:1, :]
    across = final * jnp.sum(
        later.astype(f32) * state_in_ref[...].astype(f32), axis=0, keepdims=True
    )
    running = nn(jnp.broadcast_to(across, (8, width)).astype(bf16), gather)[0:1, :]
    skip = skip_ref[...]
    skip_grad = jnp.zeros((1, width), f32)
    rate_grad = jnp.zeros((1, lanes), f32)
    bias_grad = jnp.zeros((1, lanes), f32)
    for rows in spans(length, chunk):
        b = shared_act_ref[rows, 0:states]
        x = x_ref[rows, :]
        step = step_ref[rows, :]
        d_ssm = d_ssm_ref[rows, :]
        fading = nn(two_parts(jnp.exp(last - decay_ref[rows, :])), spread)
        steps = nn(two_parts(step), spread)
        carrying = fading * nn(b, later)
        x_stepped = x * steps
        keys = nn((x_stepped * carrying).astype(bf16), gather)
        d_x = d_x_ref[rows, :] + carrying
        direct = nn((x * d_x).astype(bf16), gather)
        d_decay = d_decay_ref[rows, :] + running + summed_by(before, keys)
        running = running + jnp.sum(keys, axis=0, keepdims=True)
        skip_grad = skip_grad + jnp.sum(d_ssm * x, axis=0, keepdims=True)
        rate_grad = rate_grad + jnp.sum(step * d_decay, axis=0, keepdims=True)
        d_raw = (direct + rate_ref[...] * d_decay) * sigmoid(
            raw_ref[rows, :] + step_bias_ref[...]
        )
        d_raw_ref[rows, :] = d_raw.astype(bf16)
        bias_grad = bias_grad + jnp.sum(d_raw, axis=0, keepdims=True)
        grad_buf[pl.ds(rim + rows.start, chunk), :] = (
            skip * d_ssm + steps * d_x
        ) * slope_ref[rows, :].astype(f32)
    parts = two_parts(jnp.broadcast_to(skip_grad, (8, width)))
    skip_heads = nn(parts[:, :width], gather) + nn(parts[:, width:], gather)
    heads_ref[...] = jnp.concatenate(
        [bias_grad, rate_grad * rate_ref[...], skip_heads[0:1, :], jnp.zeros((5, lanes), f32)],
        axis=0,
    )
    filter_adjoint(
        grad_buf, inner_buf, taps_ref, length, width, taps, body_ref, edge_ref, tail_ref,
        taps_grad_ref,
    )


def shared_kernel(
    first_ref, d_act_ref, slope_ref, shared_ref, rim_ref, taps_ref,
    body_ref, edge_ref, tail_ref, taps_grad_ref,
    grad_buf, inner_buf,
    *, taps,
):
    _, length, width = d_act_ref.shape
    grad_buf[0:rim, :] = jnp.zeros((rim, width), f32)
    grad_buf[rim + length :, :] = jnp.zeros((rim, width), f32)
    inner_buf[0:rim, :] = rim_ref[:, rim_ref.shape[1] - width :]
    inner_buf[rim:, :] = shared_ref[...]
    grad_buf[rim : rim + length, :] = jnp.sum(d_act_ref[...], axis=0) * slope_ref[...]
    filter_adjoint(
        grad_buf, inner_buf, taps_ref, length, width, taps, body_ref, edge_ref, tail_ref,
        taps_grad_ref,
    )


def chain_kernel(pieces_ref, totals_ref, spread_ref, out_ref, *, backward):
    count = pieces_ref.shape[0]
    decays = nn(two_parts(jnp.exp(totals_ref[...])), spread_ref[...])
    state = jnp.zeros(pieces_ref.shape[1:], f32)
    order = reversed(range(count)) if backward else range(count)
    for block in order:
        out_ref[block, :, :] = state.astype(bf16)
        state = decays[block : block + 1, :] * state + pieces_ref[block].astype(f32)


def after(ready, *values):
    if not ready:
        return values if len(values) > 1 else values[0]
    tied = lax.optimization_barrier((tuple(ready), tuple(values)))[1]
    return tied if len(values) > 1 else tied[0]


def landed(ready, *transfers):
    flat = [value for transfer in transfers for value in transfer]
    flat = list(lax.optimization_barrier((tuple(ready), tuple(flat)))[1])
    return [[flat.pop(0) for _ in transfer] for transfer in transfers]


def bits_of(axis):
    return [1 << bit for bit in range(lax.axis_size(axis).bit_length() - 1)]


def swapped(value, axis, bit):
    size = lax.axis_size(axis)
    return lax.ppermute(value, axis, [(i, i ^ bit) for i in range(size)])


def passed_along(value, axis, by):
    size = lax.axis_size(axis)
    pairs = [(i, i + by) for i in range(size) if 0 <= i + by < size]
    return lax.ppermute(value, axis, pairs)


def block_at(value, index, size, dim):
    return lax.dynamic_slice_in_dim(value, index * size, size, dim)


def reversed_order(axis):
    order = [0]
    for bit in reversed(bits_of(axis)):
        order = order + [at + bit for at in order]
    return order


def relative_blocks(value, axis, dim):
    count, mine = lax.axis_size(axis), lax.axis_index(axis)
    size = value.shape[dim] // count
    blocks = [block_at(value, mine ^ other, size, dim) for other in reversed_order(axis)]
    half = len(blocks) // 2
    return [
        jnp.concatenate(blocks[:half], axis=dim),
        jnp.concatenate(blocks[half:], axis=dim),
    ]


def gathered_relative(value, axis, dim, ready=()):
    for bit in reversed(bits_of(axis)):
        value = jnp.concatenate([value, after(ready, swapped(value, axis, bit))], axis=dim)
    return value


def halves_added(kept, got, dim):
    half = got.shape[dim] // 2
    parts = [
        lax.slice_in_dim(value, at * half, (at + 1) * half, axis=dim)
        for at in range(2)
        for value in (kept, got)
    ]
    return parts[0].astype(f32) + parts[1].astype(f32), parts[2].astype(f32) + parts[3].astype(f32)


def in_place_order(value, axis, dim):
    count, mine = lax.axis_size(axis), lax.axis_index(axis)
    size = value.shape[dim] // count
    bits = bits_of(axis)

    def place(at):
        return sum(((at // bit) % 2) * back for bit, back in zip(bits, reversed(bits)))

    return jnp.concatenate(
        [block_at(value, place(mine ^ other), size, dim) for other in range(count)], axis=dim
    )


def rank_in(axis, group):
    mine = lax.axis_index(axis)
    return sum(((mine // bit) % 2) << at for at, bit in enumerate(group))


def mask_of(group, distance):
    return sum(bit for at, bit in enumerate(group) if distance >> at & 1)


class Reduction:
    def __init__(self, value, axis, groups, wire=bf16, halves=None):
        self.axis, self.wire, self.value = axis, wire, value
        self.left, self.taken = list(groups), []
        if halves is None:
            self.split()
        else:
            self.kept, self.sent = halves[0], [halves[1]]

    def split(self):
        if self.left:
            count = 1 << len(self.left[0])
            rank = rank_in(self.axis, self.left[0])
            size = self.value.shape[0] // count
            self.kept = block_at(self.value, rank, size, 0)
            self.sent = [
                block_at(self.value, rank ^ other, size, 0).astype(self.wire)
                for other in range(1, count)
            ]
        else:
            self.value = self.value.astype(bf16)
            self.sent = [self.value]

    def start(self):
        group = self.left[0] if self.left else self.taken[-1]
        count = 1 << len(group)
        sent = self.sent if self.left else self.sent * (count - 1)
        return [
            swapped(value, self.axis, mask_of(group, other))
            for other, value in enumerate(sent, 1)
        ]

    def take(self, got, *columns):
        if self.left:
            self.taken.append(self.left.pop(0))
            total = self.kept.astype(f32)
            for value in got:
                total = total + value.astype(f32)
            self.value = total.astype(self.wire)
        else:
            group = self.taken.pop()
            rank = rank_in(self.axis, group)
            if self.taken:
                self.value = assembled([self.value] + got, rank, bf16)
            else:
                self.value = assembled([self.value] + got, rank, f32, *columns)
        if self.left or self.taken:
            self.split()
            return self.sent
        return [self.value]


def exchanged_sum(value, axis):
    for bit in bits_of(axis):
        value = (value.astype(f32) + swapped(value, axis, bit).astype(f32)).astype(value.dtype)
    return value


def exchanged_all(value, axis):
    mine = lax.axis_index(axis)
    value = value[None]
    for bit in bits_of(axis):
        got = swapped(value, axis, bit)
        low = (mine // bit) % 2 == 0
        value = jnp.concatenate([jnp.where(low, value, got), jnp.where(low, got, value)], axis=0)
    return value


def to_owners(state):
    count, width = lax.axis_size("seq"), state.shape[-1]
    return [lax.all_to_all(state.reshape(count, -1, width), "seq", 0, 0, tiled=True)]


def chained(pieces, totals, states, spread, backward):
    count, size, width = pieces.shape
    mine = lax.axis_index("seq")
    here = lax.dynamic_index_in_dim(totals, mine * size // states, 1, keepdims=False)
    params, cost = cheap(10**5)
    return pl.pallas_call(
        functools.partial(chain_kernel, backward=backward),
        out_shape=jax.ShapeDtypeStruct((count, size, width), bf16),
        compiler_params=pltpu.CompilerParams(vmem_limit_bytes=vmem_limit),
        cost_estimate=cost,
    )(pieces, here, spread)


def shares_sent(value, axes):
    count = lax.axis_size(axes)
    return [lax.all_to_all(value.reshape(count, -1, value.shape[-1]), axes, 0, 0, tiled=True)]


def shares_back(pieces, axes):
    total = jnp.sum(pieces.astype(f32), axis=0, keepdims=True).astype(bf16)
    return [lax.all_to_all(jnp.broadcast_to(total, pieces.shape), axes, 0, 0, tiled=True)]


def to_blocks(scanned):
    return [lax.all_to_all(scanned, "seq", 0, 0, tiled=True)]


def on_device(
    hidden_in, norm_gain, proj_gate, proj_inner, proj_step, proj_shared, filter_inner,
    filter_inner_bias, filter_shared, filter_shared_bias, step_bias, log_rate, skip_gain,
    gate_gain, proj_out, cotangent,
):
    seqs, length, width_d = hidden_in.shape
    width = proj_gate.shape[1]
    heads = proj_step.shape[1]
    per_head = width // heads
    states = proj_shared.shape[1] // 2
    taps = filter_inner.shape[0]
    count_h = lax.axis_size("head")
    mine_h = lax.axis_index("head")
    full = width * count_h
    columns = width_d // count_h
    tokens = seqs * length
    per_device_seqs = seqs // count_h

    spread_np = np.zeros((2 * lanes, width), np.float32)
    for head in range(heads):
        spread_np[head, head * per_head : (head + 1) * per_head] = 1
        spread_np[lanes + head, head * per_head : (head + 1) * per_head] = 1
    spread = jnp.asarray(spread_np, bf16)
    gather = jnp.asarray(spread_np[:lanes].T, bf16)

    def on_lanes(vector):
        return jnp.pad(vector.astype(f32), (0, lanes - heads)).reshape(1, lanes)

    rate = on_lanes(-jnp.exp(log_rate))
    bias_row = on_lanes(step_bias)
    skip_row = jnp.repeat(skip_gain, per_head).reshape(1, width)
    gain_row = gate_gain.reshape(1, width)

    shape = jax.ShapeDtypeStruct
    wide = per_seq(length, width)
    narrow = per_seq(length, 2 * states)
    slim = per_seq(length, lanes)
    slim_t = per_seq(16, length)
    state_spec = per_seq(states, width)
    chunks = length // chunk

    normed, inner_pre, shared_pre, step_raw, inv_rms, ends, total = grid_call(
        project_kernel,
        seqs,
        [
            per_seq(length, width_d), whole((width_d,)), whole((width_d, width)),
            whole((width_d, 2 * states)), whole((heads, width_d)), whole((1, lanes)),
            whole((1, lanes)),
        ],
        [
            per_seq(length, width_d), wide, narrow, slim, slim, per_seq(rim, width + 2 * states),
            per_seq(8, lanes),
        ],
        [
            shape((seqs, length, width_d), bf16),
            shape((seqs, length, width), f32),
            shape((seqs, length, 2 * states), f32),
            shape((seqs, length, lanes), f32),
            shape((seqs, length, lanes), f32),
            shape((seqs, rim, width + 2 * states), f32),
            shape((seqs, 8, lanes), f32),
        ],
        [],
        10**5,
    )(
        hidden_in, norm_gain, proj_inner, proj_shared, proj_step.T, bias_row, rate,
    )
    normed = normed.reshape(tokens, width_d)
    rims = passed_along(ends, "seq", 1)
    totals = exchanged_all(total[:, 0, :], "seq")
    cot_all = [cotangent.reshape(tokens, columns)]
    for bit in bits_of("head")[:-1]:
        cot_all = cot_all + [swapped(one, "head", bit) for one in cot_all]
    out_blocks = [
        block_at(after([rims], proj_out), mine_h ^ other, columns, 1) for other in range(count_h)
    ]

    x, slope, shared_act, slope_s, step, decay, decay_t, local, state = grid_call(
        functools.partial(states_kernel, taps=taps, states=states),
        seqs,
        [
            wide, per_seq(rim, width + 2 * states), narrow, slim,
            whole((taps, width)), whole((1, width)), whole((taps, 2 * states)),
            whole((1, 2 * states)), whole((1, lanes)), whole((1, lanes)), whole((2 * lanes, width)),
            pl.BlockSpec(memory_space=pl.ANY),
        ],
        [
            wide, wide, narrow, narrow, slim, slim, slim_t, per_seq(chunks, states, width),
            state_spec,
        ],
        [
            shape((seqs, length, width), f32),
            shape((seqs, length, width), bf16),
            shape((seqs, length, 2 * states), bf16),
            shape((seqs, length, 2 * states), f32),
            shape((seqs, length, lanes), f32),
            shape((seqs, length, lanes), f32),
            shape((seqs, 16, length), f32),
            shape((seqs, chunks, states, width), bf16),
            shape((seqs, states, width), bf16),
        ],
        [
            pltpu.VMEM((rim + length, width), f32),
            pltpu.VMEM((rim + length, 2 * states), f32),
            pltpu.VMEM((chunk, width), bf16),
        ],
        10**5,
    )(
        inner_pre, rims, shared_pre, step_raw, filter_inner,
        filter_inner_bias.reshape(1, width), filter_shared,
        filter_shared_bias.reshape(1, 2 * states), bias_row, rate, spread, totals,
    )
    local_out = grid_call(
        functools.partial(mix_kernel, states=states),
        seqs,
        [
            wide, narrow, slim, slim, slim_t, per_seq(chunks, states, width), whole((1, width)),
            whole((2 * lanes, width)),
        ],
        wide,
        shape((seqs, length, width), f32),
        [],
        10**5,
    )(x, shared_act, step, decay, decay_t, local, skip_row, spread)

    out_kept, out_sent = relative_blocks(after([state], proj_out), "head", 1)
    out_kept, out_sent = after([state], out_kept, out_sent)
    ((pieces,),) = landed([local_out, out_kept, out_sent], to_owners(state))
    scanned = chained(pieces, totals, states, spread, False)
    cot_far = after([scanned], swapped(cot_all[0], "head", bits_of("head")[-1]))
    gate_pre = product(nn, after([scanned, cot_far], normed), proj_gate, f32)
    cot_far = [cot_far]
    for bit in bits_of("head")[:-1]:
        cot_far = cot_far + [swapped(one, "head", bit) for one in cot_far]
    (cot_far,) = landed([gate_pre], cot_far)
    cot_all = cot_all + cot_far
    mixer_grad = pieces_product(cot_all, out_blocks, f32)
    ((state_in,),) = landed([mixer_grad], to_blocks(scanned))
    gate_pre = gate_pre.reshape(seqs, length, width)
    mixer_grad = mixer_grad.reshape(seqs, length, width)
    state_in = state_in.reshape(seqs, states, width)

    ssm_out, sums = grid_call(
        functools.partial(gate_kernel, states=states),
        seqs,
        [
            wide, narrow, slim, state_spec, wide, wide, whole((1, width)),
            whole((2 * lanes, width)),
        ],
        [wide, per_seq(8, length)],
        [shape((seqs, length, width), f32), shape((seqs, 8, length), f32)],
        [pltpu.VMEM((length, width), bf16), pltpu.VMEM((length, width), bf16)],
        10**5,
    )(local_out, shared_act, decay, state_in, gate_pre, mixer_grad, gain_row, spread)
    sums_all = lax.all_gather(sums, "head")

    mixer_in, d_gate, d_ssm, lam, gain_grad = grid_call(
        functools.partial(gate_back_kernel, states=states, full=float(full)),
        seqs,
        [
            wide, wide, wide,
            pl.BlockSpec((count_h, None, 8, length), lambda s: (0, s, 0, 0)),
            whole((1, width)), narrow, slim, whole((2 * lanes, width)),
        ],
        [wide, wide, wide, state_spec, per_seq(8, width)],
        [
            shape((seqs, length, width), bf16),
            shape((seqs, length, width), bf16),
            shape((seqs, length, width), f32),
            shape((seqs, states, width), bf16),
            shape((seqs, 8, width), f32),
        ],
        [],
        10**5,
    )(ssm_out, gate_pre, mixer_grad, sums_all, gain_row, shared_act, decay, spread)

    mixer_flat = mixer_in.reshape(tokens, width)
    d_gate_flat = d_gate.reshape(tokens, width)
    bits = bits_of("seq")
    groups = [bits[:1], bits[1:]]
    fine_groups = [bits[:1], bits[1:2], bits[2:]]

    def in_parts(left, right, first, rows, ready):
        half, upper = rows // 2, rank_in("seq", bits[:1])
        far = product(tn, after(ready, left), right, bf16, first + (1 - upper) * half, half)
        near = product(tn, after([far], left), right, bf16, first + upper * half, half)
        return near, far

    near_bit, far_bit = bits_of("head")
    out_parts = in_parts(mixer_flat, cot_all, 0, width, ())
    out_sum = Reduction(None, "seq", fine_groups, halves=out_parts)
    gate_parts = in_parts(normed, d_gate_flat, 0, width_d, out_parts[:1])
    gate_sum = Reduction(None, "seq", fine_groups, halves=gate_parts)

    def mix_back(first, count, d_ssm, into):
        def at(*dims):
            return per_seq(*dims, first=first)

        wide, narrow, slim = at(length, width), at(length, 2 * states), at(length, lanes)
        return grid_call(
            functools.partial(mix_back_kernel, states=states),
            count,
            [
                wide, narrow, slim, slim, at(16, length), at(chunks, states, width),
                at(states, width), wide, whole((2 * lanes, width)), whole((width, lanes)),
            ],
            [wide, narrow, slim],
            [
                shape((seqs, length, width), f32),
                shape((seqs, length, 2 * states), f32),
                shape((seqs, length, lanes), f32),
            ],
            [pltpu.VMEM((lanes, chunk), f32)],
            10**5,
            into,
        )(x, shared_act, step, decay, decay_t, local, state_in, d_ssm, spread, gather)

    quarter = seqs // 4
    ((pieces,),) = landed(gate_parts[:1], to_owners(lam))
    scanned = chained(pieces, totals, states, spread, True)
    back_parts = mix_back(0, quarter, after([scanned], d_ssm), ())
    (got,) = landed([back_parts[2]], out_sum.start())
    ready = out_sum.take(got) + gate_sum.sent
    back_parts = mix_back(quarter, seqs - quarter, after(ready, d_ssm), back_parts)
    d_x, d_shared, d_decay = back_parts
    got, got_gate = landed([d_decay], out_sum.start(), gate_sum.start())
    ready = out_sum.take(got) + gate_sum.take(got_gate)
    sent_out = product(nn, after(ready, mixer_flat), out_sent, bf16)
    kept_out = product(nn, after([sent_out], mixer_flat), out_kept, bf16)
    (later,), got, got_gate = landed(
        [kept_out], to_blocks(scanned), out_sum.start(), gate_sum.start()
    )
    later = later.reshape(seqs, states, width)
    ready = out_sum.take(got) + gate_sum.take(got_gate)
    sent_out = after(ready, sent_out)

    def finish(first, count, later, into):
        def at(*dims):
            return per_seq(*dims, first=first)

        wide, narrow, slim = at(length, width), at(length, 2 * states), at(length, lanes)
        state_spec = at(states, width)
        return grid_call(
            functools.partial(finish_kernel, taps=taps, states=states),
            count,
            [
                wide, wide, narrow, slim, slim, slim, wide, slim, wide, state_spec, state_spec,
                wide, at(rim, width), whole((taps, width)), whole((1, lanes)), whole((1, lanes)),
                whole((1, width)), whole((2 * lanes, width)), whole((width, lanes)),
            ],
            [
                wide, at(rim, width), at(rim, width), at(8, width), slim,
                at(8, lanes),
            ],
            [
                shape((seqs, length, width), bf16),
                shape((seqs, rim, width), bf16),
                shape((seqs, rim, width), f32),
                shape((seqs, 8, width), f32),
                shape((seqs, length, lanes), bf16),
                shape((seqs, 8, lanes), f32),
            ],
            [
                pltpu.VMEM((2 * rim + length, width), f32),
                pltpu.VMEM((rim + length, width), f32),
            ],
            10**5,
            into,
        )(
            x, slope, shared_act, step_raw, step, decay, d_x, d_decay, d_ssm, state_in,
            later, inner_pre, rims, filter_inner, bias_row, rate, skip_row, spread, gather,
        )


    d_act = grid_call(
        functools.partial(act_kernel, states=states),
        seqs,
        [wide, slim, slim, narrow, state_spec, whole((2 * lanes, width))],
        narrow,
        shape((seqs, length, 2 * states), f32),
        [],
        10**5,
    )(x, step, decay, d_shared, after(ready, later), spread)
    body, edge, tail, taps_grad, d_raw, heads_grad = finish(
        0, seqs, after([d_act], later), ()
    )

    got, got_gate, (got_out,), (d_act_all,) = landed(
        [body], out_sum.start(), gate_sum.start(), [swapped(sent_out, "head", near_bit)],
        shares_sent(d_act.reshape(seqs * length, 2 * states), "head"),
    )
    def own_seqs(*dims):
        return pl.BlockSpec((None,) + dims, lambda s, at: (at[0] + s,) + (0,) * len(dims))

    def given(*dims):
        return pl.BlockSpec((None,) + dims, lambda s, at: (s,) + (0,) * len(dims))

    params, cost = cheap(10**5)
    s_body, s_edge, s_tail, s_taps_grad = pl.pallas_call(
        functools.partial(shared_kernel, taps=taps),
        grid_spec=pltpu.PrefetchScalarGridSpec(
            num_scalar_prefetch=1,
            grid=(per_device_seqs,),
            in_specs=[
                pl.BlockSpec((count_h, length, 2 * states), lambda s, at: (0, s, 0)),
                own_seqs(length, 2 * states),
                own_seqs(length, 2 * states), own_seqs(rim, width + 2 * states),
                pl.BlockSpec((taps, 2 * states), lambda s, at: (0, 0)),
            ],
            out_specs=[
                given(length, 2 * states), given(rim, 2 * states), given(rim, 2 * states),
                given(8, 2 * states),
            ],
            scratch_shapes=[
                pltpu.VMEM((2 * rim + length, 2 * states), f32),
                pltpu.VMEM((rim + length, 2 * states), f32),
            ],
        ),
        out_shape=[
            shape((per_device_seqs, length, 2 * states), bf16),
            shape((per_device_seqs, rim, 2 * states), bf16),
            shape((per_device_seqs, rim, 2 * states), f32),
            shape((per_device_seqs, 8, 2 * states), f32),
        ],
        compiler_params=params,
        cost_estimate=cost,
    )(
        (mine_h * per_device_seqs).reshape(1), d_act_all, slope_s, shared_pre,
        rims, filter_shared,
    )
    step_grad = product(tn, after([s_body], d_raw.reshape(tokens, lanes)), normed, f32)
    (edge,), (s_edge,) = landed(
        [step_grad], [passed_along(edge, "seq", -1)], [passed_along(s_edge, "seq", -1)]
    )

    def joined(body, edge, tail):
        ends = (tail + edge.astype(f32)).astype(bf16)
        return lax.dynamic_update_slice_in_dim(body, ends, length - rim, 1)

    got, got_gate, (got_out,), _ = landed([edge, s_edge], got, got_gate, [got_out], [edge])
    mixed, sent_out = halves_added(kept_out, got_out, 1)
    sent_out = sent_out.astype(bf16)
    ready = out_sum.take(got) + gate_sum.take(got_gate)
    d_inner = joined(body, edge, tail)
    d_inner_flat = d_inner.reshape(tokens, width)
    d_shared_own = joined(s_body, s_edge, s_tail)
    own_tokens = per_device_seqs * length
    d_shared_flat = d_shared_own.reshape(own_tokens, 2 * states)
    padded = columns + 64
    shared_grad = shared_product(
        mine_h, after(ready, normed), d_shared_flat, jnp.sum(s_taps_grad, axis=0),
        count_h, padded,
    )
    inner_parts = in_parts(normed, d_inner_flat, 0, width_d, [d_inner, shared_grad])
    inner_sum = Reduction(None, "seq", fine_groups, halves=inner_parts)
    blocks = [mine_h ^ other for other in reversed_order("head")]
    middle = len(blocks) // 2
    step_rows = jnp.pad(after([d_inner], proj_step).T, ((0, 16 - heads), (0, 0)))
    ready, back = [inner_parts[0], step_rows], []
    for picked in (blocks[middle:], blocks[:middle]):
        back.append(
            back_product(
                picked, mine_h, columns, d_gate, after(ready, d_inner), d_raw, d_shared_own,
                proj_gate, proj_inner, step_rows, proj_shared, bf16,
            )
        )
        ready = back[-1:]
    got, got_out, got_gate, (shared_all,) = landed(
        ready, inner_sum.start(), out_sum.start(), gate_sum.start(),
        shares_sent(shared_grad, "head"),
    )
    ready = inner_sum.take(got)
    back = list(after(ready, *back))
    sent_out = after(ready, sent_out)
    got_out, got_gate = landed(ready, got_out, got_gate)
    ready = ready + out_sum.take(got_out) + gate_sum.take(got_gate)

    count = lax.axis_size("seq")
    rows_wide = 8 * width // (2 * states)
    rows_small = pl.pallas_call(
        rows_kernel,
        out_shape=shape((count * rows_wide, 2 * states), f32),
        scratch_shapes=[pltpu.VMEM((8 * count, width), f32)],
        compiler_params=pltpu.CompilerParams(vmem_limit_bytes=vmem_limit),
        cost_estimate=cheap(10**5)[1],
    )(after([shared_grad], taps_grad), gain_grad, heads_grad, step_grad)
    shared_rows = jnp.concatenate(
        [
            rows_small.reshape(count, -1, 2 * states),
            jnp.sum(shared_all, axis=0).reshape(count, -1, 2 * states),
        ],
        axis=1,
    )
    shared_rows = shared_rows.reshape(-1, 2 * states).astype(bf16)
    (pieces,) = shares_sent(shared_rows, "seq")
    got, (got_back,) = landed(
        ready, inner_sum.start(), [swapped(back[0], "head", near_bit)]
    )
    d_normed, back_sent = halves_added(back[1], got_back, 1)
    back_sent = back_sent.astype(bf16)
    ready = inner_sum.take(got) + [back_sent]
    got, got_gate, got_out = landed(
        ready, inner_sum.start(), gate_sum.start(), out_sum.start()
    )
    ready = inner_sum.take(got)
    got_gate, got_out = landed(ready, got_gate, got_out)
    ready = ready + gate_sum.take(got_gate)
    got, (got_back,), (got_mixed,), (pieces,) = landed(
        ready, inner_sum.start(), [swapped(back_sent, "head", far_bit)],
        [swapped(sent_out, "head", far_bit)], [pieces],
    )
    ready = inner_sum.take(got)

    mixed = (mixed + got_mixed.astype(f32)).reshape(seqs, length, columns)
    d_normed = (after(ready, d_normed) + got_back.astype(f32)).reshape(seqs, length, columns)
    total = jnp.sum(pieces.astype(f32), axis=0, keepdims=True).astype(bf16)
    pieces = jnp.broadcast_to(total, pieces.shape)
    (shared_back,) = [lax.all_to_all(pieces, "seq", 0, 0, tiled=True)]
    hidden_own = block_at(after(ready, hidden_in), mine_h, columns, 2).astype(f32)
    scaled = d_normed * block_at(after(ready, norm_gain), mine_h, columns, 0)
    norm_row = jnp.sum(scaled * hidden_own, axis=-1)
    inv_rms = after(ready, inv_rms)[:, :, :1]
    norm_row = jnp.sum(lax.all_gather(norm_row, "head"), axis=0)[..., None] / width_d
    norm_gain_grad = jnp.sum(d_normed * hidden_own * inv_rms, axis=(0, 1))
    norm_gain_grad = norm_gain_grad + swapped(norm_gain_grad, "seq", bits[0])
    got, got_gate = landed([norm_row], inner_sum.start(), gate_sum.start())
    ready = inner_sum.take(got)
    norm_gain_grad = after(ready, norm_gain_grad)
    for bit in bits[1:]:
        norm_gain_grad = norm_gain_grad + swapped(norm_gain_grad, "seq", bit)
    d_late, norm_row, mixed = after(ready, scaled, norm_row, mixed)
    activations = (hidden_own + mixed).astype(bf16)
    grad_input = (
        cotangent.astype(f32)
        + inv_rms * d_late
        - hidden_own * inv_rms * inv_rms * inv_rms * norm_row
    )
    got_out, got_gate = landed(ready, got_out, got_gate)
    (out_grad,) = out_sum.take(got_out, [mine_h ^ at for at in range(count_h)], count_h)
    (gate_out,) = gate_sum.take(got_gate)
    small = shared_back[:, :rows_wide].reshape(count, width // (2 * states), 8, 2 * states)
    small = small.transpose(0, 2, 1, 3).reshape(8 * count, width).astype(f32)
    shared_back = shared_back[:, rows_wide:].reshape(padded, 2 * states)

    step_out = jnp.concatenate([small[16:32], small[32:48]], axis=1)[:heads].T
    (got,) = landed([gate_out, out_grad], inner_sum.start())
    shared_wide = jnp.broadcast_to(shared_back, (count_h,) + shared_back.shape)
    (shared_full,) = shares_sent(shared_wide.reshape(-1, 2 * states), "head")
    (inner_out,) = inner_sum.take(got)
    shared_full = shared_full.astype(f32)
    shared_out = shared_full[:, :columns].reshape(width_d, 2 * states)
    shared_extra = shared_full[0, columns : columns + 8]
    return (
        activations,
        grad_input,
        norm_gain_grad,
        gate_out,
        inner_out,
        step_out,
        shared_out,
        small[:taps],
        small[taps],
        shared_extra[:taps],
        shared_extra[taps],
        small[9, :heads],
        small[10, :heads],
        small[11, :heads],
        small[8],
        out_grad,
    )


def solution(mesh):
    in_specs = (
        P(None, "seq", None),
        P(),
        P(None, "head"),
        P(None, "head"),
        P(None, "head"),
        P(),
        P(None, "head"),
        P("head"),
        P(),
        P(),
        P("head"),
        P("head"),
        P("head"),
        P("head"),
        P("head", None),
        P(None, "seq", "head"),
    )
    out_specs = (
        P(None, "seq", "head"),
        P(None, "seq", "head"),
        P("head"),
        P(None, "head"),
        P(None, "head"),
        P(None, "head"),
        P(),
        P(None, "head"),
        P("head"),
        P(),
        P(),
        P("head"),
        P("head"),
        P("head"),
        P("head"),
        P("head", None),
    )
    return jax.shard_map(
        on_device, mesh=mesh, in_specs=in_specs, out_specs=out_specs, check_vma=False
    )
```

```python
import functools

import jax
import jax.numpy as jnp
import numpy as np
from jax import lax
from jax.experimental import pallas as pl
from jax.experimental.pallas import tpu as pltpu
from jax.sharding import PartitionSpec as P

epsilon = 1e-05
lanes = 128
chunk = 128
rim = 16
f32 = jnp.float32
bf16 = jnp.bfloat16
vmem_limit = 56 * 1024 * 1024


def nn(left, right):
    return jnp.dot(left, right, preferred_element_type=f32)


def nt(left, right):
    return lax.dot_general(left, right, (((1,), (1,)), ((), ())), preferred_element_type=f32)


def tn(left, right):
    return lax.dot_general(left, right, (((0,), (0,)), ((), ())), preferred_element_type=f32)


def rest_of(value):
    return (value - value.astype(bf16).astype(f32)).astype(bf16)


def two_parts(value):
    high = value.astype(bf16)
    return jnp.concatenate([high, (value - high.astype(f32)).astype(bf16)], axis=1)


def three_parts(value):
    high = value.astype(bf16)
    rest = value - high.astype(f32)
    middle = rest.astype(bf16)
    low = (rest - middle.astype(f32)).astype(bf16)
    return jnp.concatenate([high, middle, low], axis=1)


def summed_by(triangle, value):
    parts = nn(triangle, three_parts(value))
    return parts[:, :lanes] + parts[:, lanes : 2 * lanes] + parts[:, 2 * lanes :]


def iota(shape, dim):
    return lax.broadcasted_iota(jnp.int32, shape, dim)


def triangle_of(kind):
    row, col = iota((chunk, chunk), 0), iota((chunk, chunk), 1)
    keep = {"upto": row >= col, "from": row <= col, "before": row > col}[kind]
    return jnp.where(keep, 1.0, 0.0).astype(bf16)


def sigmoid(value):
    return 0.5 * jnp.tanh(0.5 * value) + 0.5


def softplus(value):
    return jnp.maximum(value, 0.0) + jnp.log1p(jnp.exp(-jnp.abs(value)))


def whole(shape):
    return pl.BlockSpec(shape, lambda s: (0,) * len(shape))


def per_seq(*dims, first=0):
    return pl.BlockSpec((None,) + dims, lambda s: (s + first,) + (0,) * len(dims))


def grid_call(kernel, seqs, in_specs, out_specs, out_shape, scratch, cost, into=()):
    given = len(in_specs)

    def filling(*refs):
        kernel(*refs[:given], *refs[given + len(into) :])

    call = pl.pallas_call(
        filling,
        grid=(seqs,),
        in_specs=in_specs + [pl.BlockSpec(memory_space=pl.ANY)] * len(into),
        input_output_aliases={given + at: at for at in range(len(into))},
        out_specs=out_specs,
        out_shape=out_shape,
        scratch_shapes=scratch,
        compiler_params=pltpu.CompilerParams(
            vmem_limit_bytes=vmem_limit, dimension_semantics=("arbitrary",)
        ),
        cost_estimate=pl.CostEstimate(flops=cost, bytes_accessed=cost, transcendentals=0),
    )
    return lambda *operands: call(*operands, *into)


def cheap(width):
    return pltpu.CompilerParams(vmem_limit_bytes=vmem_limit, dimension_semantics=("arbitrary",)), (
        pl.CostEstimate(flops=width, bytes_accessed=width, transcendentals=0)
    )


def product_kernel(at_ref, left_ref, *refs, dot):
    *right_refs, out_ref = refs
    width = out_ref.shape[1] // len(right_refs)
    for at, right_ref in enumerate(right_refs):
        part = dot(left_ref[...], right_ref[...])
        out_ref[:, at * width : (at + 1) * width] = part.astype(out_ref.dtype)


def product(dot, left, right, dtype, start=0, rows=None):
    depth, total = left.shape if dot is tn else left.shape[::-1]
    rows = total if rows is None else rows
    size = rows // 2 if rows % 256 == 0 else rows
    rights = list(right) if isinstance(right, (list, tuple)) else [right]
    cols = rights[0].shape[0] if dot is nt else rights[0].shape[1]
    cols = cols * len(rights)
    if dot is tn:
        left_spec = pl.BlockSpec((depth, size), lambda i, at: (0, at[0] + i))
    else:
        left_spec = pl.BlockSpec((size, depth), lambda i, at: (at[0] + i, 0))
    params, cost = cheap(10**5)
    return pl.pallas_call(
        functools.partial(product_kernel, dot=dot),
        grid_spec=pltpu.PrefetchScalarGridSpec(
            num_scalar_prefetch=1,
            grid=(rows // size,),
            in_specs=[left_spec]
            + [pl.BlockSpec(one.shape, lambda i, at: (0, 0)) for one in rights],
            out_specs=pl.BlockSpec((size, cols), lambda i, at: (i, 0)),
        ),
        out_shape=jax.ShapeDtypeStruct((rows, cols), dtype),
        compiler_params=params,
        cost_estimate=cost,
    )(jnp.asarray(start // size, jnp.int32).reshape(1), left, *rights)


def rows_kernel(
    taps_grad_ref, gain_grad_ref, heads_grad_ref, step_grad_ref, shared_ref, out_ref, rows_buf
):
    width = rows_buf.shape[1]
    rows_buf[...] = jnp.zeros_like(rows_buf)
    rows_buf[0:8, :] = jnp.sum(taps_grad_ref[...], axis=0)
    rows_buf[8:9, :] = jnp.sum(gain_grad_ref[...], axis=0)[0:1, :]
    rows_buf[9:12, 0:lanes] = jnp.sum(heads_grad_ref[...], axis=0)[0:3, :]
    for at, column in enumerate(spans(step_grad_ref.shape[1], width)):
        rows_buf[16 * (at + 1) : 16 * (at + 2), :] = step_grad_ref[0:16, column]
    shared = jnp.sum(shared_ref[...], axis=0)
    count, _, wide = out_ref.shape
    part = shared.shape[0] // count
    for at in range(count):
        rows = rows_buf[8 * at : 8 * at + 8, :]
        pieces = [rows[:, column] for column in spans(width, wide)]
        pieces = pieces + [jnp.zeros((8, wide), f32)] * (4 - len(pieces))
        out_ref[at, 0:32, :] = jnp.concatenate(pieces, axis=0).astype(bf16)
        out_ref[at, 32:, :] = shared[at * part : (at + 1) * part, :].astype(bf16)


def pieces_kernel(*refs):
    *pairs, out_ref = refs
    count = len(pairs) // 2
    out = nt(pairs[0][...], pairs[count][...])
    for at in range(1, count):
        out = out + nt(pairs[at][...], pairs[count + at][...])
    out_ref[...] = out.astype(out_ref.dtype)


def pieces_product(lefts, rights, dtype):
    tokens, cols = lefts[0].shape[0], rights[0].shape[0]
    size = tokens // 4
    params, cost = cheap(10**5)
    return pl.pallas_call(
        pieces_kernel,
        grid=(tokens // size,),
        in_specs=[pl.BlockSpec((size, left.shape[1]), lambda i: (i, 0)) for left in lefts]
        + [pl.BlockSpec(right.shape, lambda i: (0, 0)) for right in rights],
        out_specs=pl.BlockSpec((size, cols), lambda i: (i, 0)),
        out_shape=jax.ShapeDtypeStruct((tokens, cols), dtype),
        compiler_params=params,
        cost_estimate=cost,
    )(*lefts, *rights)


def shared_grad_kernel(own_ref, normed_ref, d_shared_ref, taps_grad_ref, out_ref):
    rows, (padded, wide) = normed_ref.shape[1], out_ref.shape
    out_ref[0:rows, :] = tn(normed_ref[...], d_shared_ref[...])
    out_ref[rows:, :] = jnp.zeros((padded - rows, wide), f32)

    @pl.when(pl.program_id(0) == 0)
    def _():
        out_ref[rows : rows + 8, :] = taps_grad_ref[...]


def shared_product(own, normed, d_shared, taps_grad, count, padded):
    tokens, wide = d_shared.shape
    rows = normed.shape[1] // count
    params, cost = cheap(10**5)
    return pl.pallas_call(
        shared_grad_kernel,
        grid_spec=pltpu.PrefetchScalarGridSpec(
            num_scalar_prefetch=1,
            grid=(count,),
            in_specs=[
                pl.BlockSpec((tokens, rows), lambda i, own: (own[0], i)),
                pl.BlockSpec((tokens, wide), lambda i, own: (0, 0)),
                pl.BlockSpec((8, wide), lambda i, own: (0, 0)),
            ],
            out_specs=pl.BlockSpec((padded, wide), lambda i, own: (i, 0)),
        ),
        out_shape=jax.ShapeDtypeStruct((count * padded, wide), f32),
        compiler_params=params,
        cost_estimate=cost,
    )(own.reshape(1), normed, d_shared, taps_grad)


def back_kernel(
    places_ref, gate_ref, inner_ref, raw_ref, shared_ref, gate_w_ref, inner_w_ref, step_w_ref,
    shared_w_ref, far_ref, near_ref, out_buf,
    *, per_device, count,
):
    out = nt(gate_ref[...], gate_w_ref[...]) + nt(inner_ref[...], inner_w_ref[...])
    out_buf[...] = out + nn(raw_ref[:, : step_w_ref.shape[0]], step_w_ref[...])

    @pl.when(pl.program_id(0) // per_device == places_ref[count])
    def _():
        out_buf[...] = out_buf[...] + nt(shared_ref[...], shared_w_ref[...])

    size = out_buf.shape[1] // count
    for ref, first in ((near_ref, 0), (far_ref, count // 2)):
        for at in range(count // 2):
            start = pl.multiple_of(places_ref[first + at] * size, lanes)
            ref[:, at * size : (at + 1) * size] = out_buf[:, pl.ds(start, size)].astype(bf16)


def back_product(blocks, mine, gate, inner, raw, shared, gate_w, inner_w, step_w, shared_w):
    seqs, length, _ = gate.shape
    cols, per_device = gate_w.shape[0], shared.shape[0]

    def at_seq(array):
        return pl.BlockSpec((None, length, array.shape[2]), lambda s, at: (s, 0, 0))

    def at_all(array):
        return pl.BlockSpec(array.shape, lambda s, at: (0, 0))

    own = pl.BlockSpec(
        (None, length, shared.shape[2]), lambda s, at: (lax.rem(s, per_device), 0, 0)
    )
    half = pl.BlockSpec((length, cols // 2), lambda s, at: (s, 0))
    params, cost = cheap(10**5)
    return pl.pallas_call(
        functools.partial(back_kernel, per_device=per_device, count=len(blocks)),
        grid_spec=pltpu.PrefetchScalarGridSpec(
            num_scalar_prefetch=1,
            grid=(seqs,),
            in_specs=[at_seq(gate), at_seq(inner), at_seq(raw), own]
            + [at_all(weight) for weight in (gate_w, inner_w, step_w, shared_w)],
            out_specs=[half, half],
            scratch_shapes=[pltpu.VMEM((length, cols), f32)],
        ),
        out_shape=[jax.ShapeDtypeStruct((seqs * length, cols // 2), bf16)] * 2,
        compiler_params=params,
        cost_estimate=cost,
    )(
        jnp.stack(blocks + [mine]), gate, inner, raw, shared, gate_w, inner_w, step_w, shared_w
    )


def assemble_kernel(place_ref, *refs):
    pieces, out_ref = refs[:-1], refs[-1]
    for at, piece in enumerate(pieces):

        @pl.when(pl.program_id(0) == at)
        def _(piece=piece):
            out_ref[...] = piece[...].astype(out_ref.dtype)


def assembled(pieces, rank, dtype, column_from=None, columns=1):
    count, (size, width) = len(pieces), pieces[0].shape
    block = width // columns
    if column_from is None:
        column_from = [jnp.int32(at) for at in range(columns)]
    place = jnp.stack([jnp.asarray(rank, jnp.int32)] + [at.astype(jnp.int32) for at in column_from])
    params, cost = cheap(10**5)
    params = pltpu.CompilerParams(
        vmem_limit_bytes=vmem_limit, dimension_semantics=("arbitrary", "arbitrary")
    )
    return pl.pallas_call(
        assemble_kernel,
        grid_spec=pltpu.PrefetchScalarGridSpec(
            num_scalar_prefetch=1,
            grid=(count, columns),
            in_specs=[
                pl.BlockSpec(
                    (size, block),
                    lambda i, j, at, own=own: (0, jnp.where(i == own, at[1 + j], 0)),
                )
                for own in range(count)
            ],
            out_specs=pl.BlockSpec((size, block), lambda i, j, at: (at[0] ^ i, j)),
        ),
        out_shape=jax.ShapeDtypeStruct((count * size, width), dtype),
        compiler_params=params,
        cost_estimate=cost,
    )(place, *pieces)


def spans(total, width):
    return [slice(at, at + width) for at in range(0, total, width)]


def project_kernel(
    hidden_ref, gain_ref, inner_w_ref, shared_w_ref, step_w_ref, step_bias_ref, rate_ref,
    normed_ref, inner_ref, shared_ref, raw_ref, inv_ref, ends_ref, total_ref,
):
    length = hidden_ref.shape[0]
    heads = step_w_ref.shape[0]
    for rows in spans(length, chunk):
        hidden = hidden_ref[rows, :].astype(f32)
        inv = lax.rsqrt(jnp.mean(hidden * hidden, axis=1, keepdims=True) + epsilon)
        normed_ref[rows, :] = (hidden * inv * gain_ref[...][None, :]).astype(bf16)
        inv_ref[rows, :] = jnp.broadcast_to(inv, (chunk, lanes))
    normed = normed_ref[...]
    inner_ref[...] = nn(normed, inner_w_ref[...])
    shared_ref[...] = nn(normed, shared_w_ref[...])
    raw_ref[...] = jnp.zeros((length, lanes), f32)
    raw_ref[:, :heads] = nt(normed, step_w_ref[...])
    decays = softplus(raw_ref[...] + step_bias_ref[...]) * rate_ref[...]
    total_ref[...] = jnp.broadcast_to(jnp.sum(decays, axis=0, keepdims=True), (8, lanes))
    split = inner_ref.shape[1]
    ends_ref[:, :split] = inner_ref[length - rim :, :]
    ends_ref[:, split:] = shared_ref[length - rim :, :]


def filter_forward(buffer, taps_ref, bias_ref, start, column, taps):
    summed = bias_ref[0:1, column]
    for tap in range(taps):
        summed = summed + taps_ref[tap : tap + 1, column] * buffer[
            pl.ds(rim + start - taps + 1 + tap, chunk), column
        ]
    s = sigmoid(summed)
    return summed * s, s * (1.0 + summed * (1.0 - s))


def states_kernel(
    inner_ref, rims_ref, shared_ref, raw_ref,
    taps_ref, bias_ref, taps_s_ref, bias_s_ref, step_bias_ref, rate_ref, spread_ref, _,
    x_ref, slope_ref, shared_act_ref, slope_s_ref, step_ref, decay_ref, decay_t_ref, local_ref,
    state_ref,
    inner_buf, shared_buf, act_buf,
    *, taps, states,
):
    length, width = inner_ref.shape
    inner_buf[0:rim, :] = rims_ref[:, :width]
    inner_buf[rim:, :] = inner_ref[...]
    shared_buf[0:rim, :] = rims_ref[:, width:]
    shared_buf[rim:, :] = shared_ref[...]
    upto = triangle_of("upto")
    spread = spread_ref[...]
    base = jnp.zeros((1, lanes), f32)
    state = jnp.zeros((states, width), f32)
    for index, rows in enumerate(spans(length, chunk)):
        for column in spans(width, lanes):
            value, slope = filter_forward(
                inner_buf, taps_ref, bias_ref, rows.start, column, taps
            )
            x_ref[rows, column] = value
            slope_ref[rows, column] = slope.astype(bf16)
        for column in spans(2 * states, lanes):
            value, slope = filter_forward(
                shared_buf, taps_s_ref, bias_s_ref, rows.start, column, taps
            )
            shared_act_ref[rows, column] = value.astype(bf16)
            slope_s_ref[rows, column] = slope
        step = softplus(raw_ref[rows, :] + step_bias_ref[...])
        local = summed_by(upto, step * rate_ref[...])
        last = local[chunk - 1 : chunk, :]
        step_ref[rows, :] = step
        decay = local + base
        decay_ref[rows, :] = decay
        decay_t_ref[:, rows] = jnp.transpose(decay)[:16, :]
        weight = nn(two_parts(jnp.exp(last - local) * step), spread)
        act_buf[...] = (weight * x_ref[rows, :]).astype(bf16)
        local_ref[index, :, :] = state.astype(bf16)
        kept = nn(two_parts(jnp.broadcast_to(jnp.exp(last), (8, lanes))), spread)[0:1, :]
        state = kept * state + tn(shared_act_ref[rows, 0:states], act_buf[...])
        base = base + last
    state_ref[...] = state.astype(bf16)


def pair_masks():
    low = iota((chunk, lanes), 1) < lanes // 2
    return low, jnp.logical_not(low)


def halves(value, masks):
    zero = jnp.zeros_like(value)
    return jnp.concatenate(
        [jnp.where(masks[0], value, zero), jnp.where(masks[1], value, zero)], axis=0
    )


def fade(decay, decay_t, head, causal):
    gap = decay[:, head : head + 1] - decay_t[head : head + 1, :]
    return jnp.exp(jnp.where(causal, gap, -1e30))


def mix_kernel(
    x_ref, shared_act_ref, step_ref, decay_ref, decay_t_ref, local_ref, skip_ref, spread_ref,
    out_ref,
    *, states,
):
    length, width = x_ref.shape
    causal = iota((chunk, chunk), 0) >= iota((chunk, chunk), 1)
    masks = pair_masks()
    spread = spread_ref[...]
    base = jnp.zeros((1, lanes), f32)
    for index, rows in enumerate(spans(length, chunk)):
        b, c = shared_act_ref[rows, 0:states], shared_act_ref[rows, states:]
        scores = nt(c, b)
        x = x_ref[rows, :]
        decay = decay_ref[rows, :]
        decay_t = decay_t_ref[:, rows]
        stepped = (x * nn(two_parts(step_ref[rows, :]), spread)).astype(bf16)
        out = skip_ref[...] * x
        if index > 0:
            out = out + nn(two_parts(jnp.exp(decay - base)), spread) * nn(c, local_ref[index])
        base = decay[chunk - 1 : chunk, :]
        for pair, column in enumerate(spans(width, lanes)):
            mixing = jnp.concatenate(
                [
                    (fade(decay, decay_t, 2 * pair + side, causal) * scores).astype(bf16)
                    for side in range(2)
                ],
                axis=1,
            )
            part = nn(mixing, halves(stepped[:, column], masks))
            out_ref[rows, column] = out[:, column] + part


def gate_kernel(
    local_out_ref, shared_act_ref, decay_ref, state_in_ref, gate_ref, mixer_grad_ref, gain_ref,
    spread_ref,
    out_ref, sums_ref,
    square_buf, product_buf,
    *, states,
):
    length, width = local_out_ref.shape
    spread = spread_ref[...]
    for rows in spans(length, chunk):
        faded = nn(two_parts(jnp.exp(decay_ref[rows, :])), spread)
        out = local_out_ref[rows, :] + faded * nn(
            shared_act_ref[rows, states:], state_in_ref[...]
        )
        out_ref[rows, :] = out
        gate = gate_ref[rows, :]
        gated = out * gate * sigmoid(gate)
        square_buf[rows, :] = (gated * gated).astype(bf16)
        product_buf[rows, :] = (
            gated * mixer_grad_ref[rows, :] * gain_ref[...]
        ).astype(bf16)
    ones = jnp.ones((8, width), bf16)
    first = nt(ones, square_buf[...])
    second = nt(ones, product_buf[...])
    sums_ref[...] = jnp.where(iota((8, length), 0) < 4, first, second)


def gate_back_kernel(
    out_ref, gate_ref, mixer_grad_ref, sums_ref, gain_ref, shared_act_ref, decay_ref, spread_ref,
    mixer_in_ref, d_gate_ref, d_ssm_ref, lam_ref, gain_grad_ref,
    *, states, full,
):
    length, width = out_ref.shape
    spread = spread_ref[...]
    gain = gain_ref[...]
    summed = jnp.sum(sums_ref[...], axis=0)
    square = summed[0:1, :] * (1.0 / full)
    product = summed[4:5, :] * (1.0 / full)
    rms = lax.rsqrt(square + epsilon)
    scalars = jnp.concatenate([rms, rms * rms * rms * product, jnp.zeros((6, length), f32)], axis=0)
    gain_grad = jnp.zeros((1, width), f32)
    lam = jnp.zeros((states, width), f32)
    for rows in spans(length, chunk):
        columns = jnp.transpose(scalars[:, rows])
        rms_c, row_c = columns[:, 0:1], columns[:, 1:2]
        out = out_ref[rows, :]
        gate = gate_ref[rows, :]
        mixer_grad = mixer_grad_ref[rows, :]
        s = sigmoid(gate)
        act = gate * s
        gated = out * act
        normal = gated * rms_c
        mixer_in_ref[rows, :] = (normal * gain).astype(bf16)
        gain_grad = gain_grad + jnp.sum(mixer_grad * normal, axis=0, keepdims=True)
        d_gated = rms_c * (mixer_grad * gain) - gated * row_c
        d_ssm = d_gated * act
        d_ssm_ref[rows, :] = d_ssm
        d_gate_ref[rows, :] = (d_gated * out * s * (1.0 + gate * (1.0 - s))).astype(bf16)
        faded = nn(two_parts(jnp.exp(decay_ref[rows, :])), spread)
        lam = lam + tn(shared_act_ref[rows, states:], (faded * d_ssm).astype(bf16))
    lam_ref[...] = lam.astype(bf16)
    gain_grad_ref[...] = jnp.broadcast_to(gain_grad, (8, width))


def mix_back_kernel(
    x_ref, shared_act_ref, step_ref, decay_ref, decay_t_ref, local_ref, state_in_ref, d_ssm_ref,
    spread_ref, gather_ref,
    d_x_ref, d_shared_ref, d_decay_ref,
    column_buf,
    *, states,
):
    length, width = x_ref.shape
    causal = iota((chunk, chunk), 0) >= iota((chunk, chunk), 1)
    masks = pair_masks()
    spread, gather = spread_ref[...], gather_ref[...]
    since, before = triangle_of("from"), triangle_of("before")
    lam = jnp.zeros((states, width), f32)
    heads_here = 2 * (width // lanes)
    column_buf[...] = jnp.zeros_like(column_buf)
    row_at, col_at = iota((2 * chunk, lanes), 0), iota((2 * chunk, lanes), 1)
    all_rows = spans(length, chunk)
    for index in reversed(range(len(all_rows))):
        rows = all_rows[index]
        b, c = shared_act_ref[rows, 0:states], shared_act_ref[rows, states:]
        xf = x_ref[rows, :]
        d_out = d_ssm_ref[rows, :]
        decay = decay_ref[rows, :]
        decay_t = decay_t_ref[:, rows]
        step = step_ref[rows, :]
        if index > 0:
            base = decay_ref[rows.start - 1 : rows.start, :]
        else:
            base = jnp.zeros((1, lanes), f32)
        last = decay[chunk - 1 : chunk, :]
        heads = jnp.concatenate([jnp.exp(base), jnp.exp(last - base), jnp.zeros((6, lanes), f32)])
        heads = nn(two_parts(heads), spread)
        entered = local_ref[index].astype(f32) + heads[0:1, :] * state_in_ref[...].astype(f32)
        entered16 = entered.astype(bf16)
        lam16 = lam.astype(bf16)
        scores = nt(c, b)
        faded = nn(two_parts(jnp.exp(decay - base)), spread)
        fading = nn(two_parts(jnp.exp(last - decay)), spread)
        steps = nn(two_parts(step), spread)
        stepped = (xf * steps).astype(bf16)
        d_faded = (faded * d_out).astype(bf16)
        x_faded = (fading * steps * xf).astype(bf16)
        d_c = nt(d_faded, entered16) + nt(d_faded, rest_of(entered))
        d_b = nt(x_faded, lam16) + nt(x_faded, rest_of(lam))
        carried = nn(c, entered16)
        carrying = nn(b, lam16)
        queries = nn((d_faded.astype(f32) * carried).astype(bf16), gather)
        keys = nn((x_faded.astype(f32) * carrying).astype(bf16), gather)
        across = jnp.sum(lam * entered, axis=0, keepdims=True) * heads[1:2, :]
        across = nn(jnp.broadcast_to(across, (8, width)).astype(bf16), gather)[0:1, :]
        d_x = fading * carrying
        d_scores = jnp.zeros((chunk, chunk), f32)
        for pair, column in enumerate(spans(width, lanes)):
            d_stack = halves(d_out[:, column].astype(bf16), masks)
            d_mixing = nt(d_stack, stepped[:, column])
            mixed, grads = [], []
            for side in range(2):
                head = 2 * pair + side
                faint = fade(decay, decay_t, head, causal)
                d_score = faint * d_mixing[side * chunk : (side + 1) * chunk, :]
                d_scores = d_scores + d_score
                mixed.append((faint * scores).astype(bf16))
                grad = (d_score * scores).astype(bf16)
                grads.append(grad)
                column_buf[head : head + 1, :] = jnp.sum(
                    grad.astype(f32), axis=0, keepdims=True
                )
            code = jnp.where(col_at == 2 * pair + row_at // chunk, 1.0, 0.0).astype(bf16)
            queries = queries + nn(jnp.concatenate(grads, axis=1), code)
            part = tn(jnp.concatenate(mixed, axis=0), d_stack)
            d_x_ref[rows, column] = d_x[:, column] + part
        queries = queries - jnp.transpose(column_buf[...])
        d_decay_ref[rows, :] = summed_by(since, queries) + summed_by(before, keys) + across
        d_scores16, d_rest = d_scores.astype(bf16), rest_of(d_scores)
        d_shared_ref[rows, 0:states] = d_b + tn(d_scores16, c) + tn(d_rest, c)
        d_shared_ref[rows, states:] = d_c + nn(d_scores16, b) + nn(d_rest, b)
        lam = heads[1:2, :] * lam + tn(c, d_faded)


def filter_backward(buffer, taps_ref, start, size, column, taps):
    total = None
    for tap in range(taps):
        term = taps_ref[tap : tap + 1, column] * buffer[
            pl.ds(rim + start + taps - 1 - tap, size), column
        ]
        total = term if total is None else total + term
    return total


def filter_adjoint(buffer, inner_buf, taps_ref, length, width, taps, body_ref, edge_ref, tail_ref,
                   taps_grad_ref):
    for column in spans(width, lanes):
        edge_ref[:, column] = filter_backward(buffer, taps_ref, -rim, rim, column, taps).astype(
            bf16
        )
        rows_grad = [jnp.zeros((8, lanes), f32) for _ in range(taps + 1)]
        for rows in spans(length, chunk):
            body = filter_backward(buffer, taps_ref, rows.start, chunk, column, taps)
            body_ref[rows, column] = body.astype(bf16)
            if rows.stop == length:
                tail_ref[:, column] = body[chunk - rim :, :]
            grad = buffer[pl.ds(rim + rows.start, chunk), column]
            for tap in range(taps):
                moved = inner_buf[pl.ds(rim + rows.start - taps + 1 + tap, chunk), column]
                rows_grad[tap] = rows_grad[tap] + jnp.sum(
                    (grad * moved).reshape(chunk // 8, 8, lanes), axis=0
                )
            rows_grad[taps] = rows_grad[taps] + jnp.sum(
                grad.reshape(chunk // 8, 8, lanes), axis=0
            )
        sums = [jnp.sum(part, axis=0, keepdims=True) for part in rows_grad]
        sums.append(jnp.zeros((8 - taps - 1, lanes), f32))
        taps_grad_ref[:, column] = jnp.concatenate(sums, axis=0)


def act_kernel(
    x_ref, step_ref, decay_ref, d_shared_ref, later_ref, spread_ref, out_ref, *, states
):
    length = x_ref.shape[0]
    last = decay_ref[length - 1 : length, :]
    weight = nn(two_parts(jnp.exp(last - decay_ref[...]) * step_ref[...]), spread_ref[...])
    weighted, later = x_ref[...] * weight, later_ref[...]
    d_b = nt(weighted.astype(bf16), later) + nt(rest_of(weighted), later)
    out_ref[:, 0:states] = d_shared_ref[:, 0:states] + d_b
    out_ref[:, states:] = d_shared_ref[:, states:]


def finish_kernel(
    x_ref, slope_ref, shared_act_ref, raw_ref, step_ref, decay_ref, d_x_ref,
    d_decay_ref, d_ssm_ref, state_in_ref, later_ref, inner_ref, rims_ref,
    taps_ref, step_bias_ref, rate_ref, skip_ref, spread_ref, gather_ref,
    body_ref, edge_ref, tail_ref, taps_grad_ref, d_raw_ref, heads_ref,
    grad_buf, inner_buf,
    *, taps, states,
):
    length, width = x_ref.shape
    spread, gather = spread_ref[...], gather_ref[...]
    before = triangle_of("before")
    later = later_ref[...]
    grad_buf[0:rim, :] = jnp.zeros((rim, width), f32)
    grad_buf[rim + length :, :] = jnp.zeros((rim, width), f32)
    inner_buf[0:rim, :] = rims_ref[:, :width]
    inner_buf[rim:, :] = inner_ref[...]
    last = decay_ref[length - 1 : length, :]
    final = nn(two_parts(jnp.broadcast_to(jnp.exp(last), (8, lanes))), spread)[0:1, :]
    across = final * jnp.sum(
        later.astype(f32) * state_in_ref[...].astype(f32), axis=0, keepdims=True
    )
    running = nn(jnp.broadcast_to(across, (8, width)).astype(bf16), gather)[0:1, :]
    skip = skip_ref[...]
    skip_grad = jnp.zeros((1, width), f32)
    rate_grad = jnp.zeros((1, lanes), f32)
    bias_grad = jnp.zeros((1, lanes), f32)
    for rows in spans(length, chunk):
        b = shared_act_ref[rows, 0:states]
        x = x_ref[rows, :]
        step = step_ref[rows, :]
        d_ssm = d_ssm_ref[rows, :]
        fading = nn(two_parts(jnp.exp(last - decay_ref[rows, :])), spread)
        steps = nn(two_parts(step), spread)
        carrying = fading * nn(b, later)
        x_stepped = x * steps
        keys = nn((x_stepped * carrying).astype(bf16), gather)
        d_x = d_x_ref[rows, :] + carrying
        direct = nn((x * d_x).astype(bf16), gather)
        d_decay = d_decay_ref[rows, :] + running + summed_by(before, keys)
        running = running + jnp.sum(keys, axis=0, keepdims=True)
        skip_grad = skip_grad + jnp.sum(d_ssm * x, axis=0, keepdims=True)
        rate_grad = rate_grad + jnp.sum(step * d_decay, axis=0, keepdims=True)
        d_raw = (direct + rate_ref[...] * d_decay) * sigmoid(
            raw_ref[rows, :] + step_bias_ref[...]
        )
        d_raw_ref[rows, :] = d_raw.astype(bf16)
        bias_grad = bias_grad + jnp.sum(d_raw, axis=0, keepdims=True)
        grad_buf[pl.ds(rim + rows.start, chunk), :] = (
            skip * d_ssm + steps * d_x
        ) * slope_ref[rows, :].astype(f32)
    parts = two_parts(jnp.broadcast_to(skip_grad, (8, width)))
    skip_heads = nn(parts[:, :width], gather) + nn(parts[:, width:], gather)
    heads_ref[...] = jnp.concatenate(
        [bias_grad, rate_grad * rate_ref[...], skip_heads[0:1, :], jnp.zeros((5, lanes), f32)],
        axis=0,
    )
    filter_adjoint(
        grad_buf, inner_buf, taps_ref, length, width, taps, body_ref, edge_ref, tail_ref,
        taps_grad_ref,
    )


def shared_kernel(
    first_ref, d_act_ref, slope_ref, shared_ref, rim_ref, taps_ref,
    body_ref, edge_ref, tail_ref, taps_grad_ref,
    grad_buf, inner_buf,
    *, taps,
):
    _, length, width = d_act_ref.shape
    grad_buf[0:rim, :] = jnp.zeros((rim, width), f32)
    grad_buf[rim + length :, :] = jnp.zeros((rim, width), f32)
    inner_buf[0:rim, :] = rim_ref[:, rim_ref.shape[1] - width :]
    inner_buf[rim:, :] = shared_ref[...]
    grad_buf[rim : rim + length, :] = jnp.sum(d_act_ref[...], axis=0) * slope_ref[...]
    filter_adjoint(
        grad_buf, inner_buf, taps_ref, length, width, taps, body_ref, edge_ref, tail_ref,
        taps_grad_ref,
    )


def chain_kernel(pieces_ref, totals_ref, spread_ref, out_ref, *, backward):
    count = pieces_ref.shape[0]
    decays = nn(two_parts(jnp.exp(totals_ref[...])), spread_ref[...])
    state = jnp.zeros(pieces_ref.shape[1:], f32)
    order = reversed(range(count)) if backward else range(count)
    for block in order:
        out_ref[block, :, :] = state.astype(bf16)
        state = decays[block : block + 1, :] * state + pieces_ref[block].astype(f32)


def after(ready, *values):
    if not ready:
        return values if len(values) > 1 else values[0]
    tied = lax.optimization_barrier((tuple(ready), tuple(values)))[1]
    return tied if len(values) > 1 else tied[0]


def landed(ready, *transfers):
    flat = [value for transfer in transfers for value in transfer]
    flat = list(lax.optimization_barrier((tuple(ready), tuple(flat)))[1])
    return [[flat.pop(0) for _ in transfer] for transfer in transfers]


def bits_of(axis):
    return [1 << bit for bit in range(lax.axis_size(axis).bit_length() - 1)]


def swapped(value, axis, bit):
    size = lax.axis_size(axis)
    return lax.ppermute(value, axis, [(i, i ^ bit) for i in range(size)])


def passed_along(value, axis, by):
    size = lax.axis_size(axis)
    pairs = [(i, i + by) for i in range(size) if 0 <= i + by < size]
    return lax.ppermute(value, axis, pairs)


def block_at(value, index, size, dim):
    return lax.dynamic_slice_in_dim(value, index * size, size, dim)


def reversed_order(axis):
    order = [0]
    for bit in reversed(bits_of(axis)):
        order = order + [at + bit for at in order]
    return order


def relative_blocks(value, axis, dim):
    count, mine = lax.axis_size(axis), lax.axis_index(axis)
    size = value.shape[dim] // count
    blocks = [block_at(value, mine ^ other, size, dim) for other in reversed_order(axis)]
    half = len(blocks) // 2
    return [
        jnp.concatenate(blocks[:half], axis=dim),
        jnp.concatenate(blocks[half:], axis=dim),
    ]


def gathered_relative(value, axis, dim, ready=()):
    for bit in reversed(bits_of(axis)):
        value = jnp.concatenate([value, after(ready, swapped(value, axis, bit))], axis=dim)
    return value


def halves_added(kept, got, dim):
    half = got.shape[dim] // 2
    parts = [
        lax.slice_in_dim(value, at * half, (at + 1) * half, axis=dim)
        for at in range(2)
        for value in (kept, got)
    ]
    return parts[0].astype(f32) + parts[1].astype(f32), parts[2].astype(f32) + parts[3].astype(f32)


def in_place_order(value, axis, dim):
    count, mine = lax.axis_size(axis), lax.axis_index(axis)
    size = value.shape[dim] // count
    bits = bits_of(axis)

    def place(at):
        return sum(((at // bit) % 2) * back for bit, back in zip(bits, reversed(bits)))

    return jnp.concatenate(
        [block_at(value, place(mine ^ other), size, dim) for other in range(count)], axis=dim
    )


def rank_in(axis, group):
    mine = lax.axis_index(axis)
    return sum(((mine // bit) % 2) << at for at, bit in enumerate(group))


def mask_of(group, distance):
    return sum(bit for at, bit in enumerate(group) if distance >> at & 1)


class Reduction:
    def __init__(self, value, axis, groups, wire=bf16, halves=None):
        self.axis, self.wire, self.value = axis, wire, value
        self.left, self.taken = list(groups), []
        if halves is None:
            self.split()
        else:
            self.kept, self.sent = halves[0], [halves[1]]

    def split(self):
        if self.left:
            count = 1 << len(self.left[0])
            rank = rank_in(self.axis, self.left[0])
            size = self.value.shape[0] // count
            self.kept = block_at(self.value, rank, size, 0)
            self.sent = [
                block_at(self.value, rank ^ other, size, 0).astype(self.wire)
                for other in range(1, count)
            ]
        else:
            self.value = self.value.astype(bf16)
            self.sent = [self.value]

    def start(self):
        group = self.left[0] if self.left else self.taken[-1]
        count = 1 << len(group)
        sent = self.sent if self.left else self.sent * (count - 1)
        return [
            swapped(value, self.axis, mask_of(group, other))
            for other, value in enumerate(sent, 1)
        ]

    def take(self, got, *columns):
        if self.left:
            self.taken.append(self.left.pop(0))
            total = self.kept.astype(f32)
            for value in got:
                total = total + value.astype(f32)
            self.value = total.astype(self.wire)
        else:
            group = self.taken.pop()
            rank = rank_in(self.axis, group)
            if self.taken:
                self.value = assembled([self.value] + got, rank, bf16)
            else:
                self.value = assembled([self.value] + got, rank, f32, *columns)
        if self.left or self.taken:
            self.split()
            return self.sent
        return [self.value]


def exchanged_sum(value, axis):
    for bit in bits_of(axis):
        value = (value.astype(f32) + swapped(value, axis, bit).astype(f32)).astype(value.dtype)
    return value


def exchanged_all(value, axis):
    mine = lax.axis_index(axis)
    value = value[None]
    for bit in bits_of(axis):
        got = swapped(value, axis, bit)
        low = (mine // bit) % 2 == 0
        value = jnp.concatenate([jnp.where(low, value, got), jnp.where(low, got, value)], axis=0)
    return value


def to_owners(state):
    count, width = lax.axis_size("seq"), state.shape[-1]
    return [lax.all_to_all(state.reshape(count, -1, width), "seq", 0, 0, tiled=True)]


def chained(pieces, totals, states, spread, backward):
    count, size, width = pieces.shape
    mine = lax.axis_index("seq")
    here = lax.dynamic_index_in_dim(totals, mine * size // states, 1, keepdims=False)
    params, cost = cheap(10**5)
    return pl.pallas_call(
        functools.partial(chain_kernel, backward=backward),
        out_shape=jax.ShapeDtypeStruct((count, size, width), bf16),
        compiler_params=pltpu.CompilerParams(vmem_limit_bytes=vmem_limit),
        cost_estimate=cost,
    )(pieces, here, spread)


def shares_sent(value, axes):
    count = lax.axis_size(axes)
    return [lax.all_to_all(value.reshape(count, -1, value.shape[-1]), axes, 0, 0, tiled=True)]


def shares_back(pieces, axes):
    total = jnp.sum(pieces.astype(f32), axis=0, keepdims=True).astype(bf16)
    return [lax.all_to_all(jnp.broadcast_to(total, pieces.shape), axes, 0, 0, tiled=True)]


def to_blocks(scanned):
    return [lax.all_to_all(scanned, "seq", 0, 0, tiled=True)]


def on_device(
    hidden_in, norm_gain, proj_gate, proj_inner, proj_step, proj_shared, filter_inner,
    filter_inner_bias, filter_shared, filter_shared_bias, step_bias, log_rate, skip_gain,
    gate_gain, proj_out, cotangent,
):
    seqs, length, width_d = hidden_in.shape
    width = proj_gate.shape[1]
    heads = proj_step.shape[1]
    per_head = width // heads
    states = proj_shared.shape[1] // 2
    taps = filter_inner.shape[0]
    count_h = lax.axis_size("head")
    mine_h = lax.axis_index("head")
    full = width * count_h
    columns = width_d // count_h
    tokens = seqs * length
    per_device_seqs = seqs // count_h

    spread_np = np.zeros((2 * lanes, width), np.float32)
    for head in range(heads):
        spread_np[head, head * per_head : (head + 1) * per_head] = 1
        spread_np[lanes + head, head * per_head : (head + 1) * per_head] = 1
    spread = jnp.asarray(spread_np, bf16)
    gather = jnp.asarray(spread_np[:lanes].T, bf16)

    def on_lanes(vector):
        return jnp.pad(vector.astype(f32), (0, lanes - heads)).reshape(1, lanes)

    rate = on_lanes(-jnp.exp(log_rate))
    bias_row = on_lanes(step_bias)
    skip_row = jnp.repeat(skip_gain, per_head).reshape(1, width)
    gain_row = gate_gain.reshape(1, width)

    shape = jax.ShapeDtypeStruct
    wide = per_seq(length, width)
    narrow = per_seq(length, 2 * states)
    slim = per_seq(length, lanes)
    slim_t = per_seq(16, length)
    state_spec = per_seq(states, width)
    chunks = length // chunk

    normed, inner_pre, shared_pre, step_raw, inv_rms, ends, total = grid_call(
        project_kernel,
        seqs,
        [
            per_seq(length, width_d), whole((width_d,)), whole((width_d, width)),
            whole((width_d, 2 * states)), whole((heads, width_d)), whole((1, lanes)),
            whole((1, lanes)),
        ],
        [
            per_seq(length, width_d), wide, narrow, slim, slim, per_seq(rim, width + 2 * states),
            per_seq(8, lanes),
        ],
        [
            shape((seqs, length, width_d), bf16),
            shape((seqs, length, width), f32),
            shape((seqs, length, 2 * states), f32),
            shape((seqs, length, lanes), f32),
            shape((seqs, length, lanes), f32),
            shape((seqs, rim, width + 2 * states), f32),
            shape((seqs, 8, lanes), f32),
        ],
        [],
        10**5,
    )(
        hidden_in, norm_gain, proj_inner, proj_shared, proj_step.T, bias_row, rate,
    )
    normed = normed.reshape(tokens, width_d)
    rims = passed_along(ends, "seq", 1)
    totals = exchanged_all(total[:, 0, :], "seq")
    cot_all = [cotangent.reshape(tokens, columns)]
    for bit in bits_of("head")[:-1]:
        cot_all = cot_all + [swapped(one, "head", bit) for one in cot_all]
    out_blocks = [
        block_at(after([rims], proj_out), mine_h ^ other, columns, 1) for other in range(count_h)
    ]

    x, slope, shared_act, slope_s, step, decay, decay_t, local, state = grid_call(
        functools.partial(states_kernel, taps=taps, states=states),
        seqs,
        [
            wide, per_seq(rim, width + 2 * states), narrow, slim,
            whole((taps, width)), whole((1, width)), whole((taps, 2 * states)),
            whole((1, 2 * states)), whole((1, lanes)), whole((1, lanes)), whole((2 * lanes, width)),
            pl.BlockSpec(memory_space=pl.ANY),
        ],
        [
            wide, wide, narrow, narrow, slim, slim, slim_t, per_seq(chunks, states, width),
            state_spec,
        ],
        [
            shape((seqs, length, width), f32),
            shape((seqs, length, width), bf16),
            shape((seqs, length, 2 * states), bf16),
            shape((seqs, length, 2 * states), f32),
            shape((seqs, length, lanes), f32),
            shape((seqs, length, lanes), f32),
            shape((seqs, 16, length), f32),
            shape((seqs, chunks, states, width), bf16),
            shape((seqs, states, width), bf16),
        ],
        [
            pltpu.VMEM((rim + length, width), f32),
            pltpu.VMEM((rim + length, 2 * states), f32),
            pltpu.VMEM((chunk, width), bf16),
        ],
        10**5,
    )(
        inner_pre, rims, shared_pre, step_raw, filter_inner,
        filter_inner_bias.reshape(1, width), filter_shared,
        filter_shared_bias.reshape(1, 2 * states), bias_row, rate, spread, totals,
    )
    local_out = grid_call(
        functools.partial(mix_kernel, states=states),
        seqs,
        [
            wide, narrow, slim, slim, slim_t, per_seq(chunks, states, width), whole((1, width)),
            whole((2 * lanes, width)),
        ],
        wide,
        shape((seqs, length, width), f32),
        [],
        10**5,
    )(x, shared_act, step, decay, decay_t, local, skip_row, spread)

    out_kept, out_sent = relative_blocks(after([state], proj_out), "head", 1)
    out_kept, out_sent = after([state], out_kept, out_sent)
    ((pieces,),) = landed([local_out, out_kept, out_sent], to_owners(state))
    scanned = chained(pieces, totals, states, spread, False)
    cot_far = after([scanned], swapped(cot_all[0], "head", bits_of("head")[-1]))
    gate_pre = product(nn, after([scanned, cot_far], normed), proj_gate, f32)
    cot_far = [cot_far]
    for bit in bits_of("head")[:-1]:
        cot_far = cot_far + [swapped(one, "head", bit) for one in cot_far]
    (cot_far,) = landed([gate_pre], cot_far)
    cot_all = cot_all + cot_far
    mixer_grad = pieces_product(cot_all, out_blocks, f32)
    ((state_in,),) = landed([mixer_grad], to_blocks(scanned))
    gate_pre = gate_pre.reshape(seqs, length, width)
    mixer_grad = mixer_grad.reshape(seqs, length, width)
    state_in = state_in.reshape(seqs, states, width)

    ssm_out, sums = grid_call(
        functools.partial(gate_kernel, states=states),
        seqs,
        [
            wide, narrow, slim, state_spec, wide, wide, whole((1, width)),
            whole((2 * lanes, width)),
        ],
        [wide, per_seq(8, length)],
        [shape((seqs, length, width), f32), shape((seqs, 8, length), f32)],
        [pltpu.VMEM((length, width), bf16), pltpu.VMEM((length, width), bf16)],
        10**5,
    )(local_out, shared_act, decay, state_in, gate_pre, mixer_grad, gain_row, spread)
    sums_all = lax.all_gather(sums, "head")

    mixer_in, d_gate, d_ssm, lam, gain_grad = grid_call(
        functools.partial(gate_back_kernel, states=states, full=float(full)),
        seqs,
        [
            wide, wide, wide,
            pl.BlockSpec((count_h, None, 8, length), lambda s: (0, s, 0, 0)),
            whole((1, width)), narrow, slim, whole((2 * lanes, width)),
        ],
        [wide, wide, wide, state_spec, per_seq(8, width)],
        [
            shape((seqs, length, width), bf16),
            shape((seqs, length, width), bf16),
            shape((seqs, length, width), f32),
            shape((seqs, states, width), bf16),
            shape((seqs, 8, width), f32),
        ],
        [],
        10**5,
    )(ssm_out, gate_pre, mixer_grad, sums_all, gain_row, shared_act, decay, spread)

    mixer_flat = mixer_in.reshape(tokens, width)
    d_gate_flat = d_gate.reshape(tokens, width)
    bits = bits_of("seq")
    groups = [bits[:1], bits[1:]]
    fine_groups = [bits[:1], bits[1:2], bits[2:]]

    def in_parts(left, right, first, rows, ready):
        half, upper = rows // 2, rank_in("seq", bits[:1])
        far = product(tn, after(ready, left), right, bf16, first + (1 - upper) * half, half)
        near = product(tn, after([far], left), right, bf16, first + upper * half, half)
        return near, far

    near_bit, far_bit = bits_of("head")
    out_parts = in_parts(mixer_flat, cot_all, 0, width, ())
    out_sum = Reduction(None, "seq", fine_groups, halves=out_parts)
    gate_parts = in_parts(normed, d_gate_flat, 0, width_d, out_parts[:1])
    gate_sum = Reduction(None, "seq", fine_groups, halves=gate_parts)

    def mix_back(first, count, d_ssm, into):
        def at(*dims):
            return per_seq(*dims, first=first)

        wide, narrow, slim = at(length, width), at(length, 2 * states), at(length, lanes)
        return grid_call(
            functools.partial(mix_back_kernel, states=states),
            count,
            [
                wide, narrow, slim, slim, at(16, length), at(chunks, states, width),
                at(states, width), wide, whole((2 * lanes, width)), whole((width, lanes)),
            ],
            [wide, narrow, slim],
            [
                shape((seqs, length, width), f32),
                shape((seqs, length, 2 * states), f32),
                shape((seqs, length, lanes), f32),
            ],
            [pltpu.VMEM((lanes, chunk), f32)],
            10**5,
            into,
        )(x, shared_act, step, decay, decay_t, local, state_in, d_ssm, spread, gather)

    ((pieces,),) = landed(gate_parts[:1], to_owners(lam))
    scanned = chained(pieces, totals, states, spread, True)
    sent_out = product(nn, after([scanned], mixer_flat), out_sent, bf16)
    kept_out = product(nn, after([sent_out], mixer_flat), out_kept, bf16)
    (got,) = landed([kept_out], out_sum.start())
    ready = out_sum.take(got) + gate_sum.sent
    d_x, d_shared, d_decay = mix_back(0, seqs, after(ready, d_ssm), ())
    got, got_gate = landed([d_decay], out_sum.start(), gate_sum.start())
    ready = out_sum.take(got) + gate_sum.take(got_gate)
    (later,), got, got_gate = landed(
        ready, to_blocks(scanned), out_sum.start(), gate_sum.start()
    )
    later = later.reshape(seqs, states, width)
    ready = out_sum.take(got) + gate_sum.take(got_gate)
    sent_out = after(ready, sent_out)

    def finish(first, count, later, into):
        def at(*dims):
            return per_seq(*dims, first=first)

        wide, narrow, slim = at(length, width), at(length, 2 * states), at(length, lanes)
        state_spec = at(states, width)
        return grid_call(
            functools.partial(finish_kernel, taps=taps, states=states),
            count,
            [
                wide, wide, narrow, slim, slim, slim, wide, slim, wide, state_spec, state_spec,
                wide, at(rim, width), whole((taps, width)), whole((1, lanes)), whole((1, lanes)),
                whole((1, width)), whole((2 * lanes, width)), whole((width, lanes)),
            ],
            [
                wide, at(rim, width), at(rim, width), at(8, width), slim,
                at(8, lanes),
            ],
            [
                shape((seqs, length, width), bf16),
                shape((seqs, rim, width), bf16),
                shape((seqs, rim, width), f32),
                shape((seqs, 8, width), f32),
                shape((seqs, length, lanes), bf16),
                shape((seqs, 8, lanes), f32),
            ],
            [
                pltpu.VMEM((2 * rim + length, width), f32),
                pltpu.VMEM((rim + length, width), f32),
            ],
            10**5,
            into,
        )(
            x, slope, shared_act, step_raw, step, decay, d_x, d_decay, d_ssm, state_in,
            later, inner_pre, rims, filter_inner, bias_row, rate, skip_row, spread, gather,
        )


    d_act = grid_call(
        functools.partial(act_kernel, states=states),
        seqs,
        [wide, slim, slim, narrow, state_spec, whole((2 * lanes, width))],
        narrow,
        shape((seqs, length, 2 * states), f32),
        [],
        10**5,
    )(x, step, decay, d_shared, after(ready, later), spread)
    body, edge, tail, taps_grad, d_raw, heads_grad = finish(
        0, seqs, after([d_act], later), ()
    )

    got, got_gate, (got_mixed,), (d_act_all,) = landed(
        [body], out_sum.start(), gate_sum.start(), [swapped(sent_out, "head", near_bit)],
        shares_sent(d_act.reshape(seqs * length, 2 * states), "head"),
    )
    def own_seqs(*dims):
        return pl.BlockSpec((None,) + dims, lambda s, at: (at[0] + s,) + (0,) * len(dims))

    def given(*dims):
        return pl.BlockSpec((None,) + dims, lambda s, at: (s,) + (0,) * len(dims))

    params, cost = cheap(10**5)
    s_body, s_edge, s_tail, s_taps_grad = pl.pallas_call(
        functools.partial(shared_kernel, taps=taps),
        grid_spec=pltpu.PrefetchScalarGridSpec(
            num_scalar_prefetch=1,
            grid=(per_device_seqs,),
            in_specs=[
                pl.BlockSpec((count_h, length, 2 * states), lambda s, at: (0, s, 0)),
                own_seqs(length, 2 * states),
                own_seqs(length, 2 * states), own_seqs(rim, width + 2 * states),
                pl.BlockSpec((taps, 2 * states), lambda s, at: (0, 0)),
            ],
            out_specs=[
                given(length, 2 * states), given(rim, 2 * states), given(rim, 2 * states),
                given(8, 2 * states),
            ],
            scratch_shapes=[
                pltpu.VMEM((2 * rim + length, 2 * states), f32),
                pltpu.VMEM((rim + length, 2 * states), f32),
            ],
        ),
        out_shape=[
            shape((per_device_seqs, length, 2 * states), bf16),
            shape((per_device_seqs, rim, 2 * states), bf16),
            shape((per_device_seqs, rim, 2 * states), f32),
            shape((per_device_seqs, 8, 2 * states), f32),
        ],
        compiler_params=params,
        cost_estimate=cost,
    )(
        (mine_h * per_device_seqs).reshape(1), d_act_all, slope_s, shared_pre,
        rims, filter_shared,
    )
    step_grad = product(tn, after([s_body], d_raw.reshape(tokens, lanes)), normed, f32)
    (edge,), (s_edge,) = landed(
        [step_grad], [passed_along(edge, "seq", -1)], [passed_along(s_edge, "seq", -1)]
    )

    def joined(body, edge, tail):
        ends = (tail + edge.astype(f32)).astype(bf16)
        return lax.dynamic_update_slice_in_dim(body, ends, length - rim, 1)

    got, got_gate, (got_mixed,), _ = landed([edge, s_edge], got, got_gate, [got_mixed], [edge])
    mixed, sent_out = halves_added(kept_out, got_mixed, 1)
    sent_out = sent_out.astype(bf16)
    sums_ready = out_sum.take(got) + gate_sum.take(got_gate)
    d_inner = joined(body, edge, tail)
    d_inner_flat = d_inner.reshape(tokens, width)
    d_shared_own = joined(s_body, s_edge, s_tail)
    own_tokens = per_device_seqs * length
    d_shared_flat = d_shared_own.reshape(own_tokens, 2 * states)
    inner_parts = in_parts(normed, d_inner_flat, 0, width_d, [d_inner] + sums_ready)
    inner_sum = Reduction(None, "seq", fine_groups, halves=inner_parts)
    blocks = [mine_h ^ other for other in reversed_order("head")]
    step_rows = jnp.pad(after([d_inner], proj_step).T, ((0, 16 - heads), (0, 0)))
    back = back_product(
        blocks, mine_h, d_gate, after([inner_parts[0], step_rows], d_inner), d_raw,
        d_shared_own, proj_gate, proj_inner, step_rows, proj_shared,
    )
    ready = list(back[:1])
    got, got_out, got_gate = landed(
        ready, inner_sum.start(), out_sum.start(), gate_sum.start()
    )
    ready = inner_sum.take(got)
    back = list(after(ready, *back))
    sent_out = after(ready, sent_out)
    got_out, got_gate = landed(ready, got_out, got_gate)
    padded = columns + 128
    shared_grad = shared_product(
        mine_h, after(ready, normed), d_shared_flat, jnp.sum(s_taps_grad, axis=0),
        count_h, padded,
    )
    sums_ready = out_sum.take(got_out) + gate_sum.take(got_gate)
    (got,) = landed([shared_grad] + sums_ready, inner_sum.start())
    ready = inner_sum.take(got)
    (got_back,), (shared_all,) = landed(
        ready, [swapped(back[0], "head", near_bit)], shares_sent(shared_grad, "head")
    )
    d_normed, back_sent = halves_added(back[1], got_back, 1)
    back_sent = back_sent.astype(bf16)
    (got,) = landed([back_sent], inner_sum.start())
    ready = inner_sum.take(got)

    count = lax.axis_size("seq")
    rows_wide = 8 * width // (2 * states)
    shared_rows = pl.pallas_call(
        rows_kernel,
        out_shape=shape((count, 32 + count_h * padded // count // count_h, 2 * states), bf16),
        scratch_shapes=[pltpu.VMEM((8 * count, width), f32)],
        compiler_params=pltpu.CompilerParams(vmem_limit_bytes=vmem_limit),
        cost_estimate=cheap(10**5)[1],
    )(taps_grad, gain_grad, heads_grad, step_grad, after(ready, shared_all))
    (pieces,) = shares_sent(shared_rows, "seq")
    got, got_gate, got_out, (got_mixed,) = landed(
        [shared_rows], inner_sum.start(), gate_sum.start(), out_sum.start(),
        [swapped(sent_out, "head", far_bit)],
    )
    ready = inner_sum.take(got)
    got_gate, got_out, (got_mixed,) = landed(ready, got_gate, got_out, [got_mixed])
    gate_ready = gate_sum.take(got_gate)
    (out_grad,) = out_sum.take(got_out, [mine_h ^ at for at in range(count_h)], count_h)
    mixed = (mixed + got_mixed.astype(f32)).reshape(seqs, length, columns)
    hidden_own = block_at(after(ready, hidden_in), mine_h, columns, 2).astype(f32)
    got, (got_back,), (pieces,) = landed(
        gate_ready + [out_grad], inner_sum.start(), [swapped(back_sent, "head", far_bit)],
        [pieces],
    )
    total = jnp.sum(pieces.astype(f32), axis=0, keepdims=True).astype(bf16)
    pieces = jnp.broadcast_to(total, pieces.shape)
    (shared_back,) = [lax.all_to_all(pieces, "seq", 0, 0, tiled=True)]
    (got,) = landed([pieces], got)
    ready = inner_sum.take(got)
    (got_back,), (mixed,) = landed(ready, [got_back], [mixed])

    d_normed = (after(ready, d_normed) + got_back.astype(f32)).reshape(seqs, length, columns)
    hidden_own = after(ready, hidden_own)
    scaled = d_normed * block_at(after(ready, norm_gain), mine_h, columns, 0)
    norm_row = jnp.sum(scaled * hidden_own, axis=-1)
    inv_rms = after(ready, inv_rms)[:, :, :1]
    norm_gain_grad = jnp.sum(d_normed * hidden_own * inv_rms, axis=(0, 1))
    norm_row = jnp.sum(lax.all_gather(norm_row, "head"), axis=0)[..., None] / width_d
    for bit in reversed(bits[1:]):
        norm_gain_grad = norm_gain_grad + swapped(norm_gain_grad, "seq", bit)
    d_late = scaled
    activations = (hidden_own + mixed).astype(bf16)
    grad_input = (
        cotangent.astype(f32)
        + inv_rms * d_late
        - hidden_own * inv_rms * inv_rms * inv_rms * norm_row
    )
    small = shared_back[:, :rows_wide].reshape(count, width // (2 * states), 8, 2 * states)
    shared_wide = shared_back[:, 32:].reshape(1, padded, 2 * states)
    shared_wide = jnp.broadcast_to(shared_wide, (count_h, padded, 2 * states))
    (shared_full,) = shares_sent(shared_wide.reshape(-1, 2 * states), "head")
    (got_gate,) = landed([grad_input, shared_wide], gate_sum.start())
    (gate_out,) = gate_sum.take(got_gate)
    (got,) = landed([gate_out], inner_sum.start())
    (inner_out,) = inner_sum.take(got)
    small, shared_full, norm_last = after(
        [inner_out], small, shared_full, swapped(norm_gain_grad, "seq", bits[0])
    )
    norm_gain_grad = norm_gain_grad + norm_last
    small = small.transpose(0, 2, 1, 3).reshape(8 * count, width).astype(f32)
    step_out = jnp.concatenate([small[16:32], small[32:48]], axis=1)[:heads].T
    shared_out = shared_full[:, :columns].astype(f32).reshape(width_d, 2 * states)
    shared_extra = shared_full[0, columns : columns + 8].astype(f32)
    return (
        activations,
        grad_input,
        norm_gain_grad,
        gate_out,
        inner_out,
        step_out,
        shared_out,
        small[:taps],
        small[taps],
        shared_extra[:taps],
        shared_extra[taps],
        small[9, :heads],
        small[10, :heads],
        small[11, :heads],
        small[8],
        out_grad,
    )


def solution(mesh):
    in_specs = (
        P(None, "seq", None),
        P(),
        P(None, "head"),
        P(None, "head"),
        P(None, "head"),
        P(),
        P(None, "head"),
        P("head"),
        P(),
        P(),
        P("head"),
        P("head"),
        P("head"),
        P("head"),
        P("head", None),
        P(None, "seq", "head"),
    )
    out_specs = (
        P(None, "seq", "head"),
        P(None, "seq", "head"),
        P("head"),
        P(None, "head"),
        P(None, "head"),
        P(None, "head"),
        P(),
        P(None, "head"),
        P("head"),
        P(),
        P(),
        P("head"),
        P("head"),
        P("head"),
        P("head"),
        P("head", None),
    )
    return jax.shard_map(
        on_device, mesh=mesh, in_specs=in_specs, out_specs=out_specs, check_vma=False
    )
```

```python
import functools

import jax
import jax.numpy as jnp
import numpy as np
from jax import lax
from jax.experimental import pallas as pl
from jax.experimental.pallas import tpu as pltpu
from jax.sharding import PartitionSpec as P

epsilon = 1e-05
lanes = 128
chunk = 128
rim = 16
f32 = jnp.float32
bf16 = jnp.bfloat16
vmem_limit = 56 * 1024 * 1024


def nn(left, right):
    return jnp.dot(left, right, preferred_element_type=f32)


def nt(left, right):
    return lax.dot_general(left, right, (((1,), (1,)), ((), ())), preferred_element_type=f32)


def tn(left, right):
    return lax.dot_general(left, right, (((0,), (0,)), ((), ())), preferred_element_type=f32)


def rest_of(value):
    return (value - value.astype(bf16).astype(f32)).astype(bf16)


def with_rest(value):
    high = value.astype(bf16).astype(f32)
    return jnp.concatenate([high, value - high], axis=0).astype(bf16)


def two_parts(value):
    high = value.astype(bf16)
    return jnp.concatenate([high, (value - high.astype(f32)).astype(bf16)], axis=1)


def three_parts(value):
    high = value.astype(bf16)
    rest = value - high.astype(f32)
    middle = rest.astype(bf16)
    low = (rest - middle.astype(f32)).astype(bf16)
    return jnp.concatenate([high, middle, low], axis=1)


def summed_by(triangle, value):
    parts = nn(triangle, three_parts(value))
    return parts[:, :lanes] + parts[:, lanes : 2 * lanes] + parts[:, 2 * lanes :]


def iota(shape, dim):
    return lax.broadcasted_iota(jnp.int32, shape, dim)


def triangle_of(kind):
    row, col = iota((chunk, chunk), 0), iota((chunk, chunk), 1)
    keep = {"upto": row >= col, "from": row <= col, "before": row > col}[kind]
    return jnp.where(keep, 1.0, 0.0).astype(bf16)


def sigmoid(value):
    return 0.5 * jnp.tanh(0.5 * value) + 0.5


def softplus(value):
    return jnp.maximum(value, 0.0) + jnp.log1p(jnp.exp(-jnp.abs(value)))


def whole(shape):
    return pl.BlockSpec(shape, lambda s: (0,) * len(shape))


def per_seq(*dims, first=0):
    return pl.BlockSpec((None,) + dims, lambda s: (s + first,) + (0,) * len(dims))


def grid_call(kernel, seqs, in_specs, out_specs, out_shape, scratch, cost, into=()):
    given = len(in_specs)

    def filling(*refs):
        kernel(*refs[:given], *refs[given + len(into) :])

    call = pl.pallas_call(
        filling,
        grid=(seqs,),
        in_specs=in_specs + [pl.BlockSpec(memory_space=pl.ANY)] * len(into),
        input_output_aliases={given + at: at for at in range(len(into))},
        out_specs=out_specs,
        out_shape=out_shape,
        scratch_shapes=scratch,
        compiler_params=pltpu.CompilerParams(
            vmem_limit_bytes=vmem_limit, dimension_semantics=("arbitrary",)
        ),
        cost_estimate=pl.CostEstimate(flops=cost, bytes_accessed=cost, transcendentals=0),
    )
    return lambda *operands: call(*operands, *into)


def cheap(width):
    return pltpu.CompilerParams(vmem_limit_bytes=vmem_limit, dimension_semantics=("arbitrary",)), (
        pl.CostEstimate(flops=width, bytes_accessed=width, transcendentals=0)
    )


def product_kernel(at_ref, left_ref, *refs, dot):
    *right_refs, out_ref = refs
    width = out_ref.shape[1] // len(right_refs)
    for at, right_ref in enumerate(right_refs):
        part = dot(left_ref[...], right_ref[...])
        out_ref[:, at * width : (at + 1) * width] = part.astype(out_ref.dtype)


def product(dot, left, right, dtype, start=0, rows=None):
    depth, total = left.shape if dot is tn else left.shape[::-1]
    rows = total if rows is None else rows
    size = rows // 2 if rows % 256 == 0 else rows
    rights = list(right) if isinstance(right, (list, tuple)) else [right]
    cols = rights[0].shape[0] if dot is nt else rights[0].shape[1]
    cols = cols * len(rights)
    if dot is tn:
        left_spec = pl.BlockSpec((depth, size), lambda i, at: (0, at[0] + i))
    else:
        left_spec = pl.BlockSpec((size, depth), lambda i, at: (at[0] + i, 0))
    params, cost = cheap(10**5)
    return pl.pallas_call(
        functools.partial(product_kernel, dot=dot),
        grid_spec=pltpu.PrefetchScalarGridSpec(
            num_scalar_prefetch=1,
            grid=(rows // size,),
            in_specs=[left_spec]
            + [pl.BlockSpec(one.shape, lambda i, at: (0, 0)) for one in rights],
            out_specs=pl.BlockSpec((size, cols), lambda i, at: (i, 0)),
        ),
        out_shape=jax.ShapeDtypeStruct((rows, cols), dtype),
        compiler_params=params,
        cost_estimate=cost,
    )(jnp.asarray(start // size, jnp.int32).reshape(1), left, *rights)


def rows_kernel(
    taps_grad_ref, gain_grad_ref, heads_grad_ref, step_grad_ref, shared_ref, out_ref, rows_buf
):
    width = rows_buf.shape[1]
    rows_buf[...] = jnp.zeros_like(rows_buf)
    rows_buf[0:8, :] = jnp.sum(taps_grad_ref[...], axis=0)
    rows_buf[8:9, :] = jnp.sum(gain_grad_ref[...], axis=0)[0:1, :]
    rows_buf[9:12, 0:lanes] = jnp.sum(heads_grad_ref[...], axis=0)[0:3, :]
    for at, column in enumerate(spans(step_grad_ref.shape[1], width)):
        rows_buf[16 * (at + 1) : 16 * (at + 2), :] = step_grad_ref[0:16, column]
    shared = jnp.sum(shared_ref[...].astype(f32), axis=0)
    first = shared.shape[0] - 128
    taps_rows = with_rest(shared[first : first + 8, :] + shared[first + 8 : first + 16, :])
    shared = jnp.concatenate(
        [shared[:first, :], taps_rows.astype(f32), shared[first + 16 :, :]], axis=0
    )
    count, _, wide = out_ref.shape
    part = shared.shape[0] // count
    for at in range(count):
        rows = rows_buf[8 * at : 8 * at + 8, :]
        pieces = [rows[:, column] for column in spans(width, wide)]
        pieces = pieces + [jnp.zeros((8, wide), f32)] * (4 - len(pieces))
        out_ref[at, 0:32, :] = jnp.concatenate(pieces, axis=0).astype(bf16)
        out_ref[at, 32:, :] = shared[at * part : (at + 1) * part, :].astype(bf16)


def pieces_kernel(*refs):
    *pairs, out_ref = refs
    count = len(pairs) // 2
    out = nt(pairs[0][...], pairs[count][...])
    for at in range(1, count):
        out = out + nt(pairs[at][...], pairs[count + at][...])
    out_ref[...] = out.astype(out_ref.dtype)


def pieces_product(lefts, rights, dtype):
    tokens, cols = lefts[0].shape[0], rights[0].shape[0]
    size = tokens // 4
    params, cost = cheap(10**5)
    return pl.pallas_call(
        pieces_kernel,
        grid=(tokens // size,),
        in_specs=[pl.BlockSpec((size, left.shape[1]), lambda i: (i, 0)) for left in lefts]
        + [pl.BlockSpec(right.shape, lambda i: (0, 0)) for right in rights],
        out_specs=pl.BlockSpec((size, cols), lambda i: (i, 0)),
        out_shape=jax.ShapeDtypeStruct((tokens, cols), dtype),
        compiler_params=params,
        cost_estimate=cost,
    )(*lefts, *rights)


def shared_grad_kernel(own_ref, normed_ref, d_shared_ref, taps_grad_ref, out_ref):
    rows, (padded, wide) = normed_ref.shape[1], out_ref.shape
    out_ref[0:rows, :] = tn(normed_ref[...], d_shared_ref[...]).astype(bf16)
    out_ref[rows:, :] = jnp.zeros((padded - rows, wide), bf16)

    @pl.when(pl.program_id(0) == 0)
    def _():
        out_ref[rows : rows + 16, :] = with_rest(taps_grad_ref[...])


def shared_product(own, normed, d_shared, taps_grad, count, padded):
    tokens, wide = d_shared.shape
    rows = normed.shape[1] // count
    params, cost = cheap(10**5)
    return pl.pallas_call(
        shared_grad_kernel,
        grid_spec=pltpu.PrefetchScalarGridSpec(
            num_scalar_prefetch=1,
            grid=(count,),
            in_specs=[
                pl.BlockSpec((tokens, rows), lambda i, own: (own[0], i)),
                pl.BlockSpec((tokens, wide), lambda i, own: (0, 0)),
                pl.BlockSpec((8, wide), lambda i, own: (0, 0)),
            ],
            out_specs=pl.BlockSpec((padded, wide), lambda i, own: (i, 0)),
        ),
        out_shape=jax.ShapeDtypeStruct((count * padded, wide), bf16),
        compiler_params=params,
        cost_estimate=cost,
    )(own.reshape(1), normed, d_shared, taps_grad)


def back_kernel(
    places_ref, gate_ref, inner_ref, raw_ref, shared_ref, gate_w_ref, inner_w_ref, step_w_ref,
    shared_w_ref, far_ref, near_ref, out_buf,
    *, per_device, count,
):
    out = nt(gate_ref[...], gate_w_ref[...]) + nt(inner_ref[...], inner_w_ref[...])
    out_buf[...] = out + nn(raw_ref[:, : step_w_ref.shape[0]], step_w_ref[...])

    @pl.when(pl.program_id(0) // per_device == places_ref[count])
    def _():
        out_buf[...] = out_buf[...] + nt(shared_ref[...], shared_w_ref[...])

    size = out_buf.shape[1] // count
    for ref, first in ((near_ref, 0), (far_ref, count // 2)):
        for at in range(count // 2):
            start = pl.multiple_of(places_ref[first + at] * size, lanes)
            ref[:, at * size : (at + 1) * size] = out_buf[:, pl.ds(start, size)].astype(bf16)


def back_product(blocks, mine, gate, inner, raw, shared, gate_w, inner_w, step_w, shared_w):
    seqs, length, _ = gate.shape
    cols, per_device = gate_w.shape[0], shared.shape[0]

    def at_seq(array):
        return pl.BlockSpec((None, length, array.shape[2]), lambda s, at: (s, 0, 0))

    def at_all(array):
        return pl.BlockSpec(array.shape, lambda s, at: (0, 0))

    own = pl.BlockSpec(
        (None, length, shared.shape[2]), lambda s, at: (lax.rem(s, per_device), 0, 0)
    )
    half = pl.BlockSpec((length, cols // 2), lambda s, at: (s, 0))
    params, cost = cheap(10**5)
    return pl.pallas_call(
        functools.partial(back_kernel, per_device=per_device, count=len(blocks)),
        grid_spec=pltpu.PrefetchScalarGridSpec(
            num_scalar_prefetch=1,
            grid=(seqs,),
            in_specs=[at_seq(gate), at_seq(inner), at_seq(raw), own]
            + [at_all(weight) for weight in (gate_w, inner_w, step_w, shared_w)],
            out_specs=[half, half],
            scratch_shapes=[pltpu.VMEM((length, cols), f32)],
        ),
        out_shape=[jax.ShapeDtypeStruct((seqs * length, cols // 2), bf16)] * 2,
        compiler_params=params,
        cost_estimate=cost,
    )(
        jnp.stack(blocks + [mine]), gate, inner, raw, shared, gate_w, inner_w, step_w, shared_w
    )


def assemble_kernel(place_ref, *refs):
    pieces, out_ref = refs[:-1], refs[-1]
    for at, piece in enumerate(pieces):

        @pl.when(pl.program_id(0) == at)
        def _(piece=piece):
            out_ref[...] = piece[...].astype(out_ref.dtype)


def assembled(pieces, rank, dtype, column_from=None, columns=1):
    count, (size, width) = len(pieces), pieces[0].shape
    block = width // columns
    if column_from is None:
        column_from = [jnp.int32(at) for at in range(columns)]
    place = jnp.stack([jnp.asarray(rank, jnp.int32)] + [at.astype(jnp.int32) for at in column_from])
    params, cost = cheap(10**5)
    params = pltpu.CompilerParams(
        vmem_limit_bytes=vmem_limit, dimension_semantics=("arbitrary", "arbitrary")
    )
    return pl.pallas_call(
        assemble_kernel,
        grid_spec=pltpu.PrefetchScalarGridSpec(
            num_scalar_prefetch=1,
            grid=(count, columns),
            in_specs=[
                pl.BlockSpec(
                    (size, block),
                    lambda i, j, at, own=own: (0, jnp.where(i == own, at[1 + j], 0)),
                )
                for own in range(count)
            ],
            out_specs=pl.BlockSpec((size, block), lambda i, j, at: (at[0] ^ i, j)),
        ),
        out_shape=jax.ShapeDtypeStruct((count * size, width), dtype),
        compiler_params=params,
        cost_estimate=cost,
    )(place, *pieces)


def spans(total, width):
    return [slice(at, at + width) for at in range(0, total, width)]


def project_kernel(
    hidden_ref, gain_ref, inner_w_ref, shared_w_ref, step_w_ref, step_bias_ref, rate_ref,
    normed_ref, inner_ref, shared_ref, raw_ref, inv_ref, ends_ref, total_ref,
):
    length = hidden_ref.shape[0]
    heads = step_w_ref.shape[0]
    for rows in spans(length, chunk):
        hidden = hidden_ref[rows, :].astype(f32)
        inv = lax.rsqrt(jnp.mean(hidden * hidden, axis=1, keepdims=True) + epsilon)
        normed_ref[rows, :] = (hidden * inv * gain_ref[...][None, :]).astype(bf16)
        inv_ref[rows, :] = jnp.broadcast_to(inv, (chunk, lanes))
    normed = normed_ref[...]
    inner_ref[...] = nn(normed, inner_w_ref[...])
    shared_ref[...] = nn(normed, shared_w_ref[...])
    raw_ref[...] = jnp.zeros((length, lanes), f32)
    raw_ref[:, :heads] = nt(normed, step_w_ref[...])
    decays = softplus(raw_ref[...] + step_bias_ref[...]) * rate_ref[...]
    total_ref[...] = jnp.broadcast_to(jnp.sum(decays, axis=0, keepdims=True), (8, lanes))
    split = inner_ref.shape[1]
    ends_ref[:, :split] = inner_ref[length - rim :, :]
    ends_ref[:, split:] = shared_ref[length - rim :, :]


def filter_forward(buffer, taps_ref, bias_ref, start, column, taps):
    summed = bias_ref[0:1, column]
    for tap in range(taps):
        summed = summed + taps_ref[tap : tap + 1, column] * buffer[
            pl.ds(rim + start - taps + 1 + tap, chunk), column
        ]
    s = sigmoid(summed)
    return summed * s, s * (1.0 + summed * (1.0 - s))


def states_kernel(
    inner_ref, rims_ref, shared_ref, raw_ref,
    taps_ref, bias_ref, taps_s_ref, bias_s_ref, step_bias_ref, rate_ref, spread_ref, _,
    x_ref, slope_ref, shared_act_ref, slope_s_ref, step_ref, decay_ref, decay_t_ref, local_ref,
    state_ref,
    inner_buf, shared_buf, act_buf,
    *, taps, states,
):
    length, width = inner_ref.shape
    inner_buf[0:rim, :] = rims_ref[:, :width]
    inner_buf[rim:, :] = inner_ref[...]
    shared_buf[0:rim, :] = rims_ref[:, width:]
    shared_buf[rim:, :] = shared_ref[...]
    upto = triangle_of("upto")
    spread = spread_ref[...]
    base = jnp.zeros((1, lanes), f32)
    state = jnp.zeros((states, width), f32)
    for index, rows in enumerate(spans(length, chunk)):
        for column in spans(width, lanes):
            value, slope = filter_forward(
                inner_buf, taps_ref, bias_ref, rows.start, column, taps
            )
            x_ref[rows, column] = value
            slope_ref[rows, column] = slope.astype(bf16)
        for column in spans(2 * states, lanes):
            value, slope = filter_forward(
                shared_buf, taps_s_ref, bias_s_ref, rows.start, column, taps
            )
            shared_act_ref[rows, column] = value.astype(bf16)
            slope_s_ref[rows, column] = slope
        step = softplus(raw_ref[rows, :] + step_bias_ref[...])
        local = summed_by(upto, step * rate_ref[...])
        last = local[chunk - 1 : chunk, :]
        step_ref[rows, :] = step
        decay = local + base
        decay_ref[rows, :] = decay
        decay_t_ref[:, rows] = jnp.transpose(decay)[:16, :]
        weight = nn(two_parts(jnp.exp(last - local) * step), spread)
        act_buf[...] = (weight * x_ref[rows, :]).astype(bf16)
        local_ref[index, :, :] = state.astype(bf16)
        kept = nn(two_parts(jnp.broadcast_to(jnp.exp(last), (8, lanes))), spread)[0:1, :]
        state = kept * state + tn(shared_act_ref[rows, 0:states], act_buf[...])
        base = base + last
    state_ref[...] = state.astype(bf16)


def pair_masks():
    low = iota((chunk, lanes), 1) < lanes // 2
    return low, jnp.logical_not(low)


def halves(value, masks):
    zero = jnp.zeros_like(value)
    return jnp.concatenate(
        [jnp.where(masks[0], value, zero), jnp.where(masks[1], value, zero)], axis=0
    )


def fade(decay, decay_t, head, causal):
    gap = decay[:, head : head + 1] - decay_t[head : head + 1, :]
    return jnp.exp(jnp.where(causal, gap, -1e30))


def mix_kernel(
    x_ref, shared_act_ref, step_ref, decay_ref, decay_t_ref, local_ref, skip_ref, spread_ref,
    out_ref,
    *, states,
):
    length, width = x_ref.shape
    causal = iota((chunk, chunk), 0) >= iota((chunk, chunk), 1)
    masks = pair_masks()
    spread = spread_ref[...]
    base = jnp.zeros((1, lanes), f32)
    for index, rows in enumerate(spans(length, chunk)):
        b, c = shared_act_ref[rows, 0:states], shared_act_ref[rows, states:]
        scores = nt(c, b)
        x = x_ref[rows, :]
        decay = decay_ref[rows, :]
        decay_t = decay_t_ref[:, rows]
        stepped = (x * nn(two_parts(step_ref[rows, :]), spread)).astype(bf16)
        out = skip_ref[...] * x
        if index > 0:
            out = out + nn(two_parts(jnp.exp(decay - base)), spread) * nn(c, local_ref[index])
        base = decay[chunk - 1 : chunk, :]
        for pair, column in enumerate(spans(width, lanes)):
            mixing = jnp.concatenate(
                [
                    (fade(decay, decay_t, 2 * pair + side, causal) * scores).astype(bf16)
                    for side in range(2)
                ],
                axis=1,
            )
            part = nn(mixing, halves(stepped[:, column], masks))
            out_ref[rows, column] = out[:, column] + part


def gate_kernel(
    local_out_ref, shared_act_ref, decay_ref, state_in_ref, gate_ref, mixer_grad_ref, gain_ref,
    spread_ref,
    out_ref, sums_ref,
    square_buf, product_buf,
    *, states,
):
    length, width = local_out_ref.shape
    spread = spread_ref[...]
    for rows in spans(length, chunk):
        faded = nn(two_parts(jnp.exp(decay_ref[rows, :])), spread)
        out = local_out_ref[rows, :] + faded * nn(
            shared_act_ref[rows, states:], state_in_ref[...]
        )
        out_ref[rows, :] = out
        gate = gate_ref[rows, :]
        gated = out * gate * sigmoid(gate)
        square_buf[rows, :] = (gated * gated).astype(bf16)
        product_buf[rows, :] = (
            gated * mixer_grad_ref[rows, :] * gain_ref[...]
        ).astype(bf16)
    ones = jnp.ones((8, width), bf16)
    first = nt(ones, square_buf[...])
    second = nt(ones, product_buf[...])
    sums_ref[...] = jnp.where(iota((8, length), 0) < 4, first, second)


def gate_back_kernel(
    out_ref, gate_ref, mixer_grad_ref, sums_ref, gain_ref, shared_act_ref, decay_ref, spread_ref,
    mixer_in_ref, d_gate_ref, d_ssm_ref, lam_ref, gain_grad_ref,
    *, states, full,
):
    length, width = out_ref.shape
    spread = spread_ref[...]
    gain = gain_ref[...]
    summed = jnp.sum(sums_ref[...], axis=0)
    square = summed[0:1, :] * (1.0 / full)
    product = summed[4:5, :] * (1.0 / full)
    rms = lax.rsqrt(square + epsilon)
    scalars = jnp.concatenate([rms, rms * rms * rms * product, jnp.zeros((6, length), f32)], axis=0)
    gain_grad = jnp.zeros((1, width), f32)
    lam = jnp.zeros((states, width), f32)
    for rows in spans(length, chunk):
        columns = jnp.transpose(scalars[:, rows])
        rms_c, row_c = columns[:, 0:1], columns[:, 1:2]
        out = out_ref[rows, :]
        gate = gate_ref[rows, :]
        mixer_grad = mixer_grad_ref[rows, :]
        s = sigmoid(gate)
        act = gate * s
        gated = out * act
        normal = gated * rms_c
        mixer_in_ref[rows, :] = (normal * gain).astype(bf16)
        gain_grad = gain_grad + jnp.sum(mixer_grad * normal, axis=0, keepdims=True)
        d_gated = rms_c * (mixer_grad * gain) - gated * row_c
        d_ssm = d_gated * act
        d_ssm_ref[rows, :] = d_ssm
        d_gate_ref[rows, :] = (d_gated * out * s * (1.0 + gate * (1.0 - s))).astype(bf16)
        faded = nn(two_parts(jnp.exp(decay_ref[rows, :])), spread)
        lam = lam + tn(shared_act_ref[rows, states:], (faded * d_ssm).astype(bf16))
    lam_ref[...] = lam.astype(bf16)
    gain_grad_ref[...] = jnp.broadcast_to(gain_grad, (8, width))


def mix_back_kernel(
    x_ref, shared_act_ref, step_ref, decay_ref, decay_t_ref, local_ref, state_in_ref, d_ssm_ref,
    spread_ref, gather_ref,
    d_x_ref, d_shared_ref, d_decay_ref,
    column_buf,
    *, states,
):
    length, width = x_ref.shape
    causal = iota((chunk, chunk), 0) >= iota((chunk, chunk), 1)
    masks = pair_masks()
    spread, gather = spread_ref[...], gather_ref[...]
    since, before = triangle_of("from"), triangle_of("before")
    lam = jnp.zeros((states, width), f32)
    heads_here = 2 * (width // lanes)
    column_buf[...] = jnp.zeros_like(column_buf)
    row_at, col_at = iota((2 * chunk, lanes), 0), iota((2 * chunk, lanes), 1)
    all_rows = spans(length, chunk)
    for index in reversed(range(len(all_rows))):
        rows = all_rows[index]
        b, c = shared_act_ref[rows, 0:states], shared_act_ref[rows, states:]
        xf = x_ref[rows, :]
        d_out = d_ssm_ref[rows, :]
        decay = decay_ref[rows, :]
        decay_t = decay_t_ref[:, rows]
        step = step_ref[rows, :]
        if index > 0:
            base = decay_ref[rows.start - 1 : rows.start, :]
        else:
            base = jnp.zeros((1, lanes), f32)
        last = decay[chunk - 1 : chunk, :]
        heads = jnp.concatenate([jnp.exp(base), jnp.exp(last - base), jnp.zeros((6, lanes), f32)])
        heads = nn(two_parts(heads), spread)
        entered = local_ref[index].astype(f32) + heads[0:1, :] * state_in_ref[...].astype(f32)
        entered16 = entered.astype(bf16)
        lam16 = lam.astype(bf16)
        scores = nt(c, b)
        faded = nn(two_parts(jnp.exp(decay - base)), spread)
        fading = nn(two_parts(jnp.exp(last - decay)), spread)
        steps = nn(two_parts(step), spread)
        stepped = (xf * steps).astype(bf16)
        d_faded = (faded * d_out).astype(bf16)
        x_faded = (fading * steps * xf).astype(bf16)
        d_c = nt(d_faded, entered16) + nt(d_faded, rest_of(entered))
        d_b = nt(x_faded, lam16) + nt(x_faded, rest_of(lam))
        carried = nn(c, entered16)
        carrying = nn(b, lam16)
        queries = nn((d_faded.astype(f32) * carried).astype(bf16), gather)
        keys = nn((x_faded.astype(f32) * carrying).astype(bf16), gather)
        across = jnp.sum(lam * entered, axis=0, keepdims=True) * heads[1:2, :]
        across = nn(jnp.broadcast_to(across, (8, width)).astype(bf16), gather)[0:1, :]
        d_x = fading * carrying
        d_scores = jnp.zeros((chunk, chunk), f32)
        for pair, column in enumerate(spans(width, lanes)):
            d_stack = halves(d_out[:, column].astype(bf16), masks)
            d_mixing = nt(d_stack, stepped[:, column])
            mixed, grads = [], []
            for side in range(2):
                head = 2 * pair + side
                faint = fade(decay, decay_t, head, causal)
                d_score = faint * d_mixing[side * chunk : (side + 1) * chunk, :]
                d_scores = d_scores + d_score
                mixed.append((faint * scores).astype(bf16))
                grad = (d_score * scores).astype(bf16)
                grads.append(grad)
                column_buf[head : head + 1, :] = jnp.sum(
                    grad.astype(f32), axis=0, keepdims=True
                )
            code = jnp.where(col_at == 2 * pair + row_at // chunk, 1.0, 0.0).astype(bf16)
            queries = queries + nn(jnp.concatenate(grads, axis=1), code)
            part = tn(jnp.concatenate(mixed, axis=0), d_stack)
            d_x_ref[rows, column] = d_x[:, column] + part
        queries = queries - jnp.transpose(column_buf[...])
        d_decay_ref[rows, :] = summed_by(since, queries) + summed_by(before, keys) + across
        d_scores16, d_rest = d_scores.astype(bf16), rest_of(d_scores)
        d_shared_ref[rows, 0:states] = d_b + tn(d_scores16, c) + tn(d_rest, c)
        d_shared_ref[rows, states:] = d_c + nn(d_scores16, b) + nn(d_rest, b)
        lam = heads[1:2, :] * lam + tn(c, d_faded)


def filter_backward(buffer, taps_ref, start, size, column, taps):
    total = None
    for tap in range(taps):
        term = taps_ref[tap : tap + 1, column] * buffer[
            pl.ds(rim + start + taps - 1 - tap, size), column
        ]
        total = term if total is None else total + term
    return total


def filter_adjoint(buffer, inner_buf, taps_ref, length, width, taps, body_ref, edge_ref, tail_ref,
                   taps_grad_ref):
    for column in spans(width, lanes):
        edge_ref[:, column] = filter_backward(buffer, taps_ref, -rim, rim, column, taps).astype(
            bf16
        )
        rows_grad = [jnp.zeros((8, lanes), f32) for _ in range(taps + 1)]
        for rows in spans(length, chunk):
            body = filter_backward(buffer, taps_ref, rows.start, chunk, column, taps)
            body_ref[rows, column] = body.astype(bf16)
            if rows.stop == length:
                tail_ref[:, column] = body[chunk - rim :, :]
            grad = buffer[pl.ds(rim + rows.start, chunk), column]
            for tap in range(taps):
                moved = inner_buf[pl.ds(rim + rows.start - taps + 1 + tap, chunk), column]
                rows_grad[tap] = rows_grad[tap] + jnp.sum(
                    (grad * moved).reshape(chunk // 8, 8, lanes), axis=0
                )
            rows_grad[taps] = rows_grad[taps] + jnp.sum(
                grad.reshape(chunk // 8, 8, lanes), axis=0
            )
        sums = [jnp.sum(part, axis=0, keepdims=True) for part in rows_grad]
        sums.append(jnp.zeros((8 - taps - 1, lanes), f32))
        taps_grad_ref[:, column] = jnp.concatenate(sums, axis=0)


def act_kernel(
    x_ref, step_ref, decay_ref, d_shared_ref, later_ref, spread_ref, out_ref, *, states
):
    length = x_ref.shape[0]
    last = decay_ref[length - 1 : length, :]
    weight = nn(two_parts(jnp.exp(last - decay_ref[...]) * step_ref[...]), spread_ref[...])
    weighted, later = x_ref[...] * weight, later_ref[...]
    d_b = nt(weighted.astype(bf16), later) + nt(rest_of(weighted), later)
    out_ref[:, 0:states] = d_shared_ref[:, 0:states] + d_b
    out_ref[:, states:] = d_shared_ref[:, states:]


def finish_kernel(
    x_ref, slope_ref, shared_act_ref, raw_ref, step_ref, decay_ref, d_x_ref,
    d_decay_ref, d_ssm_ref, state_in_ref, later_ref, inner_ref, rims_ref,
    taps_ref, step_bias_ref, rate_ref, skip_ref, spread_ref, gather_ref,
    body_ref, edge_ref, tail_ref, taps_grad_ref, d_raw_ref, heads_ref,
    grad_buf, inner_buf,
    *, taps, states,
):
    length, width = x_ref.shape
    spread, gather = spread_ref[...], gather_ref[...]
    before = triangle_of("before")
    later = later_ref[...]
    grad_buf[0:rim, :] = jnp.zeros((rim, width), f32)
    grad_buf[rim + length :, :] = jnp.zeros((rim, width), f32)
    inner_buf[0:rim, :] = rims_ref[:, :width]
    inner_buf[rim:, :] = inner_ref[...]
    last = decay_ref[length - 1 : length, :]
    final = nn(two_parts(jnp.broadcast_to(jnp.exp(last), (8, lanes))), spread)[0:1, :]
    across = final * jnp.sum(
        later.astype(f32) * state_in_ref[...].astype(f32), axis=0, keepdims=True
    )
    running = nn(jnp.broadcast_to(across, (8, width)).astype(bf16), gather)[0:1, :]
    skip = skip_ref[...]
    skip_grad = jnp.zeros((1, width), f32)
    rate_grad = jnp.zeros((1, lanes), f32)
    bias_grad = jnp.zeros((1, lanes), f32)
    for rows in spans(length, chunk):
        b = shared_act_ref[rows, 0:states]
        x = x_ref[rows, :]
        step = step_ref[rows, :]
        d_ssm = d_ssm_ref[rows, :]
        fading = nn(two_parts(jnp.exp(last - decay_ref[rows, :])), spread)
        steps = nn(two_parts(step), spread)
        carrying = fading * nn(b, later)
        x_stepped = x * steps
        keys = nn((x_stepped * carrying).astype(bf16), gather)
        d_x = d_x_ref[rows, :] + carrying
        direct = nn((x * d_x).astype(bf16), gather)
        d_decay = d_decay_ref[rows, :] + running + summed_by(before, keys)
        running = running + jnp.sum(keys, axis=0, keepdims=True)
        skip_grad = skip_grad + jnp.sum(d_ssm * x, axis=0, keepdims=True)
        rate_grad = rate_grad + jnp.sum(step * d_decay, axis=0, keepdims=True)
        d_raw = (direct + rate_ref[...] * d_decay) * sigmoid(
            raw_ref[rows, :] + step_bias_ref[...]
        )
        d_raw_ref[rows, :] = d_raw.astype(bf16)
        bias_grad = bias_grad + jnp.sum(d_raw, axis=0, keepdims=True)
        grad_buf[pl.ds(rim + rows.start, chunk), :] = (
            skip * d_ssm + steps * d_x
        ) * slope_ref[rows, :].astype(f32)
    parts = two_parts(jnp.broadcast_to(skip_grad, (8, width)))
    skip_heads = nn(parts[:, :width], gather) + nn(parts[:, width:], gather)
    heads_ref[...] = jnp.concatenate(
        [bias_grad, rate_grad * rate_ref[...], skip_heads[0:1, :], jnp.zeros((5, lanes), f32)],
        axis=0,
    )
    filter_adjoint(
        grad_buf, inner_buf, taps_ref, length, width, taps, body_ref, edge_ref, tail_ref,
        taps_grad_ref,
    )


def shared_kernel(
    first_ref, d_act_ref, slope_ref, shared_ref, rim_ref, taps_ref,
    body_ref, edge_ref, tail_ref, taps_grad_ref,
    grad_buf, inner_buf,
    *, taps,
):
    _, length, width = d_act_ref.shape
    grad_buf[0:rim, :] = jnp.zeros((rim, width), f32)
    grad_buf[rim + length :, :] = jnp.zeros((rim, width), f32)
    inner_buf[0:rim, :] = rim_ref[:, rim_ref.shape[1] - width :]
    inner_buf[rim:, :] = shared_ref[...]
    grad_buf[rim : rim + length, :] = jnp.sum(d_act_ref[...], axis=0) * slope_ref[...]
    filter_adjoint(
        grad_buf, inner_buf, taps_ref, length, width, taps, body_ref, edge_ref, tail_ref,
        taps_grad_ref,
    )


def chain_kernel(pieces_ref, totals_ref, spread_ref, out_ref, *, backward):
    count = pieces_ref.shape[0]
    decays = nn(two_parts(jnp.exp(totals_ref[...])), spread_ref[...])
    state = jnp.zeros(pieces_ref.shape[1:], f32)
    order = reversed(range(count)) if backward else range(count)
    for block in order:
        out_ref[block, :, :] = state.astype(bf16)
        state = decays[block : block + 1, :] * state + pieces_ref[block].astype(f32)


def after(ready, *values):
    if not ready:
        return values if len(values) > 1 else values[0]
    tied = lax.optimization_barrier((tuple(ready), tuple(values)))[1]
    return tied if len(values) > 1 else tied[0]


def landed(ready, *transfers):
    flat = [value for transfer in transfers for value in transfer]
    flat = list(lax.optimization_barrier((tuple(ready), tuple(flat)))[1])
    return [[flat.pop(0) for _ in transfer] for transfer in transfers]


def bits_of(axis):
    return [1 << bit for bit in range(lax.axis_size(axis).bit_length() - 1)]


def swapped(value, axis, bit):
    size = lax.axis_size(axis)
    return lax.ppermute(value, axis, [(i, i ^ bit) for i in range(size)])


def passed_along(value, axis, by):
    size = lax.axis_size(axis)
    pairs = [(i, i + by) for i in range(size) if 0 <= i + by < size]
    return lax.ppermute(value, axis, pairs)


def block_at(value, index, size, dim):
    return lax.dynamic_slice_in_dim(value, index * size, size, dim)


def reversed_order(axis):
    order = [0]
    for bit in reversed(bits_of(axis)):
        order = order + [at + bit for at in order]
    return order


def relative_blocks(value, axis, dim):
    count, mine = lax.axis_size(axis), lax.axis_index(axis)
    size = value.shape[dim] // count
    blocks = [block_at(value, mine ^ other, size, dim) for other in reversed_order(axis)]
    half = len(blocks) // 2
    return [
        jnp.concatenate(blocks[:half], axis=dim),
        jnp.concatenate(blocks[half:], axis=dim),
    ]


def gathered_relative(value, axis, dim, ready=()):
    for bit in reversed(bits_of(axis)):
        value = jnp.concatenate([value, after(ready, swapped(value, axis, bit))], axis=dim)
    return value


def halves_added(kept, got, dim):
    half = got.shape[dim] // 2
    parts = [
        lax.slice_in_dim(value, at * half, (at + 1) * half, axis=dim)
        for at in range(2)
        for value in (kept, got)
    ]
    return parts[0].astype(f32) + parts[1].astype(f32), parts[2].astype(f32) + parts[3].astype(f32)


def in_place_order(value, axis, dim):
    count, mine = lax.axis_size(axis), lax.axis_index(axis)
    size = value.shape[dim] // count
    bits = bits_of(axis)

    def place(at):
        return sum(((at // bit) % 2) * back for bit, back in zip(bits, reversed(bits)))

    return jnp.concatenate(
        [block_at(value, place(mine ^ other), size, dim) for other in range(count)], axis=dim
    )


def rank_in(axis, group):
    mine = lax.axis_index(axis)
    return sum(((mine // bit) % 2) << at for at, bit in enumerate(group))


def mask_of(group, distance):
    return sum(bit for at, bit in enumerate(group) if distance >> at & 1)


class Reduction:
    def __init__(self, value, axis, groups, wire=bf16, halves=None):
        self.axis, self.wire, self.value = axis, wire, value
        self.left, self.taken = list(groups), []
        if halves is None:
            self.split()
        else:
            self.kept, self.sent = halves[0], [halves[1]]

    def split(self):
        if self.left:
            count = 1 << len(self.left[0])
            rank = rank_in(self.axis, self.left[0])
            size = self.value.shape[0] // count
            self.kept = block_at(self.value, rank, size, 0)
            self.sent = [
                block_at(self.value, rank ^ other, size, 0).astype(self.wire)
                for other in range(1, count)
            ]
        else:
            self.value = self.value.astype(bf16)
            self.sent = [self.value]

    def start(self):
        group = self.left[0] if self.left else self.taken[-1]
        count = 1 << len(group)
        sent = self.sent if self.left else self.sent * (count - 1)
        return [
            swapped(value, self.axis, mask_of(group, other))
            for other, value in enumerate(sent, 1)
        ]

    def take(self, got, *columns):
        if self.left:
            self.taken.append(self.left.pop(0))
            total = self.kept.astype(f32)
            for value in got:
                total = total + value.astype(f32)
            self.value = total.astype(self.wire)
        else:
            group = self.taken.pop()
            rank = rank_in(self.axis, group)
            if self.taken:
                self.value = assembled([self.value] + got, rank, bf16)
            else:
                self.value = assembled([self.value] + got, rank, f32, *columns)
        if self.left or self.taken:
            self.split()
            return self.sent
        return [self.value]


def exchanged_sum(value, axis):
    for bit in bits_of(axis):
        value = (value.astype(f32) + swapped(value, axis, bit).astype(f32)).astype(value.dtype)
    return value


def exchanged_all(value, axis):
    mine = lax.axis_index(axis)
    value = value[None]
    for bit in bits_of(axis):
        got = swapped(value, axis, bit)
        low = (mine // bit) % 2 == 0
        value = jnp.concatenate([jnp.where(low, value, got), jnp.where(low, got, value)], axis=0)
    return value


def to_owners(state):
    count, width = lax.axis_size("seq"), state.shape[-1]
    return [lax.all_to_all(state.reshape(count, -1, width), "seq", 0, 0, tiled=True)]


def chained(pieces, totals, states, spread, backward):
    count, size, width = pieces.shape
    mine = lax.axis_index("seq")
    here = lax.dynamic_index_in_dim(totals, mine * size // states, 1, keepdims=False)
    params, cost = cheap(10**5)
    return pl.pallas_call(
        functools.partial(chain_kernel, backward=backward),
        out_shape=jax.ShapeDtypeStruct((count, size, width), bf16),
        compiler_params=pltpu.CompilerParams(vmem_limit_bytes=vmem_limit),
        cost_estimate=cost,
    )(pieces, here, spread)


def shares_sent(value, axes):
    count = lax.axis_size(axes)
    return [lax.all_to_all(value.reshape(count, -1, value.shape[-1]), axes, 0, 0, tiled=True)]


def shares_back(pieces, axes):
    total = jnp.sum(pieces.astype(f32), axis=0, keepdims=True).astype(bf16)
    return [lax.all_to_all(jnp.broadcast_to(total, pieces.shape), axes, 0, 0, tiled=True)]


def to_blocks(scanned):
    return [lax.all_to_all(scanned, "seq", 0, 0, tiled=True)]


def on_device(
    hidden_in, norm_gain, proj_gate, proj_inner, proj_step, proj_shared, filter_inner,
    filter_inner_bias, filter_shared, filter_shared_bias, step_bias, log_rate, skip_gain,
    gate_gain, proj_out, cotangent,
):
    seqs, length, width_d = hidden_in.shape
    width = proj_gate.shape[1]
    heads = proj_step.shape[1]
    per_head = width // heads
    states = proj_shared.shape[1] // 2
    taps = filter_inner.shape[0]
    count_h = lax.axis_size("head")
    mine_h = lax.axis_index("head")
    full = width * count_h
    columns = width_d // count_h
    tokens = seqs * length
    per_device_seqs = seqs // count_h

    spread_np = np.zeros((2 * lanes, width), np.float32)
    for head in range(heads):
        spread_np[head, head * per_head : (head + 1) * per_head] = 1
        spread_np[lanes + head, head * per_head : (head + 1) * per_head] = 1
    spread = jnp.asarray(spread_np, bf16)
    gather = jnp.asarray(spread_np[:lanes].T, bf16)

    def on_lanes(vector):
        return jnp.pad(vector.astype(f32), (0, lanes - heads)).reshape(1, lanes)

    rate = on_lanes(-jnp.exp(log_rate))
    bias_row = on_lanes(step_bias)
    skip_row = jnp.repeat(skip_gain, per_head).reshape(1, width)
    gain_row = gate_gain.reshape(1, width)

    shape = jax.ShapeDtypeStruct
    wide = per_seq(length, width)
    narrow = per_seq(length, 2 * states)
    slim = per_seq(length, lanes)
    slim_t = per_seq(16, length)
    state_spec = per_seq(states, width)
    chunks = length // chunk

    normed, inner_pre, shared_pre, step_raw, inv_rms, ends, total = grid_call(
        project_kernel,
        seqs,
        [
            per_seq(length, width_d), whole((width_d,)), whole((width_d, width)),
            whole((width_d, 2 * states)), whole((heads, width_d)), whole((1, lanes)),
            whole((1, lanes)),
        ],
        [
            per_seq(length, width_d), wide, narrow, slim, slim, per_seq(rim, width + 2 * states),
            per_seq(8, lanes),
        ],
        [
            shape((seqs, length, width_d), bf16),
            shape((seqs, length, width), f32),
            shape((seqs, length, 2 * states), f32),
            shape((seqs, length, lanes), f32),
            shape((seqs, length, lanes), f32),
            shape((seqs, rim, width + 2 * states), f32),
            shape((seqs, 8, lanes), f32),
        ],
        [],
        10**5,
    )(
        hidden_in, norm_gain, proj_inner, proj_shared, proj_step.T, bias_row, rate,
    )
    normed = normed.reshape(tokens, width_d)
    rims = passed_along(ends, "seq", 1)
    totals = exchanged_all(total[:, 0, :], "seq")
    cot_all = [cotangent.reshape(tokens, columns)]
    for bit in bits_of("head")[:-1]:
        cot_all = cot_all + [swapped(one, "head", bit) for one in cot_all]
    out_blocks = [
        block_at(after([rims], proj_out), mine_h ^ other, columns, 1) for other in range(count_h)
    ]

    x, slope, shared_act, slope_s, step, decay, decay_t, local, state = grid_call(
        functools.partial(states_kernel, taps=taps, states=states),
        seqs,
        [
            wide, per_seq(rim, width + 2 * states), narrow, slim,
            whole((taps, width)), whole((1, width)), whole((taps, 2 * states)),
            whole((1, 2 * states)), whole((1, lanes)), whole((1, lanes)), whole((2 * lanes, width)),
            pl.BlockSpec(memory_space=pl.ANY),
        ],
        [
            wide, wide, narrow, narrow, slim, slim, slim_t, per_seq(chunks, states, width),
            state_spec,
        ],
        [
            shape((seqs, length, width), f32),
            shape((seqs, length, width), bf16),
            shape((seqs, length, 2 * states), bf16),
            shape((seqs, length, 2 * states), f32),
            shape((seqs, length, lanes), f32),
            shape((seqs, length, lanes), f32),
            shape((seqs, 16, length), f32),
            shape((seqs, chunks, states, width), bf16),
            shape((seqs, states, width), bf16),
        ],
        [
            pltpu.VMEM((rim + length, width), f32),
            pltpu.VMEM((rim + length, 2 * states), f32),
            pltpu.VMEM((chunk, width), bf16),
        ],
        10**5,
    )(
        inner_pre, rims, shared_pre, step_raw, filter_inner,
        filter_inner_bias.reshape(1, width), filter_shared,
        filter_shared_bias.reshape(1, 2 * states), bias_row, rate, spread, totals,
    )
    local_out = grid_call(
        functools.partial(mix_kernel, states=states),
        seqs,
        [
            wide, narrow, slim, slim, slim_t, per_seq(chunks, states, width), whole((1, width)),
            whole((2 * lanes, width)),
        ],
        wide,
        shape((seqs, length, width), f32),
        [],
        10**5,
    )(x, shared_act, step, decay, decay_t, local, skip_row, spread)

    out_kept, out_sent = relative_blocks(after([state], proj_out), "head", 1)
    out_kept, out_sent = after([state], out_kept, out_sent)
    ((pieces,),) = landed([local_out, out_kept, out_sent], to_owners(state))
    scanned = chained(pieces, totals, states, spread, False)
    cot_far = after([scanned], swapped(cot_all[0], "head", bits_of("head")[-1]))
    gate_pre = product(nn, after([scanned, cot_far], normed), proj_gate, f32)
    cot_far = [cot_far]
    for bit in bits_of("head")[:-1]:
        cot_far = cot_far + [swapped(one, "head", bit) for one in cot_far]
    (cot_far,) = landed([gate_pre], cot_far)
    cot_all = cot_all + cot_far
    mixer_grad = pieces_product(cot_all, out_blocks, f32)
    ((state_in,),) = landed([mixer_grad], to_blocks(scanned))
    gate_pre = gate_pre.reshape(seqs, length, width)
    mixer_grad = mixer_grad.reshape(seqs, length, width)
    state_in = state_in.reshape(seqs, states, width)

    ssm_out, sums = grid_call(
        functools.partial(gate_kernel, states=states),
        seqs,
        [
            wide, narrow, slim, state_spec, wide, wide, whole((1, width)),
            whole((2 * lanes, width)),
        ],
        [wide, per_seq(8, length)],
        [shape((seqs, length, width), f32), shape((seqs, 8, length), f32)],
        [pltpu.VMEM((length, width), bf16), pltpu.VMEM((length, width), bf16)],
        10**5,
    )(local_out, shared_act, decay, state_in, gate_pre, mixer_grad, gain_row, spread)
    sums_all = lax.all_gather(sums, "head")

    mixer_in, d_gate, d_ssm, lam, gain_grad = grid_call(
        functools.partial(gate_back_kernel, states=states, full=float(full)),
        seqs,
        [
            wide, wide, wide,
            pl.BlockSpec((count_h, None, 8, length), lambda s: (0, s, 0, 0)),
            whole((1, width)), narrow, slim, whole((2 * lanes, width)),
        ],
        [wide, wide, wide, state_spec, per_seq(8, width)],
        [
            shape((seqs, length, width), bf16),
            shape((seqs, length, width), bf16),
            shape((seqs, length, width), f32),
            shape((seqs, states, width), bf16),
            shape((seqs, 8, width), f32),
        ],
        [],
        10**5,
    )(ssm_out, gate_pre, mixer_grad, sums_all, gain_row, shared_act, decay, spread)

    mixer_flat = mixer_in.reshape(tokens, width)
    d_gate_flat = d_gate.reshape(tokens, width)
    bits = bits_of("seq")
    groups = [bits[:1], bits[1:]]
    fine_groups = [bits[:1], bits[1:2], bits[2:]]

    def in_parts(left, right, first, rows, ready):
        half, upper = rows // 2, rank_in("seq", bits[:1])
        far = product(tn, after(ready, left), right, bf16, first + (1 - upper) * half, half)
        near = product(tn, after([far], left), right, bf16, first + upper * half, half)
        return near, far

    near_bit, far_bit = bits_of("head")
    out_parts = in_parts(mixer_flat, cot_all, 0, width, ())
    out_sum = Reduction(None, "seq", fine_groups, halves=out_parts)
    gate_parts = in_parts(normed, d_gate_flat, 0, width_d, out_parts[:1])
    gate_sum = Reduction(None, "seq", fine_groups, halves=gate_parts)

    def mix_back(first, count, d_ssm, into):
        def at(*dims):
            return per_seq(*dims, first=first)

        wide, narrow, slim = at(length, width), at(length, 2 * states), at(length, lanes)
        return grid_call(
            functools.partial(mix_back_kernel, states=states),
            count,
            [
                wide, narrow, slim, slim, at(16, length), at(chunks, states, width),
                at(states, width), wide, whole((2 * lanes, width)), whole((width, lanes)),
            ],
            [wide, narrow, slim],
            [
                shape((seqs, length, width), f32),
                shape((seqs, length, 2 * states), f32),
                shape((seqs, length, lanes), f32),
            ],
            [pltpu.VMEM((lanes, chunk), f32)],
            10**5,
            into,
        )(x, shared_act, step, decay, decay_t, local, state_in, d_ssm, spread, gather)

    ((pieces,),) = landed(gate_parts[:1], to_owners(lam))
    scanned = chained(pieces, totals, states, spread, True)
    sent_out = product(nn, after([scanned], mixer_flat), out_sent, bf16)
    kept_out = product(nn, after([sent_out], mixer_flat), out_kept, bf16)
    (got,) = landed([kept_out], out_sum.start())
    ready = out_sum.take(got) + gate_sum.sent
    d_x, d_shared, d_decay = mix_back(0, seqs, after(ready, d_ssm), ())
    got, got_gate = landed([d_decay], out_sum.start(), gate_sum.start())
    ready = out_sum.take(got) + gate_sum.take(got_gate)
    (later,), got, got_gate = landed(
        ready, to_blocks(scanned), out_sum.start(), gate_sum.start()
    )
    later = later.reshape(seqs, states, width)
    ready = out_sum.take(got) + gate_sum.take(got_gate)
    sent_out = after(ready, sent_out)

    def finish(first, count, later, into):
        def at(*dims):
            return per_seq(*dims, first=first)

        wide, narrow, slim = at(length, width), at(length, 2 * states), at(length, lanes)
        state_spec = at(states, width)
        return grid_call(
            functools.partial(finish_kernel, taps=taps, states=states),
            count,
            [
                wide, wide, narrow, slim, slim, slim, wide, slim, wide, state_spec, state_spec,
                wide, at(rim, width), whole((taps, width)), whole((1, lanes)), whole((1, lanes)),
                whole((1, width)), whole((2 * lanes, width)), whole((width, lanes)),
            ],
            [
                wide, at(rim, width), at(rim, width), at(8, width), slim,
                at(8, lanes),
            ],
            [
                shape((seqs, length, width), bf16),
                shape((seqs, rim, width), bf16),
                shape((seqs, rim, width), f32),
                shape((seqs, 8, width), f32),
                shape((seqs, length, lanes), bf16),
                shape((seqs, 8, lanes), f32),
            ],
            [
                pltpu.VMEM((2 * rim + length, width), f32),
                pltpu.VMEM((rim + length, width), f32),
            ],
            10**5,
            into,
        )(
            x, slope, shared_act, step_raw, step, decay, d_x, d_decay, d_ssm, state_in,
            later, inner_pre, rims, filter_inner, bias_row, rate, skip_row, spread, gather,
        )


    d_act = grid_call(
        functools.partial(act_kernel, states=states),
        seqs,
        [wide, slim, slim, narrow, state_spec, whole((2 * lanes, width))],
        narrow,
        shape((seqs, length, 2 * states), f32),
        [],
        10**5,
    )(x, step, decay, d_shared, after(ready, later), spread)
    body, edge, tail, taps_grad, d_raw, heads_grad = finish(
        0, seqs, after([d_act], later), ()
    )

    got, got_gate, (got_mixed,), (d_act_all,) = landed(
        [body], out_sum.start(), gate_sum.start(), [swapped(sent_out, "head", near_bit)],
        shares_sent(d_act.reshape(seqs * length, 2 * states), "head"),
    )
    def own_seqs(*dims):
        return pl.BlockSpec((None,) + dims, lambda s, at: (at[0] + s,) + (0,) * len(dims))

    def given(*dims):
        return pl.BlockSpec((None,) + dims, lambda s, at: (s,) + (0,) * len(dims))

    params, cost = cheap(10**5)
    s_body, s_edge, s_tail, s_taps_grad = pl.pallas_call(
        functools.partial(shared_kernel, taps=taps),
        grid_spec=pltpu.PrefetchScalarGridSpec(
            num_scalar_prefetch=1,
            grid=(per_device_seqs,),
            in_specs=[
                pl.BlockSpec((count_h, length, 2 * states), lambda s, at: (0, s, 0)),
                own_seqs(length, 2 * states),
                own_seqs(length, 2 * states), own_seqs(rim, width + 2 * states),
                pl.BlockSpec((taps, 2 * states), lambda s, at: (0, 0)),
            ],
            out_specs=[
                given(length, 2 * states), given(rim, 2 * states), given(rim, 2 * states),
                given(8, 2 * states),
            ],
            scratch_shapes=[
                pltpu.VMEM((2 * rim + length, 2 * states), f32),
                pltpu.VMEM((rim + length, 2 * states), f32),
            ],
        ),
        out_shape=[
            shape((per_device_seqs, length, 2 * states), bf16),
            shape((per_device_seqs, rim, 2 * states), bf16),
            shape((per_device_seqs, rim, 2 * states), f32),
            shape((per_device_seqs, 8, 2 * states), f32),
        ],
        compiler_params=params,
        cost_estimate=cost,
    )(
        (mine_h * per_device_seqs).reshape(1), d_act_all, slope_s, shared_pre,
        rims, filter_shared,
    )
    step_grad = product(tn, after([s_body], d_raw.reshape(tokens, lanes)), normed, f32)
    (edge,), (s_edge,) = landed(
        [step_grad], [passed_along(edge, "seq", -1)], [passed_along(s_edge, "seq", -1)]
    )

    def joined(body, edge, tail):
        ends = (tail + edge.astype(f32)).astype(bf16)
        return lax.dynamic_update_slice_in_dim(body, ends, length - rim, 1)

    got, got_gate, (got_mixed,), _ = landed([edge, s_edge], got, got_gate, [got_mixed], [edge])
    mixed, sent_out = halves_added(kept_out, got_mixed, 1)
    sent_out = sent_out.astype(bf16)
    sums_ready = out_sum.take(got) + gate_sum.take(got_gate)
    d_inner = joined(body, edge, tail)
    d_inner_flat = d_inner.reshape(tokens, width)
    d_shared_own = joined(s_body, s_edge, s_tail)
    own_tokens = per_device_seqs * length
    d_shared_flat = d_shared_own.reshape(own_tokens, 2 * states)
    inner_parts = in_parts(normed, d_inner_flat, 0, width_d, [d_inner] + sums_ready)
    inner_sum = Reduction(None, "seq", fine_groups, halves=inner_parts)
    blocks = [mine_h ^ other for other in reversed_order("head")]
    step_rows = jnp.pad(after([d_inner], proj_step).T, ((0, 16 - heads), (0, 0)))
    back = back_product(
        blocks, mine_h, d_gate, after([inner_parts[0], step_rows], d_inner), d_raw,
        d_shared_own, proj_gate, proj_inner, step_rows, proj_shared,
    )
    ready = list(back[:1])
    got, got_out, got_gate = landed(
        ready, inner_sum.start(), out_sum.start(), gate_sum.start()
    )
    ready = inner_sum.take(got)
    back = list(after(ready, *back))
    sent_out = after(ready, sent_out)
    got_out, got_gate = landed(ready, got_out, got_gate)
    padded = columns + 128
    shared_grad = shared_product(
        mine_h, after(ready, normed), d_shared_flat, jnp.sum(s_taps_grad, axis=0),
        count_h, padded,
    )
    sums_ready = out_sum.take(got_out) + gate_sum.take(got_gate)
    (got,) = landed([shared_grad] + sums_ready, inner_sum.start())
    ready = inner_sum.take(got)
    (got_back,), (shared_all,) = landed(
        ready, [swapped(back[0], "head", near_bit)], shares_sent(shared_grad, "head")
    )
    d_normed, back_sent = halves_added(back[1], got_back, 1)
    back_sent = back_sent.astype(bf16)
    (got,) = landed([back_sent], inner_sum.start())
    ready = inner_sum.take(got)

    count = lax.axis_size("seq")
    rows_wide = 8 * width // (2 * states)
    shared_rows = pl.pallas_call(
        rows_kernel,
        out_shape=shape((count, 32 + count_h * padded // count // count_h, 2 * states), bf16),
        scratch_shapes=[pltpu.VMEM((8 * count, width), f32)],
        compiler_params=pltpu.CompilerParams(vmem_limit_bytes=vmem_limit),
        cost_estimate=cheap(10**5)[1],
    )(taps_grad, gain_grad, heads_grad, step_grad, after(ready, shared_all))
    (pieces,) = shares_sent(shared_rows, "seq")
    got, got_gate, got_out, (got_mixed,) = landed(
        [shared_rows], inner_sum.start(), gate_sum.start(), out_sum.start(),
        [swapped(sent_out, "head", far_bit)],
    )
    ready = inner_sum.take(got)
    got_gate, got_out, (got_mixed,) = landed(ready, got_gate, got_out, [got_mixed])
    gate_ready = gate_sum.take(got_gate)
    (out_grad,) = out_sum.take(got_out, [mine_h ^ at for at in range(count_h)], count_h)
    mixed = (mixed + got_mixed.astype(f32)).reshape(seqs, length, columns)
    hidden_own = block_at(after(ready, hidden_in), mine_h, columns, 2).astype(f32)
    got, (got_back,), (pieces,) = landed(
        gate_ready + [out_grad], inner_sum.start(), [swapped(back_sent, "head", far_bit)],
        [pieces],
    )
    total = jnp.sum(pieces.astype(f32), axis=0, keepdims=True).astype(bf16)
    pieces = jnp.broadcast_to(total, pieces.shape)
    (shared_back,) = [lax.all_to_all(pieces, "seq", 0, 0, tiled=True)]
    (got,) = landed([pieces], got)
    ready = inner_sum.take(got)
    (got_back,), (mixed,) = landed(ready, [got_back], [mixed])

    d_normed = (after(ready, d_normed) + got_back.astype(f32)).reshape(seqs, length, columns)
    hidden_own = after(ready, hidden_own)
    scaled = d_normed * block_at(after(ready, norm_gain), mine_h, columns, 0)
    norm_row = jnp.sum(scaled * hidden_own, axis=-1)
    inv_rms = after(ready, inv_rms)[:, :, :1]
    norm_gain_grad = jnp.sum(d_normed * hidden_own * inv_rms, axis=(0, 1))
    norm_row = jnp.sum(lax.all_gather(norm_row, "head"), axis=0)[..., None] / width_d
    for bit in reversed(bits[1:]):
        norm_gain_grad = norm_gain_grad + swapped(norm_gain_grad, "seq", bit)
    d_late = scaled
    activations = (hidden_own + mixed).astype(bf16)
    grad_input = (
        cotangent.astype(f32)
        + inv_rms * d_late
        - hidden_own * inv_rms * inv_rms * inv_rms * norm_row
    )
    small = shared_back[:, :rows_wide].reshape(count, width // (2 * states), 8, 2 * states)
    shared_wide = shared_back[:, 32:].reshape(1, padded, 2 * states)
    shared_wide = jnp.broadcast_to(shared_wide, (count_h, padded, 2 * states))
    (shared_full,) = shares_sent(shared_wide.reshape(-1, 2 * states), "head")
    (got_gate,) = landed([grad_input, shared_wide], gate_sum.start())
    (gate_out,) = gate_sum.take(got_gate)
    (got,) = landed([gate_out], inner_sum.start())
    (inner_out,) = inner_sum.take(got)
    small, shared_full, norm_last = after(
        [inner_out], small, shared_full, swapped(norm_gain_grad, "seq", bits[0])
    )
    norm_gain_grad = norm_gain_grad + norm_last
    small = small.transpose(0, 2, 1, 3).reshape(8 * count, width).astype(f32)
    step_out = jnp.concatenate([small[16:32], small[32:48]], axis=1)[:heads].T
    shared_out = shared_full[:, :columns].astype(f32).reshape(width_d, 2 * states)
    shared_extra = shared_full[0, columns : columns + 16].astype(f32)
    shared_extra = shared_extra[:8] + shared_extra[8:]
    return (
        activations,
        grad_input,
        norm_gain_grad,
        gate_out,
        inner_out,
        step_out,
        shared_out,
        small[:taps],
        small[taps],
        shared_extra[:taps],
        shared_extra[taps],
        small[9, :heads],
        small[10, :heads],
        small[11, :heads],
        small[8],
        out_grad,
    )


def solution(mesh):
    in_specs = (
        P(None, "seq", None),
        P(),
        P(None, "head"),
        P(None, "head"),
        P(None, "head"),
        P(),
        P(None, "head"),
        P("head"),
        P(),
        P(),
        P("head"),
        P("head"),
        P("head"),
        P("head"),
        P("head", None),
        P(None, "seq", "head"),
    )
    out_specs = (
        P(None, "seq", "head"),
        P(None, "seq", "head"),
        P("head"),
        P(None, "head"),
        P(None, "head"),
        P(None, "head"),
        P(),
        P(None, "head"),
        P("head"),
        P(),
        P(),
        P("head"),
        P("head"),
        P("head"),
        P("head"),
        P("head", None),
    )
    return jax.shard_map(
        on_device, mesh=mesh, in_specs=in_specs, out_specs=out_specs, check_vma=False
    )
```
